256 devices in a mesh: src: 16 (over z, x_hi), dom: 16 (over y, x_lo, core).
Axes of the slice: x: 4 (x_hi: 2, x_lo: 2; x = x_hi * 2 + x_lo), y: 4, z: 8, core: 2. Of those that a mesh axis runs over, the one named last changes fastest.
Arguments:
- primary: float32 [16, 4, 32, 128, 128], P('src', None, 'dom'), may hold values from -6 to 6
- conductivity: float32 [3, 32, 128, 128], P(None, 'dom'), may hold values from 0.5 to 2
- observed: float32 [16, 4, 1024], P('src'), may hold values from -6 to 6
- receivers: int32 [16, 1024], P('src'), may hold values from 0 to 524287
Outputs:
- gradient: float32 [3, 32, 128, 128], P(None, 'dom')
- predicted: float32 [16, 4, 1024], P('src')
The draws below stay inside these ranges and needn't reach their ends.
Inputs may be any that keep to these rules, and one draw needn't show every extreme that they name: receivers may share a cell.
All inputs are finite; a program needn't handle non-finite values.
Results may differ from the reference program's by a relative error of at most 0.0001.
Values sent between devices are 32-bit elements; how exact they have to be, the bound alone decides.
No kernel may reach another device: no remote copies, remote signals or barrier semaphores. Data moves between devices by JAX's collectives and lax.ppermute only.
A program may use at most 128 MiB of HBM per device.

```python
import math
import jax
import jax.numpy as jnp
from jax import lax

SRC = 4
RECV = 1024
ITERS = 3
GROUPS = 16
NX = 32
NY = 128
NZ = 128


def touch_ends(values, rng, least, top_value):
    longest = values.shape.index(max(values.shape))
    spots = []
    for shift in (0, 1):
        where = [jax.random.randint(jax.random.fold_in(rng, axis), (), 0, length) for axis, length in enumerate(values.shape)]
        where[longest] = (where[longest] + shift) % values.shape[longest]
        spots.append(tuple(where))
    return values.at[spots[0]].set(least).at[spots[1]].set(top_value)


def block_levels(stream_key, shape, split, smallest, high):
    def one(position, parts):
        heights = jax.random.uniform(jax.random.fold_in(jax.random.fold_in(stream_key, 6), position), (parts,), jnp.float32, smallest / len(split), high / len(split))
        return jnp.repeat(jnp.exp(heights), shape[position] // parts).reshape((-1,) + (1,) * (len(shape) - position - 1))

    level = one(*split[0])
    for cut in split[1:]:
        level = level * one(*cut)
    return level


def normal_values(key, dims, deviation, reach, shards=(), kind=jnp.bfloat16):
    drawn = deviation * jax.random.normal(key, dims, jnp.float32)
    if shards:
        drawn = drawn * block_levels(key, dims, shards, -0.22, 0.18)
    return jnp.clip(drawn, -reach, reach).astype(kind)


def setup_inputs(seed: int = 0) -> dict:
    streams_of = jax.random.split(jax.random.key(seed), 5)
    primary = normal_values(streams_of[0], (GROUPS, SRC, NX, NY, NZ), 1.0, 6.0, ((0, 16), (2, 16)), jnp.float32)
    conductivity = jnp.clip(jnp.exp(math.log(2.0) - 1.3862944 * jax.random.uniform(streams_of[1], (3, NX, NY, NZ), jnp.float32) ** block_levels(streams_of[1], (3, NX, NY, NZ), ((1, 16),), -0.2, 0.2)), 0.5, 2.0)
    observed = normal_values(streams_of[2], (GROUPS, SRC, RECV), 1.0, 6.0, ((0, 16),), jnp.float32)
    receivers = touch_ends(jax.random.randint(streams_of[3], (GROUPS, RECV), 0, NX * NY * NZ), jax.random.fold_in(streams_of[3], 1), 0, (NX * NY * NZ) - 1).astype(jnp.int32)
    return dict(primary=primary, conductivity=conductivity, observed=observed, receivers=receivers)


def neighbour_upper(field, along):
    extent = field.shape[along]
    inner_part = lax.slice_in_dim(field, 1, extent, axis=along)
    zeros_part = jnp.zeros_like(lax.slice_in_dim(field, 0, 1, axis=along))
    return jnp.concatenate([inner_part, zeros_part], axis=along)


def neighbour_lower(field, along):
    extent = field.shape[along]
    inner_part = lax.slice_in_dim(field, 0, extent - 1, axis=along)
    zeros_part = jnp.zeros_like(lax.slice_in_dim(field, 0, 1, axis=along))
    return jnp.concatenate([zeros_part, inner_part], axis=along)


def face_pair(conduct, along):
    return 0.5 * (conduct + neighbour_upper(conduct, along)), 0.5 * (conduct + neighbour_lower(conduct, along))


def face_list_of(conduct):
    return [face_pair(conduct[component], component) for component in range(3)]


def diagonal_of(face_list):
    result = face_list[0][0] + face_list[0][1]
    for component in (1, 2):
        result = result + face_list[component][0] + face_list[component][1]
    return result


def operate(field, face_list, diagonal):
    result = diagonal * field
    for component in range(3):
        upper, lower = face_list[component]
        result = result - upper * neighbour_upper(field, component + 1) - lower * neighbour_lower(field, component + 1)
    return result


def column(values):
    return values[:, None, None, None]


def inner_sums(left, right):
    return jnp.sum(left * right, axis=(1, 2, 3))


def precond_solve(right_side, face_list, diagonal):
    iterate = jnp.zeros_like(right_side)
    residual = right_side
    scaled = residual / diagonal
    direction = scaled
    norm_now = inner_sums(residual, scaled)
    for iteration in range(ITERS):
        image = operate(direction, face_list, diagonal)
        step_len = column(norm_now / inner_sums(direction, image))
        iterate = iterate + step_len * direction
        residual = residual - step_len * image
        if iteration + 1 < ITERS:
            scaled = residual / diagonal
            norm_next = inner_sums(residual, scaled)
            direction = scaled + column(norm_next / norm_now) * direction
            norm_now = norm_next
    return iterate


def gradient_terms(potential, adjoint):
    pieces = []
    for component in range(3):
        along = component + 1
        upper_term = (potential - neighbour_upper(potential, along)) * (adjoint - neighbour_upper(adjoint, along))
        lower_term = (potential - neighbour_lower(potential, along)) * (adjoint - neighbour_lower(adjoint, along))
        pieces.append(-0.5 * jnp.sum(upper_term + lower_term, axis=0))
    return jnp.stack(pieces)


def reference(primary, conductivity, observed, receivers):
    face_list = face_list_of(conductivity)
    diagonal = diagonal_of(face_list)
    unit_faces = face_list_of(jnp.ones_like(conductivity))
    unit_diagonal = diagonal_of(unit_faces)

    def per_group(running, entries):
        primary_g, observed_g, cells_g = entries
        right_side = operate(primary_g, unit_faces, unit_diagonal) - operate(primary_g, face_list, diagonal)
        potential = primary_g + precond_solve(right_side, face_list, diagonal)
        flattened = potential.reshape(potential.shape[0], -1)
        predicted = jnp.take(flattened, cells_g, axis=1)
        source = jnp.zeros_like(flattened).at[:, cells_g].add(predicted - observed_g).reshape(potential.shape)
        adjoint = precond_solve(source, face_list, diagonal)
        return running + gradient_terms(potential, adjoint), predicted

    start = jnp.zeros(conductivity.shape, jnp.float32)
    summed_grad, predicted = lax.scan(per_group, start, (primary, observed, receivers))
    return summed_grad, predicted
```

```python
import functools
import jax
import jax.numpy as jnp
from jax import lax
from jax.experimental import pallas as pl
from jax.experimental.pallas import tpu as pltpu
from jax.sharding import Mesh, PartitionSpec as P

F32 = jnp.float32
BF16 = jnp.bfloat16
LIMIT = 48 * 1024 * 1024
DEEP = 12
KEPT = 4
CHIPS = 8


def pieces_of(values):
    first = values.astype(BF16)
    rest = values - first.astype(F32)
    second = rest.astype(BF16)
    third = (rest - second.astype(F32)).astype(BF16)
    return first, second, third


def fold(plane):
    return jnp.sum(plane.reshape(plane.shape[0] // 8, 8, plane.shape[1]), axis=0)


def ahead(plane, axis):
    return pltpu.roll(plane, plane.shape[axis] - 1, axis)


def behind(plane, axis):
    return pltpu.roll(plane, 1, axis)


def neighbours(field, s, i, kx, ky, kz):
    mid = field[s, i]
    total = kx[i] * field[s, i + 1] + kx[i - 1] * field[s, i - 1]
    total = total + ky[i] * ahead(mid, 0) + behind(ky[i] * mid, 0)
    return total + kz[i] * ahead(mid, 1) + behind(kz[i] * mid, 1)


def krylov(t0, t1, t2, kx, ky, kz, dinv, dg):
    sources = t0.shape[0]

    def apply_planes(source, target, first, last):
        def body(i, carry):
            for s in range(sources):
                target[s, i] = source[s, i] - dinv[i] * neighbours(source, s, i, kx, ky, kz)
            return carry

        lax.fori_loop(first, last + 1, body, 0)

    apply_planes(t0, t1, 2, 9)
    apply_planes(t1, t2, 3, 8)

    def body(i, sums):
        sums = list(sums)
        for s in range(sources):
            a0, a1, a2 = t0[s, i], t1[s, i], t2[s, i]
            a3 = a2 - dinv[i] * neighbours(t2, s, i, kx, ky, kz)
            d = dg[i]
            b1 = a0 - a1
            b2 = b1 - (a1 - a2)
            b3 = b2 - ((a1 - a2) - (a2 - a3))
            d0, d1, d2, e1, e2 = d * a0, d * a1, d * a2, d * b1, d * b2
            terms = [
                d0 * a0, d0 * a1, d1 * a1, d1 * a2, d2 * a2, d2 * a3,
                d0 * b1, e1 * b1, e1 * b2, e2 * b2, e2 * b3,
            ]
            for k, term in enumerate(terms):
                sums[k * sources + s] = sums[k * sources + s] + fold(term)
        return tuple(sums)

    zero = jnp.zeros((8, t0.shape[3]), F32)
    sums = lax.fori_loop(4, 8, body, (zero,) * (11 * sources))
    rows = [jnp.sum(x) * jnp.ones((1, 128), F32) for x in sums]
    rows = rows + [jnp.zeros((1, 128), F32)] * (24 - len(rows))
    return jnp.concatenate(rows, axis=0)


def weights_of(moments):
    t = [moments[2 * k : 2 * k + 2] for k in range(6)]
    m = [t[0]] + [moments[2 * k : 2 * k + 2] for k in range(6, 11)]
    near = t[1] < 0.5 * t[0]
    g = [jnp.where(near, t[k + 1], m[k] - m[k + 1]) for k in range(5)]
    h = [jnp.where(near, t[k], m[k]) for k in range(3)]
    l1 = g[1] / g[0]
    l2 = g[2] / g[0]
    d1 = g[2] - l1 * g[1]
    e2 = g[3] - l2 * g[1]
    l21 = e2 / d1
    d2 = g[4] - l2 * g[2] - l21 * e2
    y1 = h[1] - l1 * h[0]
    y2 = h[2] - l2 * h[0] - l21 * y1
    c2 = y2 / d2
    c1 = y1 / d1 - l21 * c2
    c0 = h[0] / g[0] - l1 * c1 - l2 * c2
    w0 = jnp.where(near, c0, c0 + c1 + c2)
    w1 = jnp.where(near, c1, -(c1 + 2.0 * c2))
    return w0, w1, c2


def one_hot(count, first, picked):
    place = lax.broadcasted_iota(jnp.int32, (count, picked.shape[1]), 0) + first
    return place == picked


def forward_kernel(
    p_own, p_pair, p_low, p_low_pair, p_high, p_high_pair,
    c_own, c_pair, c_low, c_low_pair, c_high, c_high_pair, cells,
    kx, ky, kz, dinv, dg, prim, t0, t1, t2, sent, cond, hot,
):
    block = 2 * lax.axis_index("y") + lax.axis_index("xl")
    core = lax.axis_index("c")
    here = pl.ds(2 * core, 2)
    other = pl.ds(2 - 2 * core, 2)
    for base, first, second in ((0, p_low, p_low_pair), (4, p_own, p_pair), (8, p_high, p_high_pair)):
        prim[:, pl.ds(base + 2 * core, 2)] = first[...]
        prim[:, pl.ds(base + 2 - 2 * core, 2)] = second[...]
    for base, first, second in ((0, c_low, c_low_pair), (4, c_own, c_pair), (8, c_high, c_high_pair)):
        cond[:, pl.ds(base + 2 * core, 2)] = first[...]
        cond[:, pl.ds(base + 2 - 2 * core, 2)] = second[...]
    rows, lanes = prim.shape[2], prim.shape[3]
    shape = (rows, lanes)
    row_at = lax.broadcasted_iota(jnp.int32, shape, 0)
    lane_at = lax.broadcasted_iota(jnp.int32, shape, 1)
    mask_y = jnp.where(row_at < rows - 1, 1.0, 0.0).astype(F32)
    mask_z = jnp.where(lane_at < lanes - 1, 1.0, 0.0).astype(F32)
    edge = jnp.where(row_at == 0, 0.5, 0.0) + jnp.where(row_at == rows - 1, 0.5, 0.0)
    edge = edge + jnp.where(lane_at == 0, 0.5, 0.0) + jnp.where(lane_at == lanes - 1, 0.5, 0.0)
    unit = (6.0 - edge).astype(F32)
    layers = 4 * CHIPS

    kx[0] = 0.5 * (cond[0, 0] + cond[0, 1])

    def coefficients(i, carry):
        layer = 4 * block - 4 + i
        inside = jnp.where(jnp.logical_and(layer >= 0, layer < layers), 1.0, 0.0).astype(F32)
        first = 0.5 * (cond[0, i] + cond[0, i + 1])
        kx[i] = first
        along_y = cond[1, i]
        along_z = cond[2, i]
        up_y = 0.5 * (along_y + ahead(along_y, 0)) * mask_y
        up_z = 0.5 * (along_z + ahead(along_z, 1)) * mask_z
        ky[i] = up_y
        kz[i] = up_z
        low_y = behind(up_y, 0)
        low_z = behind(up_z, 1)
        up_y = jnp.where(row_at == rows - 1, 0.5 * along_y, up_y)
        up_z = jnp.where(lane_at == lanes - 1, 0.5 * along_z, up_z)
        low_y = jnp.where(row_at == 0, 0.5 * along_y, low_y)
        low_z = jnp.where(lane_at == 0, 0.5 * along_z, low_z)
        diagonal = first + kx[i - 1] + up_y + low_y + up_z + low_z
        inverse = jnp.where(inside > 0.5, 1.0 / diagonal, 0.0)
        dg[i] = diagonal
        dinv[i] = inverse
        return carry

    lax.fori_loop(1, 11, coefficients, 0)

    def right_side(i, carry):
        layer = 4 * block - 4 + i
        outer = jnp.where(jnp.logical_or(layer == 0, layer == layers - 1), 0.5, 0.0).astype(F32)
        diagonal = (unit - outer) - dg[i]
        upper, lower = 1.0 - kx[i], 1.0 - kx[i - 1]
        diff_y = mask_y - ky[i]
        diff_z = mask_z - kz[i]
        inverse = dinv[i]
        for s in range(2):
            mid = prim[s, i]
            total = diagonal * mid - upper * prim[s, i + 1] - lower * prim[s, i - 1]
            total = total - diff_y * ahead(mid, 0) - behind(diff_y * mid, 0)
            total = total - diff_z * ahead(mid, 1) - behind(diff_z * mid, 1)
            t0[s, i] = inverse * total
        return carry

    lax.fori_loop(1, 11, right_side, 0)
    moments = krylov(t0, t1, t2, kx, ky, kz, dinv, dg)

    picked = cells[...]
    row_of = picked // lanes
    lane_of = picked - row_of * lanes
    count = picked.shape[1]
    for j in range(4):
        rows_hot = one_hot(rows, (4 * block + j) * rows, row_of)
        rows_hot = jnp.where(rows_hot, 1.0, 0.0).astype(BF16)
        for piece in range(3):
            hot[pl.ds((piece * 4 + j) * rows, rows)] = rows_hot
    lane_hot = one_hot(lanes, 0, lane_of)
    samples = []
    for field in (prim, t0, t1, t2):
        for s in range(2):
            turned = [jnp.transpose(field[s, 4 + j]) for j in range(4)]
            parts = [pieces_of(x) for x in turned]
            left = jnp.concatenate([parts[j][k] for k in range(3) for j in range(4)], axis=1)
            spread = jnp.dot(left, hot[...], preferred_element_type=F32)
            samples.append(jnp.sum(jnp.where(lane_hot, spread, 0.0), axis=0, keepdims=True))
    sample = jnp.concatenate(samples, axis=0)
    for k in range(CHIPS):
        sent[k, :, :count] = sample
        for j in range(3):
            sent[k, :, count + 128 * j : count + 128 * (j + 1)] = moments[8 * j : 8 * j + 8]


def adjoint_kernel(
    got, observed, cells, kx, ky, kz, dinv, dg, prim, f0, f1, f2,
    a0, a1, a2, pot, predicted, sent, heavy,
):
    block = 2 * lax.axis_index("y") + lax.axis_index("xl")
    core = lax.axis_index("c")
    rows, lanes = prim.shape[2], prim.shape[3]
    count = cells.shape[1]
    total = got[0]
    for k in range(1, CHIPS):
        total = total + got[k]
    moments = jnp.concatenate([total[:, count + 128 * j : count + 128 * (j + 1)] for j in range(3)], axis=0)
    weights = weights_of(moments)
    sample = total[:, :count]
    value = sample[0:2]
    for k in range(3):
        value = value + weights[k][:, 0:1] * sample[2 * k + 2 : 2 * k + 4]
    predicted[...] = value
    seen = jnp.where(core == 0, observed[0:2], observed[2:4])
    misfit = value - seen
    for i in range(6):
        for s in range(2):
            w = [weights[k][s : s + 1, :] for k in range(3)]
            pot[s, i] = prim[s, i + 3] + w[0] * f0[s, i + 3] + w[1] * f1[s, i + 3] + w[2] * f2[s, i + 3]

    picked = cells[...]
    row_of = picked // lanes
    lane_of = picked - row_of * lanes
    lane_hot = one_hot(lanes, 0, lane_of)
    for s in range(2):
        spread = jnp.where(lane_hot, misfit[s : s + 1], 0.0)
        for k, piece in enumerate(pieces_of(spread)):
            heavy[pl.ds(s * lanes, lanes), count * k : count * (k + 1)] = piece

    def scatter(i, carry):
        rows_hot = one_hot(rows, (4 * block - 4 + i) * rows, row_of)
        rows_hot = jnp.where(rows_hot, 1.0, 0.0).astype(BF16)
        left = jnp.concatenate([rows_hot] * 3, axis=1)
        source = lax.dot_general(
            left, heavy[...], (((1,), (1,)), ((), ())), preferred_element_type=F32
        )
        inverse = dinv[i]
        for s in range(2):
            a0[s, i] = inverse * source[:, s * lanes : (s + 1) * lanes]
        return carry

    lax.fori_loop(1, 11, scatter, 0)
    moments = krylov(a0, a1, a2, kx, ky, kz, dinv, dg)
    for k in range(CHIPS):
        sent[k] = moments


def gradient_kernel(got, a0, a1, a2, pot, pred, pred_pair, kept, given, predicted, adj):
    core = lax.axis_index("c")
    moments = got[0]
    for k in range(1, CHIPS):
        moments = moments + got[k]
    weights = weights_of(moments)
    rows, lanes = pot.shape[2], pot.shape[3]
    row_at = lax.broadcasted_iota(jnp.int32, (rows, lanes), 0)
    lane_at = lax.broadcasted_iota(jnp.int32, (rows, lanes), 1)
    predicted[pl.ds(core, 1)] = pred[...][None]
    predicted[pl.ds(1 - core, 1)] = pred_pair[...][None]
    for i in range(6):
        for s in range(2):
            w = [weights[k][s : s + 1, :] for k in range(3)]
            adj[s, i] = w[0] * a0[s, i + 3] + w[1] * a1[s, i + 3] + w[2] * a2[s, i + 3]

    def along(mid_p, mid_a, axis, at):
        last = mid_p.shape[axis] - 1
        next_p = jnp.where(at == last, 0.0, ahead(mid_p, axis))
        next_a = jnp.where(at == last, 0.0, ahead(mid_a, axis))
        upper = (mid_p - next_p) * (mid_a - next_a)
        lower = jnp.where(at == 0, mid_p * mid_a, behind(upper, axis))
        return upper + lower

    for target, first in ((given, 1 + 2 * (1 - core)), (kept, 1 + 2 * core)):
        for j in range(2):
            i = first + j
            sums = [0.0, 0.0, 0.0]
            for s in range(2):
                mid_p, mid_a = pot[s, i], adj[s, i]
                upper = (mid_p - pot[s, i + 1]) * (mid_a - adj[s, i + 1])
                lower = (mid_p - pot[s, i - 1]) * (mid_a - adj[s, i - 1])
                sums[0] = sums[0] + upper + lower
                sums[1] = sums[1] + along(mid_p, mid_a, 0, row_at)
                sums[2] = sums[2] + along(mid_p, mid_a, 1, lane_at)
            for k in range(3):
                target[:, 2 * k + j] = (-0.5 * sums[k]).reshape(rows // 8, 8, lanes)


def call(kernel, outs, scratch=()):
    vmem = pl.BlockSpec(memory_space=pltpu.VMEM)

    def run(*args):
        return pl.pallas_call(
            kernel,
            out_shape=tuple(jax.ShapeDtypeStruct(x, F32) for x in outs),
            in_specs=[vmem] * len(args),
            out_specs=tuple([vmem] * len(outs)),
            scratch_shapes=list(scratch),
            compiler_params=pltpu.CompilerParams(vmem_limit_bytes=LIMIT),
        )(*args)

    return run


NAMES = ("xh", "y", "xl", "c")


def routes(sizes, move):
    pairs = []
    nx, ny = sizes
    index = lambda h, y, l, c: ((h * ny + y) * 2 + l) * 2 + c
    for h in range(nx):
        for y in range(ny):
            for l in range(2):
                for c in range(2):
                    target = move(h, y, l, c)
                    if target is not None:
                        pairs.append((index(h, y, l, c), index(*target)))
    return pairs


def per_device(high_count, primary, conductivity, observed, receivers):
    chain = CHIPS // 2
    sizes = (high_count, chain)
    core = lax.axis_index("c")

    def step(by, flip, around):
        def move(h, y, l, c):
            block = 2 * y + l + by
            if block < 0 or block >= CHIPS:
                return None
            c = 1 - c if flip else c
            side = 2 * h + l
            if around:
                wrap = 1 if (l == 1) else -1
                side = (side + wrap) % (2 * high_count)
                return (side // 2, block // 2, side % 2, c)
            return (h, block // 2, block % 2, c)

        return routes(sizes, move)

    def send(x, pairs):
        return lax.ppermute(x, NAMES, pairs)

    fields = primary[0]
    same = lax.dynamic_slice_in_dim(fields, 2 * core, 2, axis=0)
    cross = lax.dynamic_slice_in_dim(fields, 2 - 2 * core, 2, axis=0)
    swap = routes(sizes, lambda h, y, l, c: (h, y, l, 1 - c))
    c_low = send(conductivity, step(1, False, True))
    c_high = send(conductivity, step(-1, False, True))
    p_low = send(same, step(1, False, False))
    p_high = send(same, step(-1, False, False))
    p_low_pair = send(cross, step(1, True, False))
    p_high_pair = send(cross, step(-1, True, False))
    p_pair = send(cross, swap)
    c_pair = send(conductivity, swap)
    c_low_pair = send(c_low, swap)
    c_high_pair = send(c_high, swap)

    rows, lanes = primary.shape[3], primary.shape[4]
    count = receivers.shape[1]
    deep = (DEEP, rows, lanes)
    pairs = (2, DEEP, rows, lanes)
    payload = (CHIPS, 8, count + 384)
    kx, ky, kz, dinv, dg, prim, f0, f1, f2, sent = call(
        forward_kernel,
        [deep] * 5 + [pairs] * 4 + [payload],
        [pltpu.VMEM((3,) + deep, F32), pltpu.VMEM((12 * rows, count), BF16)],
    )(
        same, p_pair, p_low, p_low_pair, p_high, p_high_pair,
        conductivity, c_pair, c_low, c_low_pair, c_high, c_high_pair, receivers,
    )
    got = lax.all_to_all(sent, ("y", "xl"), 0, 0, tiled=True)
    six = (2, 6, rows, lanes)
    a0, a1, a2, pot, pred, sent = call(
        adjoint_kernel,
        [pairs] * 3 + [six, (2, count), (CHIPS, 24, 128)],
        [pltpu.VMEM((2 * lanes, 3 * count), BF16)],
    )(got, observed[0], receivers, kx, ky, kz, dinv, dg, prim, f0, f1, f2)
    pred_pair = send(pred, swap)
    got = lax.all_to_all(sent, ("y", "xl"), 0, 0, tiled=True)
    chunks = (rows // 8, 6, 8, lanes)
    kept, given, predicted = call(
        gradient_kernel, [chunks, chunks, (2, 2, count)], [pltpu.VMEM(six, F32)]
    )(got, a0, a1, a2, pot, pred, pred_pair)
    total = kept + send(given, swap)
    parts = lax.all_to_all(total, ("z", "xh"), 0, 0, tiled=True)
    share = jnp.sum(parts, axis=0, keepdims=True)
    spread = jnp.broadcast_to(share, chunks)
    whole = lax.all_to_all(spread, ("z", "xh"), 0, 0, tiled=True)
    grad = jnp.transpose(whole, (1, 0, 2, 3)).reshape(3, 2, rows, lanes)
    return grad, predicted.reshape(1, 4, count)


def solution(mesh):
    groups = mesh.shape["src"]
    high = 2 if groups > 1 else 1
    devices = mesh.devices.reshape(groups // high, high, CHIPS // 2, 2, 2)
    inner = Mesh(devices, ("z", "xh", "y", "xl", "c"))
    src, dom = ("z", "xh"), ("y", "xl", "c")
    return jax.shard_map(
        functools.partial(per_device, high),
        mesh=inner,
        in_specs=(P(src, None, dom, None, None), P(None, dom, None, None), P(src, None, None), P(src, None)),
        out_specs=(P(None, dom, None, None), P(src, None, None)),
        check_vma=False,
    )
```

```python
import functools
import jax
import jax.numpy as jnp
from jax import lax
from jax.experimental import pallas as pl
from jax.experimental.pallas import tpu as pltpu
from jax.sharding import Mesh, PartitionSpec as P

F32 = jnp.float32
BF16 = jnp.bfloat16
MEBI = 1024 * 1024
DEEP = 12
KEPT = 4
CHIPS = 8


def pieces_of(values):
    first = values.astype(BF16)
    rest = values - first.astype(F32)
    second = rest.astype(BF16)
    third = (rest - second.astype(F32)).astype(BF16)
    return first, second, third


def fold(plane):
    return jnp.sum(plane.reshape(plane.shape[0] // 8, 8, plane.shape[1]), axis=0)


def ahead(plane, axis):
    return pltpu.roll(plane, plane.shape[axis] - 1, axis)


def behind(plane, axis):
    return pltpu.roll(plane, 1, axis)


def neighbours(field, s, i, kx, ky, kz):
    mid = field[s, i]
    total = kx[i] * field[s, i + 1] + kx[i - 1] * field[s, i - 1]
    total = total + ky[i] * ahead(mid, 0) + behind(ky[i] * mid, 0)
    return total + kz[i] * ahead(mid, 1) + behind(kz[i] * mid, 1)


def krylov(t0, t1, t2, kx, ky, kz, dinv, dg):
    sources = t0.shape[0]

    def apply_planes(source, target, first, last):
        def body(i, carry):
            for s in range(sources):
                target[s, i] = source[s, i] - dinv[i] * neighbours(source, s, i, kx, ky, kz)
            return carry

        lax.fori_loop(first, last + 1, body, 0)

    apply_planes(t0, t1, 2, 9)
    apply_planes(t1, t2, 3, 8)

    def body(i, sums):
        sums = list(sums)
        for s in range(sources):
            a0, a1, a2 = t0[s, i], t1[s, i], t2[s, i]
            a3 = a2 - dinv[i] * neighbours(t2, s, i, kx, ky, kz)
            d = dg[i]
            b1 = a0 - a1
            b2 = b1 - (a1 - a2)
            b3 = b2 - ((a1 - a2) - (a2 - a3))
            d0, d1, d2, e1, e2 = d * a0, d * a1, d * a2, d * b1, d * b2
            terms = [
                d0 * a0, d0 * a1, d1 * a1, d1 * a2, d2 * a2, d2 * a3,
                d0 * b1, e1 * b1, e1 * b2, e2 * b2, e2 * b3,
            ]
            for k, term in enumerate(terms):
                sums[k * sources + s] = sums[k * sources + s] + fold(term)
        return tuple(sums)

    zero = jnp.zeros((8, t0.shape[3]), F32)
    sums = lax.fori_loop(4, 8, body, (zero,) * (11 * sources))
    rows = [jnp.sum(x) * jnp.ones((1, 128), F32) for x in sums]
    rows = rows + [jnp.zeros((1, 128), F32)] * (24 - len(rows))
    return jnp.concatenate(rows, axis=0)


def weights_of(moments):
    t = [moments[2 * k : 2 * k + 2] for k in range(6)]
    m = [t[0]] + [moments[2 * k : 2 * k + 2] for k in range(6, 11)]
    near = t[1] < 0.5 * t[0]
    g = [jnp.where(near, t[k + 1], m[k] - m[k + 1]) for k in range(5)]
    h = [jnp.where(near, t[k], m[k]) for k in range(3)]
    l1 = g[1] / g[0]
    l2 = g[2] / g[0]
    d1 = g[2] - l1 * g[1]
    e2 = g[3] - l2 * g[1]
    l21 = e2 / d1
    d2 = g[4] - l2 * g[2] - l21 * e2
    y1 = h[1] - l1 * h[0]
    y2 = h[2] - l2 * h[0] - l21 * y1
    c2 = y2 / d2
    c1 = y1 / d1 - l21 * c2
    c0 = h[0] / g[0] - l1 * c1 - l2 * c2
    w0 = jnp.where(near, c0, c0 + c1 + c2)
    w1 = jnp.where(near, c1, -(c1 + 2.0 * c2))
    return w0, w1, c2


def one_hot(count, first, picked):
    place = lax.broadcasted_iota(jnp.int32, (count, picked.shape[1]), 0) + first
    return place == picked


def forward_kernel(
    p_own, p_pair, p_low, p_low_pair, p_high, p_high_pair,
    c_own, c_pair, c_low, c_low_pair, c_high, c_high_pair, cells,
    kx, ky, kz, dinv, dg, prim, t0, t1, t2, sent, cond, hot, left,
):
    block = 2 * lax.axis_index("y") + lax.axis_index("xl")
    core = lax.axis_index("c")
    here = pl.ds(2 * core, 2)
    for base, first, second in ((0, p_low, p_low_pair), (4, p_own, p_pair), (8, p_high, p_high_pair)):
        prim[:, pl.ds(base + 2 * core, 2)] = first[here]
        prim[:, pl.ds(base + 2 - 2 * core, 2)] = second[here]
    for base, first, second in ((0, c_low, c_low_pair), (4, c_own, c_pair), (8, c_high, c_high_pair)):
        cond[:, pl.ds(base + 2 * core, 2)] = first[...]
        cond[:, pl.ds(base + 2 - 2 * core, 2)] = second[...]
    rows, lanes = prim.shape[2], prim.shape[3]
    shape = (rows, lanes)
    row_at = lax.broadcasted_iota(jnp.int32, shape, 0)
    lane_at = lax.broadcasted_iota(jnp.int32, shape, 1)
    mask_y = jnp.where(row_at < rows - 1, 1.0, 0.0).astype(F32)
    mask_z = jnp.where(lane_at < lanes - 1, 1.0, 0.0).astype(F32)
    edge = jnp.where(row_at == 0, 0.5, 0.0) + jnp.where(row_at == rows - 1, 0.5, 0.0)
    edge = edge + jnp.where(lane_at == 0, 0.5, 0.0) + jnp.where(lane_at == lanes - 1, 0.5, 0.0)
    unit = (6.0 - edge).astype(F32)
    layers = 4 * CHIPS

    kx[0] = 0.5 * (cond[0, 0] + cond[0, 1])

    def coefficients(i, carry):
        layer = 4 * block - 4 + i
        inside = jnp.where(jnp.logical_and(layer >= 0, layer < layers), 1.0, 0.0).astype(F32)
        first = 0.5 * (cond[0, i] + cond[0, i + 1])
        kx[i] = first
        along_y = cond[1, i]
        along_z = cond[2, i]
        up_y = 0.5 * (along_y + ahead(along_y, 0)) * mask_y
        up_z = 0.5 * (along_z + ahead(along_z, 1)) * mask_z
        ky[i] = up_y
        kz[i] = up_z
        low_y = behind(up_y, 0)
        low_z = behind(up_z, 1)
        up_y = jnp.where(row_at == rows - 1, 0.5 * along_y, up_y)
        up_z = jnp.where(lane_at == lanes - 1, 0.5 * along_z, up_z)
        low_y = jnp.where(row_at == 0, 0.5 * along_y, low_y)
        low_z = jnp.where(lane_at == 0, 0.5 * along_z, low_z)
        diagonal = first + kx[i - 1] + up_y + low_y + up_z + low_z
        inverse = jnp.where(inside > 0.5, 1.0 / diagonal, 0.0)
        dg[i] = diagonal
        dinv[i] = inverse
        return carry

    lax.fori_loop(1, 11, coefficients, 0)

    def right_side(i, carry):
        layer = 4 * block - 4 + i
        outer = jnp.where(jnp.logical_or(layer == 0, layer == layers - 1), 0.5, 0.0).astype(F32)
        diagonal = (unit - outer) - dg[i]
        upper, lower = 1.0 - kx[i], 1.0 - kx[i - 1]
        diff_y = mask_y - ky[i]
        diff_z = mask_z - kz[i]
        inverse = dinv[i]
        for s in range(2):
            mid = prim[s, i]
            total = diagonal * mid - upper * prim[s, i + 1] - lower * prim[s, i - 1]
            total = total - diff_y * ahead(mid, 0) - behind(diff_y * mid, 0)
            total = total - diff_z * ahead(mid, 1) - behind(diff_z * mid, 1)
            t0[s, i] = inverse * total
        return carry

    lax.fori_loop(1, 11, right_side, 0)
    moments = krylov(t0, t1, t2, kx, ky, kz, dinv, dg)

    picked = cells[...]
    row_of = picked // lanes
    lane_of = picked - row_of * lanes
    count = picked.shape[1]
    for j in range(4):
        rows_hot = one_hot(rows, (4 * block + j) * rows, row_of)
        rows_hot = jnp.where(rows_hot, 1.0, 0.0).astype(BF16)
        for piece in range(3):
            hot[pl.ds((piece * 4 + j) * rows, rows)] = rows_hot
    lane_hot = one_hot(lanes, 0, lane_of)
    for f, field in enumerate((prim, t0, t1, t2)):
        for s in range(2):
            for j in range(4):
                parts = pieces_of(jnp.transpose(field[s, 4 + j]))
                for k in range(3):
                    start = (k * 4 + j) * rows
                    left[pl.ds((2 * f + s) * lanes, lanes), start : start + rows] = parts[k]
    spread = jnp.dot(left[...], hot[...], preferred_element_type=F32)
    samples = [
        jnp.sum(jnp.where(lane_hot, spread[k * lanes : (k + 1) * lanes], 0.0), axis=0, keepdims=True)
        for k in range(8)
    ]
    sample = jnp.concatenate(samples, axis=0)
    for k in range(CHIPS):
        sent[k, :, :count] = sample
        for j in range(3):
            sent[k, :, count + 128 * j : count + 128 * (j + 1)] = moments[8 * j : 8 * j + 8]


def adjoint_kernel(
    got, observed, cells, kx, ky, kz, dinv, dg, prim, f0, f1, f2,
    a0, a1, a2, pot, predicted, sent, heavy, hot,
):
    block = 2 * lax.axis_index("y") + lax.axis_index("xl")
    core = lax.axis_index("c")
    rows, lanes = prim.shape[2], prim.shape[3]
    count = cells.shape[1]
    total = got[0]
    for k in range(1, CHIPS):
        total = total + got[k]
    moments = jnp.concatenate([total[:, count + 128 * j : count + 128 * (j + 1)] for j in range(3)], axis=0)
    weights = weights_of(moments)
    sample = total[:, :count]
    value = sample[0:2]
    for k in range(3):
        value = value + weights[k][:, 0:1] * sample[2 * k + 2 : 2 * k + 4]
    predicted[...] = value
    seen = jnp.where(core == 0, observed[0:2], observed[2:4])
    misfit = value - seen
    for i in range(6):
        for s in range(2):
            w = [weights[k][s : s + 1, :] for k in range(3)]
            pot[s, i] = prim[s, i + 3] + w[0] * f0[s, i + 3] + w[1] * f1[s, i + 3] + w[2] * f2[s, i + 3]

    picked = cells[...]
    row_of = picked // lanes
    lane_of = picked - row_of * lanes
    lane_hot = one_hot(lanes, 0, lane_of)
    for s in range(2):
        spread = jnp.where(lane_hot, misfit[s : s + 1], 0.0)
        for k, piece in enumerate(pieces_of(spread)):
            heavy[k, pl.ds(s * lanes, lanes)] = piece
    for i in range(10):
        rows_hot = one_hot(rows, (4 * block - 3 + i) * rows, row_of)
        hot[pl.ds(i * rows, rows)] = jnp.where(rows_hot, 1.0, 0.0).astype(BF16)
    placed = [
        lax.dot_general(hot[...], heavy[k], (((1,), (1,)), ((), ())), preferred_element_type=F32)
        for k in range(3)
    ]
    source = placed[0] + placed[1] + placed[2]
    for i in range(10):
        inverse = dinv[i + 1]
        for s in range(2):
            a0[s, i + 1] = inverse * source[i * rows : (i + 1) * rows, s * lanes : (s + 1) * lanes]
    moments = krylov(a0, a1, a2, kx, ky, kz, dinv, dg)
    for k in range(CHIPS):
        sent[k] = moments


def gradient_kernel(got, a0, a1, a2, pot, pred, pred_pair, kept, given, predicted, adj):
    core = lax.axis_index("c")
    moments = got[0]
    for k in range(1, CHIPS):
        moments = moments + got[k]
    weights = weights_of(moments)
    rows, lanes = pot.shape[2], pot.shape[3]
    row_at = lax.broadcasted_iota(jnp.int32, (rows, lanes), 0)
    lane_at = lax.broadcasted_iota(jnp.int32, (rows, lanes), 1)
    predicted[pl.ds(core, 1)] = pred[...][None]
    predicted[pl.ds(1 - core, 1)] = pred_pair[...][None]
    for i in range(6):
        for s in range(2):
            w = [weights[k][s : s + 1, :] for k in range(3)]
            adj[s, i] = w[0] * a0[s, i + 3] + w[1] * a1[s, i + 3] + w[2] * a2[s, i + 3]

    def along(mid_p, mid_a, axis, at):
        last = mid_p.shape[axis] - 1
        next_p = jnp.where(at == last, 0.0, ahead(mid_p, axis))
        next_a = jnp.where(at == last, 0.0, ahead(mid_a, axis))
        upper = (mid_p - next_p) * (mid_a - next_a)
        lower = jnp.where(at == 0, mid_p * mid_a, behind(upper, axis))
        return upper + lower

    for target, first in ((given, 1 + 2 * (1 - core)), (kept, 1 + 2 * core)):
        for j in range(2):
            i = first + j
            sums = [0.0, 0.0, 0.0]
            for s in range(2):
                mid_p, mid_a = pot[s, i], adj[s, i]
                upper = (mid_p - pot[s, i + 1]) * (mid_a - adj[s, i + 1])
                lower = (mid_p - pot[s, i - 1]) * (mid_a - adj[s, i - 1])
                sums[0] = sums[0] + upper + lower
                sums[1] = sums[1] + along(mid_p, mid_a, 0, row_at)
                sums[2] = sums[2] + along(mid_p, mid_a, 1, lane_at)
            for k in range(3):
                target[:, 2 * k + j] = (-0.5 * sums[k]).reshape(rows // 8, 8, lanes)


def call(kernel, limit, outs, scratch=()):
    vmem = pl.BlockSpec(memory_space=pltpu.VMEM)

    def run(*args):
        return pl.pallas_call(
            kernel,
            out_shape=tuple(jax.ShapeDtypeStruct(x, F32) for x in outs),
            in_specs=[vmem] * len(args),
            out_specs=tuple([vmem] * len(outs)),
            scratch_shapes=list(scratch),
            compiler_params=pltpu.CompilerParams(vmem_limit_bytes=limit * MEBI),
        )(*args)

    return run


NAMES = ("xh", "y", "xl", "c")


def routes(sizes, move):
    pairs = []
    nx, ny = sizes
    index = lambda h, y, l, c: ((h * ny + y) * 2 + l) * 2 + c
    for h in range(nx):
        for y in range(ny):
            for l in range(2):
                for c in range(2):
                    target = move(h, y, l, c)
                    if target is not None:
                        pairs.append((index(h, y, l, c), index(*target)))
    return pairs


def per_device(high_count, primary, conductivity, observed, receivers):
    chain = CHIPS // 2
    sizes = (high_count, chain)
    def step(by, around):
        def move(h, y, l, c):
            block = 2 * y + l + by
            if block < 0 or block >= CHIPS:
                return None
            side = 2 * h + l
            if around:
                wrap = 1 if (l == 1) else -1
                side = (side + wrap) % (2 * high_count)
                return (side // 2, block // 2, side % 2, c)
            return (h, block // 2, block % 2, c)

        return routes(sizes, move)

    def send(x, pairs):
        return lax.ppermute(x, NAMES, pairs)

    fields = primary[0]
    swap = routes(sizes, lambda h, y, l, c: (h, y, l, 1 - c))
    p_low = send(fields, step(1, False))
    p_high = send(fields, step(-1, False))
    c_low = send(conductivity, step(1, True))
    c_high = send(conductivity, step(-1, True))
    p_pair = send(fields, swap)
    c_pair = send(conductivity, swap)
    c_low_pair = send(c_low, swap)
    c_high_pair = send(c_high, swap)
    p_low_pair = send(p_low, swap)
    p_high_pair = send(p_high, swap)

    rows, lanes = primary.shape[3], primary.shape[4]
    count = receivers.shape[1]
    deep = (DEEP, rows, lanes)
    pairs = (2, DEEP, rows, lanes)
    payload = (CHIPS, 8, count + 384)
    kx, ky, kz, dinv, dg, prim, f0, f1, f2, sent = call(
        forward_kernel,
        26,
        [deep] * 5 + [pairs] * 4 + [payload],
        [pltpu.VMEM((3,) + deep, F32), pltpu.VMEM((12 * rows, count), BF16), pltpu.VMEM((8 * lanes, 12 * rows), BF16)],
    )(
        fields, p_pair, p_low, p_low_pair, p_high, p_high_pair,
        conductivity, c_pair, c_low, c_low_pair, c_high, c_high_pair, receivers,
    )
    got = lax.all_to_all(sent, ("y", "xl"), 0, 0, tiled=True)
    six = (2, 6, rows, lanes)
    a0, a1, a2, pot, pred, sent = call(
        adjoint_kernel,
        18,
        [pairs] * 3 + [six, (2, count), (CHIPS, 24, 128)],
        [pltpu.VMEM((3, 2 * lanes, count), BF16), pltpu.VMEM((10 * rows, count), BF16)],
    )(got, observed[0], receivers, kx, ky, kz, dinv, dg, prim, f0, f1, f2)
    pred_pair = send(pred, swap)
    got = lax.all_to_all(sent, ("y", "xl"), 0, 0, tiled=True)
    chunks = (rows // 8, 6, 8, lanes)
    kept, given, predicted = call(
        gradient_kernel, 8, [chunks, chunks, (2, 2, count)], [pltpu.VMEM(six, F32)]
    )(got, a0, a1, a2, pot, pred, pred_pair)
    total = kept + send(given, swap)
    parts = lax.all_to_all(total, ("z", "xh"), 0, 0, tiled=True)
    share = jnp.sum(parts, axis=0, keepdims=True)
    spread = jnp.broadcast_to(share, chunks)
    whole = lax.all_to_all(spread, ("z", "xh"), 0, 0, tiled=True)
    grad = jnp.transpose(whole, (1, 0, 2, 3)).reshape(3, 2, rows, lanes)
    return grad, predicted.reshape(1, 4, count)


def solution(mesh):
    groups = mesh.shape["src"]
    high = 2 if groups > 1 else 1
    devices = mesh.devices.reshape(groups // high, high, CHIPS // 2, 2, 2)
    inner = Mesh(devices, ("z", "xh", "y", "xl", "c"))
    src, dom = ("z", "xh"), ("y", "xl", "c")
    return jax.shard_map(
        functools.partial(per_device, high),
        mesh=inner,
        in_specs=(P(src, None, dom, None, None), P(None, dom, None, None), P(src, None, None), P(src, None)),
        out_specs=(P(None, dom, None, None), P(src, None, None)),
        check_vma=False,
    )
```

```python
import functools
import jax
import jax.numpy as jnp
from jax import lax
from jax.experimental import pallas as pl
from jax.experimental.pallas import tpu as pltpu
from jax.sharding import Mesh, PartitionSpec as P

F32 = jnp.float32
BF16 = jnp.bfloat16
MEBI = 1024 * 1024
DEEP = 12
KEPT = 4
CHIPS = 8


def pieces_of(values):
    first = values.astype(BF16)
    rest = values - first.astype(F32)
    second = rest.astype(BF16)
    third = (rest - second.astype(F32)).astype(BF16)
    return first, second, third


def fold(plane):
    return jnp.sum(plane.reshape(plane.shape[0] // 8, 8, plane.shape[1]), axis=0)


def ahead(plane, axis):
    return pltpu.roll(plane, plane.shape[axis] - 1, axis)


def behind(plane, axis):
    return pltpu.roll(plane, 1, axis)


def neighbours(field, s, i, kx, ky, kz):
    mid = field[s, i]
    total = kx[i] * field[s, i + 1] + kx[i - 1] * field[s, i - 1]
    total = total + ky[i] * ahead(mid, 0) + behind(ky[i] * mid, 0)
    return total + kz[i] * ahead(mid, 1) + behind(kz[i] * mid, 1)


def krylov(t0, t1, t2, kx, ky, kz, dinv, dg):
    sources = t0.shape[0]

    def apply_planes(source, target, first, last):
        def body(i, carry):
            for s in range(sources):
                target[s, i] = source[s, i] - dinv[i] * neighbours(source, s, i, kx, ky, kz)
            return carry

        lax.fori_loop(first, last + 1, body, 0)

    apply_planes(t0, t1, 2, 9)
    apply_planes(t1, t2, 3, 8)

    def body(i, sums):
        sums = list(sums)
        for s in range(sources):
            a0, a1, a2 = t0[s, i], t1[s, i], t2[s, i]
            a3 = a2 - dinv[i] * neighbours(t2, s, i, kx, ky, kz)
            d = dg[i]
            b1 = a0 - a1
            b2 = b1 - (a1 - a2)
            b3 = b2 - ((a1 - a2) - (a2 - a3))
            d0, d1, d2, e1, e2 = d * a0, d * a1, d * a2, d * b1, d * b2
            terms = [
                d0 * a0, d0 * a1, d1 * a1, d1 * a2, d2 * a2, d2 * a3,
                d0 * b1, e1 * b1, e1 * b2, e2 * b2, e2 * b3,
            ]
            for k, term in enumerate(terms):
                sums[k * sources + s] = sums[k * sources + s] + fold(term)
        return tuple(sums)

    zero = jnp.zeros((8, t0.shape[3]), F32)
    sums = lax.fori_loop(4, 8, body, (zero,) * (11 * sources))
    row_at = lax.broadcasted_iota(jnp.int32, (8, 128), 0)
    lane_at = lax.broadcasted_iota(jnp.int32, (8, 128), 1)
    packed = jnp.zeros((8, 128), F32)
    for n, x in enumerate(sums):
        here = jnp.logical_and(row_at == n % sources, lane_at == n // sources)
        packed = jnp.where(here, jnp.sum(x), packed)
    return packed


def weights_of(moments):
    t = [moments[0:2, k : k + 1] for k in range(6)]
    m = [t[0]] + [moments[0:2, k : k + 1] for k in range(6, 11)]
    near = t[1] < 0.5 * t[0]
    g = [jnp.where(near, t[k + 1], m[k] - m[k + 1]) for k in range(5)]
    h = [jnp.where(near, t[k], m[k]) for k in range(3)]
    l1 = g[1] / g[0]
    l2 = g[2] / g[0]
    d1 = g[2] - l1 * g[1]
    e2 = g[3] - l2 * g[1]
    l21 = e2 / d1
    d2 = g[4] - l2 * g[2] - l21 * e2
    y1 = h[1] - l1 * h[0]
    y2 = h[2] - l2 * h[0] - l21 * y1
    c2 = y2 / d2
    c1 = y1 / d1 - l21 * c2
    c0 = h[0] / g[0] - l1 * c1 - l2 * c2
    w0 = jnp.where(near, c0, c0 + c1 + c2)
    w1 = jnp.where(near, c1, -(c1 + 2.0 * c2))
    return w0, w1, c2


def one_hot(count, first, picked):
    place = lax.broadcasted_iota(jnp.int32, (count, picked.shape[1]), 0) + first
    return place == picked


def edges(rows, lanes):
    row_at = lax.broadcasted_iota(jnp.int32, (rows, lanes), 0)
    lane_at = lax.broadcasted_iota(jnp.int32, (rows, lanes), 1)
    mask_y = jnp.where(row_at < rows - 1, 1.0, 0.0).astype(F32)
    mask_z = jnp.where(lane_at < lanes - 1, 1.0, 0.0).astype(F32)
    return row_at, lane_at, mask_y, mask_z


def in_plane(along_y, along_z):
    rows, lanes = along_y.shape
    row_at, lane_at, mask_y, mask_z = edges(rows, lanes)
    up_y = 0.5 * (along_y + ahead(along_y, 0)) * mask_y
    up_z = 0.5 * (along_z + ahead(along_z, 1)) * mask_z
    low_y = jnp.where(row_at == 0, 0.5 * along_y, behind(up_y, 0))
    low_z = jnp.where(lane_at == 0, 0.5 * along_z, behind(up_z, 1))
    top_y = jnp.where(row_at == rows - 1, 0.5 * along_y, up_y)
    top_z = jnp.where(lane_at == lanes - 1, 0.5 * along_z, up_z)
    return up_y, up_z, top_y + low_y + top_z + low_z


def own_kernel(p_own, p_pair, c_own, c_pair, cells, prim, first, ky, kz, plane_dg, hot, hot_own, sample, left):
    block = 2 * lax.axis_index("y") + lax.axis_index("xl")
    core = lax.axis_index("c")
    here = pl.ds(2 * core, 2)
    other = pl.ds(2 - 2 * core, 2)
    prim[:, here] = p_own[here]
    prim[:, other] = p_pair[here]
    first[here] = c_own[0]
    first[other] = c_pair[0]
    rows, lanes = prim.shape[2], prim.shape[3]
    for source, base in ((c_own, 2 * core), (c_pair, 2 - 2 * core)):
        for j in range(2):
            up_y, up_z, part = in_plane(source[1, j], source[2, j])
            ky[base + j] = up_y
            kz[base + j] = up_z
            plane_dg[base + j] = part
    picked = cells[...]
    row_of = picked // lanes
    lane_of = picked - row_of * lanes
    for i in range(10):
        rows_hot = one_hot(rows, (4 * block - 3 + i) * rows, row_of)
        rows_hot = jnp.where(rows_hot, 1.0, 0.0).astype(BF16)
        hot[pl.ds(i * rows, rows)] = rows_hot
        if 3 <= i < 7:
            for piece in range(3):
                hot_own[pl.ds((piece * KEPT + i - 3) * rows, rows)] = rows_hot
    gather([(prim, 0)], left, hot_own, one_hot(lanes, 0, lane_of), sample)


def gather(fields, left, hot_own, lane_hot, sample):
    lanes = lane_hot.shape[0]
    for f, (field, first) in enumerate(fields):
        rows = field.shape[2]
        for s in range(2):
            for j in range(KEPT):
                parts = pieces_of(jnp.transpose(field[s, first + j]))
                for k in range(3):
                    start = (k * KEPT + j) * rows
                    left[pl.ds((2 * f + s) * lanes, lanes), start : start + rows] = parts[k]
    spread = jnp.dot(left[...], hot_own[...], preferred_element_type=F32)
    found = [
        jnp.sum(jnp.where(lane_hot, spread[k * lanes : (k + 1) * lanes], 0.0), axis=0, keepdims=True)
        for k in range(2 * len(fields))
    ]
    sample[...] = jnp.concatenate(found, axis=0)


def forward_kernel(
    p_mid, p_low, p_low_pair, p_high, p_high_pair,
    c_mid, c_low, c_low_pair, c_high, c_high_pair, ky_mid, kz_mid, dg_mid, cells, hot_own, p_sample,
    kx, ky, kz, dinv, dg, prim, t0, t1, t2, sent, cond, left, found,
):
    block = 2 * lax.axis_index("y") + lax.axis_index("xl")
    core = lax.axis_index("c")
    here = pl.ds(2 * core, 2)
    prim[:, 4:8] = p_mid[...]
    cond[4:8] = c_mid[...]
    for base, first, second in ((0, p_low, p_low_pair), (8, p_high, p_high_pair)):
        prim[:, pl.ds(base + 2 * core, 2)] = first[here]
        prim[:, pl.ds(base + 2 - 2 * core, 2)] = second[here]
    for base, first, second in ((0, c_low, c_low_pair), (8, c_high, c_high_pair)):
        cond[pl.ds(base + 2 * core, 2)] = first[0]
        cond[pl.ds(base + 2 - 2 * core, 2)] = second[0]
        for source, start in ((first, base + 2 * core), (second, base + 2 - 2 * core)):
            for j in range(2):
                up_y, up_z, part = in_plane(source[1, j], source[2, j])
                ky[start + j] = up_y
                kz[start + j] = up_z
                dg[start + j] = part
    ky[4:8] = ky_mid[...]
    kz[4:8] = kz_mid[...]
    dg[4:8] = dg_mid[...]
    rows, lanes = prim.shape[2], prim.shape[3]
    row_at, lane_at, mask_y, mask_z = edges(rows, lanes)
    edge = jnp.where(row_at == 0, 0.5, 0.0) + jnp.where(row_at == rows - 1, 0.5, 0.0)
    edge = edge + jnp.where(lane_at == 0, 0.5, 0.0) + jnp.where(lane_at == lanes - 1, 0.5, 0.0)
    unit = (6.0 - edge).astype(F32)
    layers = 4 * CHIPS

    kx[0] = 0.5 * (cond[0] + cond[1])

    def coefficients(i, carry):
        layer = 4 * block - 4 + i
        inside = jnp.where(jnp.logical_and(layer >= 0, layer < layers), 1.0, 0.0).astype(F32)
        first = 0.5 * (cond[i] + cond[i + 1])
        kx[i] = first
        diagonal = first + kx[i - 1] + dg[i]
        inverse = jnp.where(inside > 0.5, 1.0 / diagonal, 0.0)
        dg[i] = diagonal
        dinv[i] = inverse
        return carry

    lax.fori_loop(1, 11, coefficients, 0)

    def right_side(i, carry):
        layer = 4 * block - 4 + i
        outer = jnp.where(jnp.logical_or(layer == 0, layer == layers - 1), 0.5, 0.0).astype(F32)
        diagonal = (unit - outer) - dg[i]
        upper, lower = 1.0 - kx[i], 1.0 - kx[i - 1]
        diff_y = mask_y - ky[i]
        diff_z = mask_z - kz[i]
        inverse = dinv[i]
        for s in range(2):
            mid = prim[s, i]
            total = diagonal * mid - upper * prim[s, i + 1] - lower * prim[s, i - 1]
            total = total - diff_y * ahead(mid, 0) - behind(diff_y * mid, 0)
            total = total - diff_z * ahead(mid, 1) - behind(diff_z * mid, 1)
            t0[s, i] = inverse * total
        return carry

    lax.fori_loop(1, 11, right_side, 0)
    moments = krylov(t0, t1, t2, kx, ky, kz, dinv, dg)

    picked = cells[...]
    lane_of = picked - (picked // lanes) * lanes
    count = picked.shape[1]
    gather([(t0, 4), (t1, 4), (t2, 4)], left, hot_own, one_hot(lanes, 0, lane_of), found)
    for k in range(CHIPS):
        sent[k, 0:2, :count] = p_sample[...]
        sent[k, 2:8, :count] = found[...]
        sent[k, :, count:] = moments


def adjoint_kernel(
    got, observed, cells, hot, kx, ky, kz, dinv, dg, prim, f0, f1, f2,
    a0, a1, a2, pot, predicted, sent, heavy,
):
    core = lax.axis_index("c")
    rows, lanes = prim.shape[2], prim.shape[3]
    count = cells.shape[1]
    total = got[0]
    for k in range(1, CHIPS):
        total = total + got[k]
    weights = weights_of(total[:, count:])
    sample = total[:, :count]
    value = sample[0:2]
    for k in range(3):
        value = value + weights[k] * sample[2 * k + 2 : 2 * k + 4]
    predicted[...] = value
    seen = jnp.where(core == 0, observed[0:2], observed[2:4])
    misfit = value - seen
    for i in range(6):
        for s in range(2):
            w = [weights[k][s : s + 1, :] for k in range(3)]
            pot[s, i] = prim[s, i + 3] + w[0] * f0[s, i + 3] + w[1] * f1[s, i + 3] + w[2] * f2[s, i + 3]

    picked = cells[...]
    lane_of = picked - (picked // lanes) * lanes
    lane_hot = one_hot(lanes, 0, lane_of)
    for s in range(2):
        spread = jnp.where(lane_hot, misfit[s : s + 1], 0.0)
        for k, piece in enumerate(pieces_of(spread)):
            heavy[k, pl.ds(s * lanes, lanes)] = piece
    placed = [
        lax.dot_general(hot[...], heavy[k], (((1,), (1,)), ((), ())), preferred_element_type=F32)
        for k in range(3)
    ]
    source = placed[0] + placed[1] + placed[2]
    for i in range(10):
        inverse = dinv[i + 1]
        for s in range(2):
            a0[s, i + 1] = inverse * source[i * rows : (i + 1) * rows, s * lanes : (s + 1) * lanes]
    moments = krylov(a0, a1, a2, kx, ky, kz, dinv, dg)
    for k in range(CHIPS):
        sent[k] = moments


def gradient_kernel(got, a0, a1, a2, pot, pred, pred_pair, kept, given, predicted, adj):
    core = lax.axis_index("c")
    moments = got[0]
    for k in range(1, CHIPS):
        moments = moments + got[k]
    weights = weights_of(moments)
    rows, lanes = pot.shape[2], pot.shape[3]
    row_at = lax.broadcasted_iota(jnp.int32, (rows, lanes), 0)
    lane_at = lax.broadcasted_iota(jnp.int32, (rows, lanes), 1)
    predicted[pl.ds(core, 1)] = pred[...][None]
    predicted[pl.ds(1 - core, 1)] = pred_pair[...][None]
    for i in range(6):
        for s in range(2):
            w = [weights[k][s : s + 1, :] for k in range(3)]
            adj[s, i] = w[0] * a0[s, i + 3] + w[1] * a1[s, i + 3] + w[2] * a2[s, i + 3]

    def along(mid_p, mid_a, axis, at):
        last = mid_p.shape[axis] - 1
        next_p = jnp.where(at == last, 0.0, ahead(mid_p, axis))
        next_a = jnp.where(at == last, 0.0, ahead(mid_a, axis))
        upper = (mid_p - next_p) * (mid_a - next_a)
        lower = jnp.where(at == 0, mid_p * mid_a, behind(upper, axis))
        return upper + lower

    for target, first in ((given, 1 + 2 * (1 - core)), (kept, 1 + 2 * core)):
        for j in range(2):
            i = first + j
            sums = [0.0, 0.0, 0.0]
            for s in range(2):
                mid_p, mid_a = pot[s, i], adj[s, i]
                upper = (mid_p - pot[s, i + 1]) * (mid_a - adj[s, i + 1])
                lower = (mid_p - pot[s, i - 1]) * (mid_a - adj[s, i - 1])
                sums[0] = sums[0] + upper + lower
                sums[1] = sums[1] + along(mid_p, mid_a, 0, row_at)
                sums[2] = sums[2] + along(mid_p, mid_a, 1, lane_at)
            for k in range(3):
                target[:, 2 * k + j] = (-0.5 * sums[k]).reshape(target.shape[0], target.shape[2], lanes)


def call(kernel, limit, outs, scratch=()):
    vmem = pl.BlockSpec(memory_space=pltpu.VMEM)

    def run(*args):
        return pl.pallas_call(
            kernel,
            out_shape=tuple(jax.ShapeDtypeStruct(x, kind) for x, kind in outs),
            in_specs=[vmem] * len(args),
            out_specs=tuple([vmem] * len(outs)),
            scratch_shapes=list(scratch),
            compiler_params=pltpu.CompilerParams(vmem_limit_bytes=limit * MEBI),
        )(*args)

    return run


NAMES = ("xh", "y", "xl", "c")


def routes(sizes, move):
    pairs = []
    nx, ny = sizes
    index = lambda h, y, l, c: ((h * ny + y) * 2 + l) * 2 + c
    for h in range(nx):
        for y in range(ny):
            for l in range(2):
                for c in range(2):
                    target = move(h, y, l, c)
                    if target is not None:
                        pairs.append((index(h, y, l, c), index(*target)))
    return pairs


def per_device(high_count, primary, conductivity, observed, receivers):
    chain = CHIPS // 2
    sizes = (high_count, chain)
    def step(by, around):
        def move(h, y, l, c):
            block = 2 * y + l + by
            if block < 0 or block >= CHIPS:
                return None
            side = 2 * h + l
            if around:
                wrap = 1 if (l == 1) else -1
                side = (side + wrap) % (2 * high_count)
                return (side // 2, block // 2, side % 2, c)
            return (h, block // 2, block % 2, c)

        return routes(sizes, move)

    def send(x, pairs):
        return lax.ppermute(x, NAMES, pairs)

    fields = primary[0]
    swap = routes(sizes, lambda h, y, l, c: (h, y, l, 1 - c))
    p_low = send(fields, step(1, False))
    p_high = send(fields, step(-1, False))
    c_low = send(conductivity, step(1, True))
    c_high = send(conductivity, step(-1, True))
    p_pair = send(fields, swap)
    c_pair = send(conductivity, swap)
    c_low_pair = send(c_low, swap)
    c_high_pair = send(c_high, swap)
    p_low_pair = send(p_low, swap)
    p_high_pair = send(p_high, swap)

    rows, lanes = primary.shape[3], primary.shape[4]
    count = receivers.shape[1]
    f32 = lambda *shape: (shape, F32)
    deep = f32(DEEP, rows, lanes)
    pairs = f32(2, DEEP, rows, lanes)
    four = f32(KEPT, rows, lanes)
    p_mid, c_mid, ky_mid, kz_mid, dg_mid, hot, hot_own, p_sample = call(
        own_kernel,
        14,
        [
            f32(2, KEPT, rows, lanes), four, four, four, four,
            ((10 * rows, count), BF16), ((3 * KEPT * rows, count), BF16), f32(2, count),
        ],
        [pltpu.VMEM((2 * lanes, 3 * KEPT * rows), BF16)],
    )(fields, p_pair, conductivity, c_pair, receivers)
    kx, ky, kz, dinv, dg, prim, f0, f1, f2, sent = call(
        forward_kernel,
        20,
        [deep] * 5 + [pairs] * 4 + [f32(CHIPS, 8, count + 128)],
        [
            pltpu.VMEM((DEEP, rows, lanes), F32),
            pltpu.VMEM((6 * lanes, 3 * KEPT * rows), BF16),
            pltpu.VMEM((6, count), F32),
        ],
    )(
        p_mid, p_low, p_low_pair, p_high, p_high_pair,
        c_mid, c_low, c_low_pair, c_high, c_high_pair, ky_mid, kz_mid, dg_mid, receivers, hot_own, p_sample,
    )
    got = lax.all_to_all(sent, ("y", "xl"), 0, 0, tiled=True)
    six = (2, 6, rows, lanes)
    a0, a1, a2, pot, pred, sent = call(
        adjoint_kernel,
        16,
        [pairs] * 3 + [f32(*six), f32(2, count), f32(CHIPS, 8, 128)],
        [pltpu.VMEM((3, 2 * lanes, count), BF16)],
    )(got, observed[0], receivers, hot, kx, ky, kz, dinv, dg, prim, f0, f1, f2)
    pred_pair = send(pred, swap)
    got = lax.all_to_all(sent, ("y", "xl"), 0, 0, tiled=True)
    slabs = lax.axis_size("z")
    chunks = (slabs, 6, rows // slabs, lanes)
    kept, given, predicted = call(
        gradient_kernel, 8, [f32(*chunks), f32(*chunks), f32(2, 2, count)], [pltpu.VMEM(six, F32)]
    )(got, a0, a1, a2, pot, pred, pred_pair)
    total = kept + send(given, swap)
    parts = lax.all_to_all(total, "z", 0, 0, tiled=True)
    share = jnp.sum(parts, axis=0, keepdims=True)
    if high_count > 1:
        share = share + lax.ppermute(share, "xh", [(0, 1), (1, 0)])
    spread = jnp.broadcast_to(share, chunks)
    whole = lax.all_to_all(spread, "z", 0, 0, tiled=True)
    grad = jnp.transpose(whole, (1, 0, 2, 3)).reshape(3, 2, rows, lanes)
    return grad, predicted.reshape(1, 4, count)


def solution(mesh):
    groups = mesh.shape["src"]
    high = 2 if groups > 1 else 1
    devices = mesh.devices.reshape(groups // high, high, CHIPS // 2, 2, 2)
    inner = Mesh(devices, ("z", "xh", "y", "xl", "c"))
    src, dom = ("z", "xh"), ("y", "xl", "c")
    return jax.shard_map(
        functools.partial(per_device, high),
        mesh=inner,
        in_specs=(P(src, None, dom, None, None), P(None, dom, None, None), P(src, None, None), P(src, None)),
        out_specs=(P(None, dom, None, None), P(src, None, None)),
        check_vma=False,
    )
```

```python
import functools
import jax
import jax.numpy as jnp
from jax import lax
from jax.experimental import pallas as pl
from jax.experimental.pallas import tpu as pltpu
from jax.sharding import Mesh, PartitionSpec as P

F32 = jnp.float32
BF16 = jnp.bfloat16
MEBI = 1024 * 1024
DEEP = 12
KEPT = 4
CHIPS = 8


def pieces_of(values):
    first = values.astype(BF16)
    rest = values - first.astype(F32)
    second = rest.astype(BF16)
    third = (rest - second.astype(F32)).astype(BF16)
    return first, second, third


def fold(plane):
    return jnp.sum(plane.reshape(plane.shape[0] // 8, 8, plane.shape[1]), axis=0)


def ahead(plane, axis):
    return pltpu.roll(plane, plane.shape[axis] - 1, axis)


def behind(plane, axis):
    return pltpu.roll(plane, 1, axis)


def neighbours(field, s, i, kx, ky, kz):
    mid = field[s, i]
    total = kx[i] * field[s, i + 1] + kx[i - 1] * field[s, i - 1]
    total = total + ky[i] * ahead(mid, 0) + behind(ky[i] * mid, 0)
    return total + kz[i] * ahead(mid, 1) + behind(kz[i] * mid, 1)


def krylov(t0, t1, t2, kx, ky, kz, dinv, dg):
    sources = t0.shape[0]

    def apply_planes(source, target, first, last):
        def body(i, carry):
            for s in range(sources):
                target[s, i] = source[s, i] - dinv[i] * neighbours(source, s, i, kx, ky, kz)
            return carry

        lax.fori_loop(first, last + 1, body, 0)

    apply_planes(t0, t1, 2, 9)
    apply_planes(t1, t2, 3, 8)

    def body(i, sums):
        sums = list(sums)
        for s in range(sources):
            a0, a1, a2 = t0[s, i], t1[s, i], t2[s, i]
            a3 = a2 - dinv[i] * neighbours(t2, s, i, kx, ky, kz)
            d = dg[i]
            b1 = a0 - a1
            b2 = b1 - (a1 - a2)
            b3 = b2 - ((a1 - a2) - (a2 - a3))
            d0, d1, d2, e1, e2 = d * a0, d * a1, d * a2, d * b1, d * b2
            terms = [
                d0 * a0, d0 * a1, d1 * a1, d1 * a2, d2 * a2, d2 * a3,
                d0 * b1, e1 * b1, e1 * b2, e2 * b2, e2 * b3,
            ]
            for k, term in enumerate(terms):
                sums[k * sources + s] = sums[k * sources + s] + fold(term)
        return tuple(sums)

    zero = jnp.zeros((8, t0.shape[3]), F32)
    sums = lax.fori_loop(4, 8, body, (zero,) * (11 * sources))
    row_at = lax.broadcasted_iota(jnp.int32, (8, 128), 0)
    lane_at = lax.broadcasted_iota(jnp.int32, (8, 128), 1)
    packed = jnp.zeros((8, 128), F32)
    for n, x in enumerate(sums):
        here = jnp.logical_and(row_at == n % sources, lane_at == n // sources)
        packed = jnp.where(here, jnp.sum(x), packed)
    return packed


def weights_of(moments):
    t = [moments[0:2, k : k + 1] for k in range(6)]
    m = [t[0]] + [moments[0:2, k : k + 1] for k in range(6, 11)]
    near = t[1] < 0.5 * t[0]
    g = [jnp.where(near, t[k + 1], m[k] - m[k + 1]) for k in range(5)]
    h = [jnp.where(near, t[k], m[k]) for k in range(3)]
    l1 = g[1] / g[0]
    l2 = g[2] / g[0]
    d1 = g[2] - l1 * g[1]
    e2 = g[3] - l2 * g[1]
    l21 = e2 / d1
    d2 = g[4] - l2 * g[2] - l21 * e2
    y1 = h[1] - l1 * h[0]
    y2 = h[2] - l2 * h[0] - l21 * y1
    c2 = y2 / d2
    c1 = y1 / d1 - l21 * c2
    c0 = h[0] / g[0] - l1 * c1 - l2 * c2
    w0 = jnp.where(near, c0, c0 + c1 + c2)
    w1 = jnp.where(near, c1, -(c1 + 2.0 * c2))
    return w0, w1, c2


def one_hot(count, first, picked):
    place = lax.broadcasted_iota(jnp.int32, (count, picked.shape[1]), 0) + first
    return place == picked


def edges(rows, lanes):
    row_at = lax.broadcasted_iota(jnp.int32, (rows, lanes), 0)
    lane_at = lax.broadcasted_iota(jnp.int32, (rows, lanes), 1)
    mask_y = jnp.where(row_at < rows - 1, 1.0, 0.0).astype(F32)
    mask_z = jnp.where(lane_at < lanes - 1, 1.0, 0.0).astype(F32)
    return row_at, lane_at, mask_y, mask_z


def in_plane(along_y, along_z):
    rows, lanes = along_y.shape
    row_at, lane_at, mask_y, mask_z = edges(rows, lanes)
    up_y = 0.5 * (along_y + ahead(along_y, 0)) * mask_y
    up_z = 0.5 * (along_z + ahead(along_z, 1)) * mask_z
    low_y = jnp.where(row_at == 0, 0.5 * along_y, behind(up_y, 0))
    low_z = jnp.where(lane_at == 0, 0.5 * along_z, behind(up_z, 1))
    top_y = jnp.where(row_at == rows - 1, 0.5 * along_y, up_y)
    top_z = jnp.where(lane_at == lanes - 1, 0.5 * along_z, up_z)
    return up_y, up_z, top_y + low_y + top_z + low_z


def own_kernel(p_own, p_pair, c_own, c_pair, cells, prim, first, ky, kz, plane_dg, hot, hot_own, sample, left):
    block = 2 * lax.axis_index("y") + lax.axis_index("xl")
    core = lax.axis_index("c")
    here = pl.ds(2 * core, 2)
    other = pl.ds(2 - 2 * core, 2)
    prim[:, here] = p_own[here]
    prim[:, other] = p_pair[here]
    first[here] = c_own[0]
    first[other] = c_pair[0]
    rows, lanes = prim.shape[2], prim.shape[3]
    for source, base in ((c_own, 2 * core), (c_pair, 2 - 2 * core)):
        for j in range(2):
            up_y, up_z, part = in_plane(source[1, j], source[2, j])
            ky[base + j] = up_y
            kz[base + j] = up_z
            plane_dg[base + j] = part
    picked = cells[...]
    row_of = picked // lanes
    lane_of = picked - row_of * lanes
    for i in range(10):
        rows_hot = one_hot(rows, (4 * block - 3 + i) * rows, row_of)
        rows_hot = jnp.where(rows_hot, 1.0, 0.0).astype(BF16)
        hot[pl.ds(i * rows, rows)] = rows_hot
        if 3 <= i < 7:
            for piece in range(3):
                hot_own[pl.ds((piece * KEPT + i - 3) * rows, rows)] = rows_hot
    gather([(prim, 0)], left, hot_own, one_hot(lanes, 0, lane_of), sample)


def gather(fields, left, hot_own, lane_hot, sample):
    lanes = lane_hot.shape[0]
    for f, (field, first) in enumerate(fields):
        rows = field.shape[2]
        for s in range(2):
            for j in range(KEPT):
                parts = pieces_of(jnp.transpose(field[s, first + j]))
                for k in range(3):
                    start = (k * KEPT + j) * rows
                    left[pl.ds((2 * f + s) * lanes, lanes), start : start + rows] = parts[k]
    spread = jnp.dot(left[...], hot_own[...], preferred_element_type=F32)
    found = [
        jnp.sum(jnp.where(lane_hot, spread[k * lanes : (k + 1) * lanes], 0.0), axis=0, keepdims=True)
        for k in range(2 * len(fields))
    ]
    sample[...] = jnp.concatenate(found, axis=0)


def forward_kernel(
    p_mid, p_low, p_low_pair, p_high, p_high_pair,
    c_mid, c_low, c_low_pair, c_high, c_high_pair, ky_mid, kz_mid, dg_mid, cells, hot_own, p_sample,
    kx, ky, kz, dinv, dg, prim, t0, t1, t2, sent, cond, left, found,
):
    block = 2 * lax.axis_index("y") + lax.axis_index("xl")
    core = lax.axis_index("c")
    here = pl.ds(2 * core, 2)
    prim[:, 4:8] = p_mid[...]
    cond[4:8] = c_mid[...]
    for base, first, second in ((0, p_low, p_low_pair), (8, p_high, p_high_pair)):
        prim[:, pl.ds(base + 2 * core, 2)] = first[here]
        prim[:, pl.ds(base + 2 - 2 * core, 2)] = second[here]
    for base, first, second in ((0, c_low, c_low_pair), (8, c_high, c_high_pair)):
        cond[pl.ds(base + 2 * core, 2)] = first[0]
        cond[pl.ds(base + 2 - 2 * core, 2)] = second[0]
        for source, start in ((first, base + 2 * core), (second, base + 2 - 2 * core)):
            for j in range(2):
                up_y, up_z, part = in_plane(source[1, j], source[2, j])
                ky[start + j] = up_y
                kz[start + j] = up_z
                dg[start + j] = part
    ky[4:8] = ky_mid[...]
    kz[4:8] = kz_mid[...]
    dg[4:8] = dg_mid[...]
    rows, lanes = prim.shape[2], prim.shape[3]
    row_at, lane_at, mask_y, mask_z = edges(rows, lanes)
    edge = jnp.where(row_at == 0, 0.5, 0.0) + jnp.where(row_at == rows - 1, 0.5, 0.0)
    edge = edge + jnp.where(lane_at == 0, 0.5, 0.0) + jnp.where(lane_at == lanes - 1, 0.5, 0.0)
    unit = (6.0 - edge).astype(F32)
    layers = 4 * CHIPS

    kx[0] = 0.5 * (cond[0] + cond[1])

    def coefficients(i, carry):
        layer = 4 * block - 4 + i
        inside = jnp.where(jnp.logical_and(layer >= 0, layer < layers), 1.0, 0.0).astype(F32)
        first = 0.5 * (cond[i] + cond[i + 1])
        kx[i] = first
        diagonal = first + kx[i - 1] + dg[i]
        inverse = jnp.where(inside > 0.5, 1.0 / diagonal, 0.0)
        dg[i] = diagonal
        dinv[i] = inverse
        return carry

    lax.fori_loop(1, 11, coefficients, 0)

    def right_side(i, carry):
        layer = 4 * block - 4 + i
        outer = jnp.where(jnp.logical_or(layer == 0, layer == layers - 1), 0.5, 0.0).astype(F32)
        diagonal = (unit - outer) - dg[i]
        upper, lower = 1.0 - kx[i], 1.0 - kx[i - 1]
        diff_y = mask_y - ky[i]
        diff_z = mask_z - kz[i]
        inverse = dinv[i]
        for s in range(2):
            mid = prim[s, i]
            total = diagonal * mid - upper * prim[s, i + 1] - lower * prim[s, i - 1]
            total = total - diff_y * ahead(mid, 0) - behind(diff_y * mid, 0)
            total = total - diff_z * ahead(mid, 1) - behind(diff_z * mid, 1)
            t0[s, i] = inverse * total
        return carry

    lax.fori_loop(1, 11, right_side, 0)
    moments = krylov(t0, t1, t2, kx, ky, kz, dinv, dg)

    picked = cells[...]
    lane_of = picked - (picked // lanes) * lanes
    count = picked.shape[1]
    gather([(t0, 4), (t1, 4), (t2, 4)], left, hot_own, one_hot(lanes, 0, lane_of), found)
    for k in range(CHIPS):
        sent[k, 0:2, :count] = p_sample[...]
        sent[k, 2:8, :count] = found[...]
        sent[k, :, count:] = moments


def adjoint_kernel(
    got, observed, cells, hot, kx, ky, kz, dinv, dg, prim, f0, f1, f2,
    b0, b1, b2, pot, predicted, sent, heavy, a0, a1, a2,
):
    core = lax.axis_index("c")
    rows, lanes = prim.shape[2], prim.shape[3]
    count = cells.shape[1]
    total = got[0]
    for k in range(1, CHIPS):
        total = total + got[k]
    weights = weights_of(total[:, count:])
    sample = total[:, :count]
    value = sample[0:2]
    for k in range(3):
        value = value + weights[k] * sample[2 * k + 2 : 2 * k + 4]
    predicted[...] = value
    seen = jnp.where(core == 0, observed[0:2], observed[2:4])
    misfit = value - seen
    for i in range(6):
        for s in range(2):
            w = [weights[k][s : s + 1, :] for k in range(3)]
            pot[s, i] = prim[s, i + 3] + w[0] * f0[s, i + 3] + w[1] * f1[s, i + 3] + w[2] * f2[s, i + 3]

    picked = cells[...]
    lane_of = picked - (picked // lanes) * lanes
    lane_hot = one_hot(lanes, 0, lane_of)
    for s in range(2):
        spread = jnp.where(lane_hot, misfit[s : s + 1], 0.0)
        for k, piece in enumerate(pieces_of(spread)):
            heavy[k, pl.ds(s * lanes, lanes)] = piece
    placed = [
        lax.dot_general(hot[...], heavy[k], (((1,), (1,)), ((), ())), preferred_element_type=F32)
        for k in range(3)
    ]
    source = placed[0] + placed[1] + placed[2]
    for i in range(10):
        inverse = dinv[i + 1]
        for s in range(2):
            a0[s, i + 1] = inverse * source[i * rows : (i + 1) * rows, s * lanes : (s + 1) * lanes]
    moments = krylov(a0, a1, a2, kx, ky, kz, dinv, dg)
    for k in range(CHIPS):
        sent[k] = moments
    for near, deep in ((b0, a0), (b1, a1), (b2, a2)):
        near[...] = deep[:, 3:9]


def gradient_kernel(got, a0, a1, a2, pot, pred, pred_pair, kept, given, predicted, adj):
    core = lax.axis_index("c")
    moments = got[0]
    for k in range(1, CHIPS):
        moments = moments + got[k]
    weights = weights_of(moments)
    rows, lanes = pot.shape[2], pot.shape[3]
    row_at = lax.broadcasted_iota(jnp.int32, (rows, lanes), 0)
    lane_at = lax.broadcasted_iota(jnp.int32, (rows, lanes), 1)
    predicted[pl.ds(core, 1)] = pred[...][None]
    predicted[pl.ds(1 - core, 1)] = pred_pair[...][None]
    for i in range(6):
        for s in range(2):
            w = [weights[k][s : s + 1, :] for k in range(3)]
            adj[s, i] = w[0] * a0[s, i] + w[1] * a1[s, i] + w[2] * a2[s, i]

    def along(mid_p, mid_a, axis, at):
        last = mid_p.shape[axis] - 1
        next_p = jnp.where(at == last, 0.0, ahead(mid_p, axis))
        next_a = jnp.where(at == last, 0.0, ahead(mid_a, axis))
        upper = (mid_p - next_p) * (mid_a - next_a)
        lower = jnp.where(at == 0, mid_p * mid_a, behind(upper, axis))
        return upper + lower

    for target, first in ((given, 1 + 2 * (1 - core)), (kept, 1 + 2 * core)):
        for j in range(2):
            i = first + j
            sums = [0.0, 0.0, 0.0]
            for s in range(2):
                mid_p, mid_a = pot[s, i], adj[s, i]
                upper = (mid_p - pot[s, i + 1]) * (mid_a - adj[s, i + 1])
                lower = (mid_p - pot[s, i - 1]) * (mid_a - adj[s, i - 1])
                sums[0] = sums[0] + upper + lower
                sums[1] = sums[1] + along(mid_p, mid_a, 0, row_at)
                sums[2] = sums[2] + along(mid_p, mid_a, 1, lane_at)
            for k in range(3):
                target[:, 2 * k + j] = (-0.5 * sums[k]).reshape(target.shape[0], target.shape[2], lanes)


def call(kernel, limit, outs, scratch=(), flops=0):
    vmem = pl.BlockSpec(memory_space=pltpu.VMEM)

    def run(*args):
        return pl.pallas_call(
            kernel,
            out_shape=tuple(jax.ShapeDtypeStruct(x, kind) for x, kind in outs),
            in_specs=[vmem] * len(args),
            out_specs=tuple([vmem] * len(outs)),
            scratch_shapes=list(scratch),
            cost_estimate=pl.CostEstimate(flops=flops, bytes_accessed=8 * MEBI, transcendentals=0),
            compiler_params=pltpu.CompilerParams(vmem_limit_bytes=limit * MEBI),
        )(*args)

    return run


NAMES = ("xh", "y", "xl", "c")


def routes(sizes, move):
    pairs = []
    nx, ny = sizes
    index = lambda h, y, l, c: ((h * ny + y) * 2 + l) * 2 + c
    for h in range(nx):
        for y in range(ny):
            for l in range(2):
                for c in range(2):
                    target = move(h, y, l, c)
                    if target is not None:
                        pairs.append((index(h, y, l, c), index(*target)))
    return pairs


def per_device(high_count, primary, conductivity, observed, receivers):
    chain = CHIPS // 2
    sizes = (high_count, chain)
    def step(by, around):
        def move(h, y, l, c):
            block = 2 * y + l + by
            if block < 0 or block >= CHIPS:
                return None
            side = 2 * h + l
            if around:
                wrap = 1 if (l == 1) else -1
                side = (side + wrap) % (2 * high_count)
                return (side // 2, block // 2, side % 2, c)
            return (h, block // 2, block % 2, c)

        return routes(sizes, move)

    def send(x, pairs):
        return lax.ppermute(x, NAMES, pairs)

    fields = primary[0]
    swap = routes(sizes, lambda h, y, l, c: (h, y, l, 1 - c))
    p_low = send(fields, step(1, False))
    p_high = send(fields, step(-1, False))
    c_low = send(conductivity, step(1, True))
    c_high = send(conductivity, step(-1, True))
    p_pair = send(fields, swap)
    c_pair = send(conductivity, swap)

    rows, lanes = primary.shape[3], primary.shape[4]
    count = receivers.shape[1]
    f32 = lambda *shape: (shape, F32)
    deep = f32(DEEP, rows, lanes)
    pairs = f32(2, DEEP, rows, lanes)
    four = f32(KEPT, rows, lanes)
    p_mid, c_mid, ky_mid, kz_mid, dg_mid, hot, hot_own, p_sample = call(
        own_kernel,
        14,
        [
            f32(2, KEPT, rows, lanes), four, four, four, four,
            ((10 * rows, count), BF16), ((3 * KEPT * rows, count), BF16), f32(2, count),
        ],
        [pltpu.VMEM((2 * lanes, 3 * KEPT * rows), BF16)],
        flops=10**10,
    )(fields, p_pair, conductivity, c_pair, receivers)
    c_low, c_high, p_sample = lax.optimization_barrier((c_low, c_high, p_sample))
    c_low_pair, c_high_pair = send(c_low, swap), send(c_high, swap)
    p_low, p_high, p_sample = lax.optimization_barrier((p_low, p_high, p_sample))
    p_low_pair, p_high_pair = send(p_low, swap), send(p_high, swap)
    kx, ky, kz, dinv, dg, prim, f0, f1, f2, sent = call(
        forward_kernel,
        20,
        [deep] * 5 + [pairs] * 4 + [f32(CHIPS, 8, count + 128)],
        [
            pltpu.VMEM((DEEP, rows, lanes), F32),
            pltpu.VMEM((6 * lanes, 3 * KEPT * rows), BF16),
            pltpu.VMEM((6, count), F32),
        ],
    )(
        p_mid, p_low, p_low_pair, p_high, p_high_pair,
        c_mid, c_low, c_low_pair, c_high, c_high_pair, ky_mid, kz_mid, dg_mid, receivers, hot_own, p_sample,
    )
    got = lax.all_to_all(sent, ("y", "xl"), 0, 0, tiled=True)
    six = (2, 6, rows, lanes)
    a0, a1, a2, pot, pred, sent = call(
        adjoint_kernel,
        18,
        [f32(*six)] * 4 + [f32(2, count), f32(CHIPS, 8, 128)],
        [pltpu.VMEM((3, 2 * lanes, count), BF16)] + [pltpu.VMEM((2, DEEP, rows, lanes), F32)] * 3,
    )(got, observed[0], receivers, hot, kx, ky, kz, dinv, dg, prim, f0, f1, f2)
    pred_pair = send(pred, swap)
    got = lax.all_to_all(sent, ("y", "xl"), 0, 0, tiled=True)
    slabs = lax.axis_size("z")
    chunks = (slabs, 6, rows // slabs, lanes)
    kept, given, predicted = call(
        gradient_kernel, 8, [f32(*chunks), f32(*chunks), f32(2, 2, count)], [pltpu.VMEM(six, F32)]
    )(got, a0, a1, a2, pot, pred, pred_pair)
    total = kept + send(given, swap)
    parts = lax.all_to_all(total, "z", 0, 0, tiled=True)
    share = jnp.sum(parts, axis=0, keepdims=True)
    if high_count > 1:
        share = share + lax.ppermute(share, "xh", [(0, 1), (1, 0)])
    spread = jnp.broadcast_to(share, chunks)
    whole = lax.all_to_all(spread, "z", 0, 0, tiled=True)
    grad = jnp.transpose(whole, (1, 0, 2, 3)).reshape(3, 2, rows, lanes)
    return grad, predicted.reshape(1, 4, count)


def solution(mesh):
    groups = mesh.shape["src"]
    high = 2 if groups > 1 else 1
    devices = mesh.devices.reshape(groups // high, high, CHIPS // 2, 2, 2)
    inner = Mesh(devices, ("z", "xh", "y", "xl", "c"))
    src, dom = ("z", "xh"), ("y", "xl", "c")
    return jax.shard_map(
        functools.partial(per_device, high),
        mesh=inner,
        in_specs=(P(src, None, dom, None, None), P(None, dom, None, None), P(src, None, None), P(src, None)),
        out_specs=(P(None, dom, None, None), P(src, None, None)),
        check_vma=False,
    )
```

```python
import functools
import jax
import jax.numpy as jnp
from jax import lax
from jax.experimental import pallas as pl
from jax.experimental.pallas import tpu as pltpu
from jax.sharding import Mesh, PartitionSpec as P

F32 = jnp.float32
BF16 = jnp.bfloat16
MEBI = 1024 * 1024
DEEP = 12
KEPT = 4
CHIPS = 8


def pieces_of(values):
    first = values.astype(BF16)
    rest = values - first.astype(F32)
    second = rest.astype(BF16)
    third = (rest - second.astype(F32)).astype(BF16)
    return first, second, third


def fold(plane):
    return jnp.sum(plane.reshape(plane.shape[0] // 8, 8, plane.shape[1]), axis=0)


def ahead(plane, axis):
    return pltpu.roll(plane, plane.shape[axis] - 1, axis)


def behind(plane, axis):
    return pltpu.roll(plane, 1, axis)


def neighbours(field, s, i, kx, ky, kz):
    mid = field[s, i]
    total = kx[i] * field[s, i + 1] + kx[i - 1] * field[s, i - 1]
    total = total + ky[i] * ahead(mid, 0) + behind(ky[i] * mid, 0)
    return total + kz[i] * ahead(mid, 1) + behind(kz[i] * mid, 1)


def krylov(t0, t1, t2, kx, ky, kz, dinv, dg):
    sources = t0.shape[0]

    def apply_planes(source, target, first, last):
        def body(i, carry):
            for s in range(sources):
                target[s, i] = source[s, i] - dinv[i] * neighbours(source, s, i, kx, ky, kz)
            return carry

        lax.fori_loop(first, last + 1, body, 0)

    apply_planes(t0, t1, 2, 9)
    apply_planes(t1, t2, 3, 8)

    def body(i, sums):
        sums = list(sums)
        for s in range(sources):
            a0, a1, a2 = t0[s, i], t1[s, i], t2[s, i]
            a3 = a2 - dinv[i] * neighbours(t2, s, i, kx, ky, kz)
            d = dg[i]
            b1 = a0 - a1
            b2 = b1 - (a1 - a2)
            b3 = b2 - ((a1 - a2) - (a2 - a3))
            d0, d1, d2, e1, e2 = d * a0, d * a1, d * a2, d * b1, d * b2
            terms = [
                d0 * a0, d0 * a1, d1 * a1, d1 * a2, d2 * a2, d2 * a3,
                d0 * b1, e1 * b1, e1 * b2, e2 * b2, e2 * b3,
            ]
            for k, term in enumerate(terms):
                sums[k * sources + s] = sums[k * sources + s] + fold(term)
        return tuple(sums)

    zero = jnp.zeros((8, t0.shape[3]), F32)
    sums = lax.fori_loop(4, 8, body, (zero,) * (11 * sources))
    row_at = lax.broadcasted_iota(jnp.int32, (8, 128), 0)
    lane_at = lax.broadcasted_iota(jnp.int32, (8, 128), 1)
    packed = jnp.zeros((8, 128), F32)
    for n, x in enumerate(sums):
        here = jnp.logical_and(row_at == n % sources, lane_at == n // sources)
        packed = jnp.where(here, jnp.sum(x), packed)
    return packed


def weights_of(moments):
    t = [moments[0:2, k : k + 1] for k in range(6)]
    m = [t[0]] + [moments[0:2, k : k + 1] for k in range(6, 11)]
    near = t[1] < 0.5 * t[0]
    g = [jnp.where(near, t[k + 1], m[k] - m[k + 1]) for k in range(5)]
    h = [jnp.where(near, t[k], m[k]) for k in range(3)]
    l1 = g[1] / g[0]
    l2 = g[2] / g[0]
    d1 = g[2] - l1 * g[1]
    e2 = g[3] - l2 * g[1]
    l21 = e2 / d1
    d2 = g[4] - l2 * g[2] - l21 * e2
    y1 = h[1] - l1 * h[0]
    y2 = h[2] - l2 * h[0] - l21 * y1
    c2 = y2 / d2
    c1 = y1 / d1 - l21 * c2
    c0 = h[0] / g[0] - l1 * c1 - l2 * c2
    w0 = jnp.where(near, c0, c0 + c1 + c2)
    w1 = jnp.where(near, c1, -(c1 + 2.0 * c2))
    return w0, w1, c2


def one_hot(count, first, picked):
    place = lax.broadcasted_iota(jnp.int32, (count, picked.shape[1]), 0) + first
    return place == picked


def edges(rows, lanes):
    row_at = lax.broadcasted_iota(jnp.int32, (rows, lanes), 0)
    lane_at = lax.broadcasted_iota(jnp.int32, (rows, lanes), 1)
    mask_y = jnp.where(row_at < rows - 1, 1.0, 0.0).astype(F32)
    mask_z = jnp.where(lane_at < lanes - 1, 1.0, 0.0).astype(F32)
    return row_at, lane_at, mask_y, mask_z


def in_plane(along_y, along_z):
    rows, lanes = along_y.shape
    row_at, lane_at, mask_y, mask_z = edges(rows, lanes)
    up_y = 0.5 * (along_y + ahead(along_y, 0)) * mask_y
    up_z = 0.5 * (along_z + ahead(along_z, 1)) * mask_z
    low_y = jnp.where(row_at == 0, 0.5 * along_y, behind(up_y, 0))
    low_z = jnp.where(lane_at == 0, 0.5 * along_z, behind(up_z, 1))
    top_y = jnp.where(row_at == rows - 1, 0.5 * along_y, up_y)
    top_z = jnp.where(lane_at == lanes - 1, 0.5 * along_z, up_z)
    return up_y, up_z, top_y + low_y + top_z + low_z


def own_kernel(p_own, p_pair, c_own, c_pair, cells, prim, first, ky, kz, plane_dg, hot, hot_own, sample, left):
    block = 2 * lax.axis_index("y") + lax.axis_index("xl")
    core = lax.axis_index("c")
    here = pl.ds(2 * core, 2)
    other = pl.ds(2 - 2 * core, 2)
    prim[:, here] = p_own[here]
    prim[:, other] = p_pair[here]
    first[here] = c_own[0]
    first[other] = c_pair[0]
    rows, lanes = prim.shape[2], prim.shape[3]
    for source, base in ((c_own, 2 * core), (c_pair, 2 - 2 * core)):
        for j in range(2):
            up_y, up_z, part = in_plane(source[1, j], source[2, j])
            ky[base + j] = up_y
            kz[base + j] = up_z
            plane_dg[base + j] = part
    picked = cells[...]
    row_of = picked // lanes
    lane_of = picked - row_of * lanes
    for i in range(10):
        rows_hot = one_hot(rows, (4 * block - 3 + i) * rows, row_of)
        rows_hot = jnp.where(rows_hot, 1.0, 0.0).astype(BF16)
        hot[pl.ds(i * rows, rows)] = rows_hot
        if 3 <= i < 7:
            for piece in range(3):
                hot_own[pl.ds((piece * KEPT + i - 3) * rows, rows)] = rows_hot
    gather([(prim, 0)], left, hot_own, one_hot(lanes, 0, lane_of), sample)


def gather(fields, left, hot_own, lane_hot, sample):
    lanes = lane_hot.shape[0]
    for f, (field, first) in enumerate(fields):
        rows = field.shape[2]
        for s in range(2):
            for j in range(KEPT):
                parts = pieces_of(jnp.transpose(field[s, first + j]))
                for k in range(3):
                    start = (k * KEPT + j) * rows
                    left[pl.ds((2 * f + s) * lanes, lanes), start : start + rows] = parts[k]
    spread = jnp.dot(left[...], hot_own[...], preferred_element_type=F32)
    found = [
        jnp.sum(jnp.where(lane_hot, spread[k * lanes : (k + 1) * lanes], 0.0), axis=0, keepdims=True)
        for k in range(2 * len(fields))
    ]
    sample[...] = jnp.concatenate(found, axis=0)


def forward_kernel(
    p_mid, p_low, p_low_pair, p_high, p_high_pair,
    c_mid, c_low, c_low_pair, c_high, c_high_pair, ky_mid, kz_mid, dg_mid, cells, hot_own, p_sample,
    kx, ky, kz, dinv, dg, prim, t0, t1, t2, sent, cond, left, found,
):
    block = 2 * lax.axis_index("y") + lax.axis_index("xl")
    core = lax.axis_index("c")
    here = pl.ds(2 * core, 2)
    prim[:, 4:8] = p_mid[...]
    cond[4:8] = c_mid[...]
    for base, first, second in ((0, p_low, p_low_pair), (8, p_high, p_high_pair)):
        prim[:, pl.ds(base + 2 * core, 2)] = first[here]
        prim[:, pl.ds(base + 2 - 2 * core, 2)] = second[here]
    for base, first, second in ((0, c_low, c_low_pair), (8, c_high, c_high_pair)):
        cond[pl.ds(base + 2 * core, 2)] = first[0]
        cond[pl.ds(base + 2 - 2 * core, 2)] = second[0]
        for source, start in ((first, base + 2 * core), (second, base + 2 - 2 * core)):
            for j in range(2):
                up_y, up_z, part = in_plane(source[1, j], source[2, j])
                ky[start + j] = up_y
                kz[start + j] = up_z
                dg[start + j] = part
    ky[4:8] = ky_mid[...]
    kz[4:8] = kz_mid[...]
    dg[4:8] = dg_mid[...]
    rows, lanes = prim.shape[2], prim.shape[3]
    row_at, lane_at, mask_y, mask_z = edges(rows, lanes)
    edge = jnp.where(row_at == 0, 0.5, 0.0) + jnp.where(row_at == rows - 1, 0.5, 0.0)
    edge = edge + jnp.where(lane_at == 0, 0.5, 0.0) + jnp.where(lane_at == lanes - 1, 0.5, 0.0)
    unit = (6.0 - edge).astype(F32)
    layers = 4 * CHIPS

    kx[0] = 0.5 * (cond[0] + cond[1])

    def coefficients(i, carry):
        layer = 4 * block - 4 + i
        inside = jnp.where(jnp.logical_and(layer >= 0, layer < layers), 1.0, 0.0).astype(F32)
        first = 0.5 * (cond[i] + cond[i + 1])
        kx[i] = first
        diagonal = first + kx[i - 1] + dg[i]
        inverse = jnp.where(inside > 0.5, 1.0 / diagonal, 0.0)
        dg[i] = diagonal
        dinv[i] = inverse
        return carry

    lax.fori_loop(1, 11, coefficients, 0)

    def right_side(i, carry):
        layer = 4 * block - 4 + i
        outer = jnp.where(jnp.logical_or(layer == 0, layer == layers - 1), 0.5, 0.0).astype(F32)
        diagonal = (unit - outer) - dg[i]
        upper, lower = 1.0 - kx[i], 1.0 - kx[i - 1]
        diff_y = mask_y - ky[i]
        diff_z = mask_z - kz[i]
        inverse = dinv[i]
        for s in range(2):
            mid = prim[s, i]
            total = diagonal * mid - upper * prim[s, i + 1] - lower * prim[s, i - 1]
            total = total - diff_y * ahead(mid, 0) - behind(diff_y * mid, 0)
            total = total - diff_z * ahead(mid, 1) - behind(diff_z * mid, 1)
            t0[s, i] = inverse * total
        return carry

    lax.fori_loop(1, 11, right_side, 0)
    moments = krylov(t0, t1, t2, kx, ky, kz, dinv, dg)

    picked = cells[...]
    lane_of = picked - (picked // lanes) * lanes
    count = picked.shape[1]
    gather([(t0, 4), (t1, 4), (t2, 4)], left, hot_own, one_hot(lanes, 0, lane_of), found)
    for k in range(CHIPS):
        sent[k, 0:2, :count] = p_sample[...]
        sent[k, 2:8, :count] = found[...]
        sent[k, :, count:] = moments


def adjoint_kernel(
    got, observed, cells, hot, kx, ky, kz, dinv, dg, prim, f0, f1, f2,
    b0, b1, b2, pot, predicted, sent, heavy, a0, a1, a2,
):
    core = lax.axis_index("c")
    rows, lanes = prim.shape[2], prim.shape[3]
    count = cells.shape[1]
    total = got[0]
    for k in range(1, CHIPS):
        total = total + got[k]
    weights = weights_of(total[:, count:])
    sample = total[:, :count]
    value = sample[0:2]
    for k in range(3):
        value = value + weights[k] * sample[2 * k + 2 : 2 * k + 4]
    predicted[...] = value
    seen = jnp.where(core == 0, observed[0:2], observed[2:4])
    misfit = value - seen
    for i in range(6):
        for s in range(2):
            w = [weights[k][s : s + 1, :] for k in range(3)]
            pot[s, i] = prim[s, i + 3] + w[0] * f0[s, i + 3] + w[1] * f1[s, i + 3] + w[2] * f2[s, i + 3]

    picked = cells[...]
    lane_of = picked - (picked // lanes) * lanes
    lane_hot = one_hot(lanes, 0, lane_of)
    for s in range(2):
        spread = jnp.where(lane_hot, misfit[s : s + 1], 0.0)
        for k, piece in enumerate(pieces_of(spread)):
            heavy[k, pl.ds(s * lanes, lanes)] = piece
    placed = [
        lax.dot_general(hot[...], heavy[k], (((1,), (1,)), ((), ())), preferred_element_type=F32)
        for k in range(3)
    ]
    source = placed[0] + placed[1] + placed[2]
    for i in range(10):
        inverse = dinv[i + 1]
        for s in range(2):
            a0[s, i + 1] = inverse * source[i * rows : (i + 1) * rows, s * lanes : (s + 1) * lanes]
    moments = krylov(a0, a1, a2, kx, ky, kz, dinv, dg)
    for k in range(CHIPS):
        sent[k] = moments
    for near, deep in ((b0, a0), (b1, a1), (b2, a2)):
        near[...] = deep[:, 3:9]


def gradient_kernel(got, a0, a1, a2, pot, kept, given, adj):
    core = lax.axis_index("c")
    moments = got[0]
    for k in range(1, CHIPS):
        moments = moments + got[k]
    weights = weights_of(moments)
    rows, lanes = pot.shape[2], pot.shape[3]
    row_at = lax.broadcasted_iota(jnp.int32, (rows, lanes), 0)
    lane_at = lax.broadcasted_iota(jnp.int32, (rows, lanes), 1)
    for i in range(6):
        for s in range(2):
            w = [weights[k][s : s + 1, :] for k in range(3)]
            adj[s, i] = w[0] * a0[s, i] + w[1] * a1[s, i] + w[2] * a2[s, i]

    def along(mid_p, mid_a, axis, at):
        last = mid_p.shape[axis] - 1
        next_p = jnp.where(at == last, 0.0, ahead(mid_p, axis))
        next_a = jnp.where(at == last, 0.0, ahead(mid_a, axis))
        upper = (mid_p - next_p) * (mid_a - next_a)
        lower = jnp.where(at == 0, mid_p * mid_a, behind(upper, axis))
        return upper + lower

    for target, first in ((given, 1 + 2 * (1 - core)), (kept, 1 + 2 * core)):
        for j in range(2):
            i = first + j
            sums = [0.0, 0.0, 0.0]
            for s in range(2):
                mid_p, mid_a = pot[s, i], adj[s, i]
                upper = (mid_p - pot[s, i + 1]) * (mid_a - adj[s, i + 1])
                lower = (mid_p - pot[s, i - 1]) * (mid_a - adj[s, i - 1])
                sums[0] = sums[0] + upper + lower
                sums[1] = sums[1] + along(mid_p, mid_a, 0, row_at)
                sums[2] = sums[2] + along(mid_p, mid_a, 1, lane_at)
            for k in range(3):
                target[:, 2 * k + j] = (-0.5 * sums[k]).reshape(target.shape[0], target.shape[2], lanes)


def call(kernel, limit, outs, scratch=()):
    vmem = pl.BlockSpec(memory_space=pltpu.VMEM)

    def run(*args):
        return pl.pallas_call(
            kernel,
            out_shape=tuple(jax.ShapeDtypeStruct(x, kind) for x, kind in outs),
            in_specs=[vmem] * len(args),
            out_specs=tuple([vmem] * len(outs)),
            scratch_shapes=list(scratch),
            compiler_params=pltpu.CompilerParams(vmem_limit_bytes=limit * MEBI),
        )(*args)

    return run


NAMES = ("xh", "y", "xl", "c")


def routes(sizes, move):
    pairs = []
    nx, ny = sizes
    index = lambda h, y, l, c: ((h * ny + y) * 2 + l) * 2 + c
    for h in range(nx):
        for y in range(ny):
            for l in range(2):
                for c in range(2):
                    target = move(h, y, l, c)
                    if target is not None:
                        pairs.append((index(h, y, l, c), index(*target)))
    return pairs


def per_device(high_count, primary, conductivity, observed, receivers):
    chain = CHIPS // 2
    sizes = (high_count, chain)
    def step(by, around):
        def move(h, y, l, c):
            block = 2 * y + l + by
            if block < 0 or block >= CHIPS:
                return None
            side = 2 * h + l
            if around:
                wrap = 1 if (l == 1) else -1
                side = (side + wrap) % (2 * high_count)
                return (side // 2, block // 2, side % 2, c)
            return (h, block // 2, block % 2, c)

        return routes(sizes, move)

    def send(x, pairs):
        return lax.ppermute(x, NAMES, pairs)

    fields = primary[0]
    swap = routes(sizes, lambda h, y, l, c: (h, y, l, 1 - c))
    p_low = send(fields, step(1, False))
    p_high = send(fields, step(-1, False))
    c_low = send(conductivity, step(1, True))
    c_high = send(conductivity, step(-1, True))
    p_pair = send(fields, swap)
    c_pair = send(conductivity, swap)

    rows, lanes = primary.shape[3], primary.shape[4]
    count = receivers.shape[1]
    f32 = lambda *shape: (shape, F32)
    deep = f32(DEEP, rows, lanes)
    pairs = f32(2, DEEP, rows, lanes)
    four = f32(KEPT, rows, lanes)
    p_mid, c_mid, ky_mid, kz_mid, dg_mid, hot, hot_own, p_sample = call(
        own_kernel,
        14,
        [
            f32(2, KEPT, rows, lanes), four, four, four, four,
            ((10 * rows, count), BF16), ((3 * KEPT * rows, count), BF16), f32(2, count),
        ],
        [pltpu.VMEM((2 * lanes, 3 * KEPT * rows), BF16)],
    )(fields, p_pair, conductivity, c_pair, receivers)
    c_low, c_high, p_sample = lax.optimization_barrier((c_low, c_high, p_sample))
    c_low_pair, c_high_pair = send(c_low, swap), send(c_high, swap)
    p_low, p_high, p_sample = lax.optimization_barrier((p_low, p_high, p_sample))
    p_low_pair, p_high_pair = send(p_low, swap), send(p_high, swap)
    kx, ky, kz, dinv, dg, prim, f0, f1, f2, sent = call(
        forward_kernel,
        20,
        [deep] * 5 + [pairs] * 4 + [f32(CHIPS, 8, count + 128)],
        [
            pltpu.VMEM((DEEP, rows, lanes), F32),
            pltpu.VMEM((6 * lanes, 3 * KEPT * rows), BF16),
            pltpu.VMEM((6, count), F32),
        ],
    )(
        p_mid, p_low, p_low_pair, p_high, p_high_pair,
        c_mid, c_low, c_low_pair, c_high, c_high_pair, ky_mid, kz_mid, dg_mid, receivers, hot_own, p_sample,
    )
    got = lax.all_to_all(sent, ("y", "xl"), 0, 0, tiled=True)
    six = (2, 6, rows, lanes)
    a0, a1, a2, pot, pred, sent = call(
        adjoint_kernel,
        18,
        [f32(*six)] * 4 + [f32(2, count), f32(CHIPS, 8, 128)],
        [pltpu.VMEM((3, 2 * lanes, count), BF16)] + [pltpu.VMEM((2, DEEP, rows, lanes), F32)] * 3,
    )(got, observed[0], receivers, hot, kx, ky, kz, dinv, dg, prim, f0, f1, f2)
    got = lax.all_to_all(sent, ("y", "xl"), 0, 0, tiled=True)
    slabs = lax.axis_size("z")
    chunks = (slabs, 6, rows // slabs, lanes)
    kept, given = call(gradient_kernel, 8, [f32(*chunks)] * 2, [pltpu.VMEM(six, F32)])(got, a0, a1, a2, pot)
    given, pred = lax.optimization_barrier((given, pred))
    total = kept + send(given, swap)
    pred_pair = send(pred, swap)
    even = lax.axis_index("c") == 0
    predicted = jnp.where(even, jnp.concatenate([pred, pred_pair]), jnp.concatenate([pred_pair, pred]))
    parts = lax.all_to_all(total, "z", 0, 0, tiled=True)
    share = jnp.sum(parts, axis=0, keepdims=True)
    if high_count > 1:
        share = share + lax.ppermute(share, "xh", [(0, 1), (1, 0)])
    spread = jnp.broadcast_to(share, chunks)
    whole = lax.all_to_all(spread, "z", 0, 0, tiled=True)
    grad = jnp.transpose(whole, (1, 0, 2, 3)).reshape(3, 2, rows, lanes)
    return grad, predicted[None]


def solution(mesh):
    groups = mesh.shape["src"]
    high = 2 if groups > 1 else 1
    devices = mesh.devices.reshape(groups // high, high, CHIPS // 2, 2, 2)
    inner = Mesh(devices, ("z", "xh", "y", "xl", "c"))
    src, dom = ("z", "xh"), ("y", "xl", "c")
    return jax.shard_map(
        functools.partial(per_device, high),
        mesh=inner,
        in_specs=(P(src, None, dom, None, None), P(None, dom, None, None), P(src, None, None), P(src, None)),
        out_specs=(P(None, dom, None, None), P(src, None, None)),
        check_vma=False,
    )
```

```python
import functools
import jax
import jax.numpy as jnp
from jax import lax
from jax.experimental import pallas as pl
from jax.experimental.pallas import tpu as pltpu
from jax.sharding import Mesh, PartitionSpec as P

F32 = jnp.float32
BF16 = jnp.bfloat16
MEBI = 1024 * 1024
DEEP = 12
KEPT = 4
CHIPS = 8
LANES = 128


def pieces_of(values):
    first = values.astype(BF16)
    rest = values - first.astype(F32)
    second = rest.astype(BF16)
    third = (rest - second.astype(F32)).astype(BF16)
    return first, second, third


def fold(plane):
    return jnp.sum(plane.reshape(plane.shape[0] // 8, 8, plane.shape[1]), axis=0)


def ahead(plane, axis):
    return pltpu.roll(plane, plane.shape[axis] - 1, axis)


def behind(plane, axis):
    return pltpu.roll(plane, 1, axis)


def neighbours(field, s, i, kx, ky, kz):
    mid = field[s, i]
    total = kx[i] * field[s, i + 1] + kx[i - 1] * field[s, i - 1]
    total = total + ky[i] * ahead(mid, 0) + behind(ky[i] * mid, 0)
    return total + kz[i] * ahead(mid, 1) + behind(kz[i] * mid, 1)


def krylov(t0, t1, t2, kx, ky, kz, dinv, dg):
    sources = t0.shape[0]

    def apply_planes(source, target, first, last):
        def body(i, carry):
            for s in range(sources):
                target[s, i] = source[s, i] - dinv[i] * neighbours(source, s, i, kx, ky, kz)
            return carry

        lax.fori_loop(first, last + 1, body, 0, unroll=True)

    apply_planes(t0, t1, 2, 9)
    apply_planes(t1, t2, 3, 8)

    def body(i, sums):
        sums = list(sums)
        for s in range(sources):
            a0, a1, a2 = t0[s, i], t1[s, i], t2[s, i]
            a3 = a2 - dinv[i] * neighbours(t2, s, i, kx, ky, kz)
            d = dg[i]
            b1 = a0 - a1
            b2 = b1 - (a1 - a2)
            b3 = b2 - ((a1 - a2) - (a2 - a3))
            d0, d1, d2, e1, e2 = d * a0, d * a1, d * a2, d * b1, d * b2
            terms = [
                d0 * a0, d0 * a1, d1 * a1, d1 * a2, d2 * a2, d2 * a3,
                d0 * b1, e1 * b1, e1 * b2, e2 * b2, e2 * b3,
            ]
            for k, term in enumerate(terms):
                sums[k * sources + s] = sums[k * sources + s] + fold(term)
        return tuple(sums)

    zero = jnp.zeros((8, t0.shape[3]), F32)
    sums = lax.fori_loop(4, 8, body, (zero,) * (11 * sources), unroll=True)
    row_at = lax.broadcasted_iota(jnp.int32, (8, 128), 0)
    lane_at = lax.broadcasted_iota(jnp.int32, (8, 128), 1)
    packed = jnp.zeros((8, 128), F32)
    for n, x in enumerate(sums):
        here = jnp.logical_and(row_at == n % sources, lane_at == n // sources)
        packed = jnp.where(here, jnp.sum(x), packed)
    return packed


def weights_of(moments):
    t = [moments[0:2, k : k + 1] for k in range(6)]
    m = [t[0]] + [moments[0:2, k : k + 1] for k in range(6, 11)]
    near = t[1] < 0.5 * t[0]
    g = [jnp.where(near, t[k + 1], m[k] - m[k + 1]) for k in range(5)]
    h = [jnp.where(near, t[k], m[k]) for k in range(3)]
    l1 = g[1] / g[0]
    l2 = g[2] / g[0]
    d1 = g[2] - l1 * g[1]
    e2 = g[3] - l2 * g[1]
    l21 = e2 / d1
    d2 = g[4] - l2 * g[2] - l21 * e2
    y1 = h[1] - l1 * h[0]
    y2 = h[2] - l2 * h[0] - l21 * y1
    c2 = y2 / d2
    c1 = y1 / d1 - l21 * c2
    c0 = h[0] / g[0] - l1 * c1 - l2 * c2
    w0 = jnp.where(near, c0, c0 + c1 + c2)
    w1 = jnp.where(near, c1, -(c1 + 2.0 * c2))
    return w0, w1, c2


def one_hot(count, first, picked):
    place = lax.broadcasted_iota(jnp.int32, (count, picked.shape[1]), 0) + first
    return place == picked


def edges(rows, lanes):
    row_at = lax.broadcasted_iota(jnp.int32, (rows, lanes), 0)
    lane_at = lax.broadcasted_iota(jnp.int32, (rows, lanes), 1)
    mask_y = jnp.where(row_at < rows - 1, 1.0, 0.0).astype(F32)
    mask_z = jnp.where(lane_at < lanes - 1, 1.0, 0.0).astype(F32)
    return row_at, lane_at, mask_y, mask_z


def in_plane(along_y, along_z):
    rows, lanes = along_y.shape
    row_at, lane_at, mask_y, mask_z = edges(rows, lanes)
    up_y = 0.5 * (along_y + ahead(along_y, 0)) * mask_y
    up_z = 0.5 * (along_z + ahead(along_z, 1)) * mask_z
    low_y = jnp.where(row_at == 0, 0.5 * along_y, behind(up_y, 0))
    low_z = jnp.where(lane_at == 0, 0.5 * along_z, behind(up_z, 1))
    top_y = jnp.where(row_at == rows - 1, 0.5 * along_y, up_y)
    top_z = jnp.where(lane_at == lanes - 1, 0.5 * along_z, up_z)
    return up_y, up_z, top_y + low_y + top_z + low_z


def hot_kernel(cells, hot, hot_own):
    block = 2 * lax.axis_index("y") + lax.axis_index("xl")
    rows = hot.shape[0] // 10
    row_of = cells[...] // LANES
    for i in range(10):
        rows_hot = one_hot(rows, (4 * block - 3 + i) * rows, row_of)
        rows_hot = jnp.where(rows_hot, 1.0, 0.0).astype(BF16)
        hot[pl.ds(i * rows, rows)] = rows_hot
        if 3 <= i < 7:
            for piece in range(3):
                hot_own[pl.ds((piece * KEPT + i - 3) * rows, rows)] = rows_hot


def own_kernel(p_own, p_pair, c_own, c_pair, cells, hot_own, prim, first, ky, kz, plane_dg, sample, left):
    core = lax.axis_index("c")
    here = pl.ds(2 * core, 2)
    other = pl.ds(2 - 2 * core, 2)
    prim[:, here] = p_own[here]
    prim[:, other] = p_pair[here]
    first[here] = c_own[0]
    first[other] = c_pair[0]
    rows, lanes = prim.shape[2], prim.shape[3]
    for source, base in ((c_own, 2 * core), (c_pair, 2 - 2 * core)):
        for j in range(2):
            up_y, up_z, part = in_plane(source[1, j], source[2, j])
            ky[base + j] = up_y
            kz[base + j] = up_z
            plane_dg[base + j] = part
    picked = cells[...]
    lane_of = picked - (picked // lanes) * lanes
    gather([(prim, 0)], left, hot_own, one_hot(lanes, 0, lane_of), sample)


def gather(fields, left, hot_own, lane_hot, sample):
    lanes = lane_hot.shape[0]
    for f, (field, first) in enumerate(fields):
        rows = field.shape[2]
        for s in range(2):
            for j in range(KEPT):
                parts = pieces_of(jnp.transpose(field[s, first + j]))
                for k in range(3):
                    start = (k * KEPT + j) * rows
                    left[pl.ds((2 * f + s) * lanes, lanes), start : start + rows] = parts[k]
    spread = jnp.dot(left[...], hot_own[...], preferred_element_type=F32)
    found = [
        jnp.sum(jnp.where(lane_hot, spread[k * lanes : (k + 1) * lanes], 0.0), axis=0, keepdims=True)
        for k in range(2 * len(fields))
    ]
    sample[...] = jnp.concatenate(found, axis=0)


def forward_kernel(
    p_mid, p_low, p_low_pair, p_high, p_high_pair,
    c_mid, c_low, c_low_pair, c_high, c_high_pair, ky_mid, kz_mid, dg_mid, cells, hot_own, p_sample,
    kx, ky, kz, dinv, dg, prim, t0, t1, t2, sent, cond, left, found,
):
    block = 2 * lax.axis_index("y") + lax.axis_index("xl")
    core = lax.axis_index("c")
    here = pl.ds(2 * core, 2)
    prim[:, 4:8] = p_mid[...]
    cond[4:8] = c_mid[...]
    for base, first, second in ((0, p_low, p_low_pair), (8, p_high, p_high_pair)):
        prim[:, pl.ds(base + 2 * core, 2)] = first[here]
        prim[:, pl.ds(base + 2 - 2 * core, 2)] = second[here]
    for base, first, second in ((0, c_low, c_low_pair), (8, c_high, c_high_pair)):
        cond[pl.ds(base + 2 * core, 2)] = first[0]
        cond[pl.ds(base + 2 - 2 * core, 2)] = second[0]
        for source, start in ((first, base + 2 * core), (second, base + 2 - 2 * core)):
            for j in range(2):
                up_y, up_z, part = in_plane(source[1, j], source[2, j])
                ky[start + j] = up_y
                kz[start + j] = up_z
                dg[start + j] = part
    ky[4:8] = ky_mid[...]
    kz[4:8] = kz_mid[...]
    dg[4:8] = dg_mid[...]
    rows, lanes = prim.shape[2], prim.shape[3]
    row_at, lane_at, mask_y, mask_z = edges(rows, lanes)
    edge = jnp.where(row_at == 0, 0.5, 0.0) + jnp.where(row_at == rows - 1, 0.5, 0.0)
    edge = edge + jnp.where(lane_at == 0, 0.5, 0.0) + jnp.where(lane_at == lanes - 1, 0.5, 0.0)
    unit = (6.0 - edge).astype(F32)
    layers = 4 * CHIPS

    kx[0] = 0.5 * (cond[0] + cond[1])

    def coefficients(i, carry):
        layer = 4 * block - 4 + i
        inside = jnp.where(jnp.logical_and(layer >= 0, layer < layers), 1.0, 0.0).astype(F32)
        first = 0.5 * (cond[i] + cond[i + 1])
        kx[i] = first
        diagonal = first + kx[i - 1] + dg[i]
        inverse = jnp.where(inside > 0.5, 1.0 / diagonal, 0.0)
        dg[i] = diagonal
        dinv[i] = inverse
        return carry

    lax.fori_loop(1, 11, coefficients, 0)

    def right_side(i, carry):
        layer = 4 * block - 4 + i
        outer = jnp.where(jnp.logical_or(layer == 0, layer == layers - 1), 0.5, 0.0).astype(F32)
        diagonal = (unit - outer) - dg[i]
        upper, lower = 1.0 - kx[i], 1.0 - kx[i - 1]
        diff_y = mask_y - ky[i]
        diff_z = mask_z - kz[i]
        inverse = dinv[i]
        for s in range(2):
            mid = prim[s, i]
            total = diagonal * mid - upper * prim[s, i + 1] - lower * prim[s, i - 1]
            total = total - diff_y * ahead(mid, 0) - behind(diff_y * mid, 0)
            total = total - diff_z * ahead(mid, 1) - behind(diff_z * mid, 1)
            t0[s, i] = inverse * total
        return carry

    lax.fori_loop(1, 11, right_side, 0, unroll=True)
    moments = krylov(t0, t1, t2, kx, ky, kz, dinv, dg)

    picked = cells[...]
    lane_of = picked - (picked // lanes) * lanes
    count = picked.shape[1]
    gather([(t0, 4), (t1, 4), (t2, 4)], left, hot_own, one_hot(lanes, 0, lane_of), found)
    for k in range(CHIPS):
        sent[k, 0:2, :count] = p_sample[...]
        sent[k, 2:8, :count] = found[...]
        sent[k, :, count:] = moments


def adjoint_kernel(
    got, observed, cells, hot, kx, ky, kz, dinv, dg, prim, f0, f1, f2,
    b0, b1, b2, pot, predicted, sent, heavy, a0, a1, a2,
):
    core = lax.axis_index("c")
    rows, lanes = prim.shape[2], prim.shape[3]
    count = cells.shape[1]
    total = got[0]
    for k in range(1, CHIPS):
        total = total + got[k]
    weights = weights_of(total[:, count:])
    sample = total[:, :count]
    value = sample[0:2]
    for k in range(3):
        value = value + weights[k] * sample[2 * k + 2 : 2 * k + 4]
    predicted[...] = value
    seen = jnp.where(core == 0, observed[0:2], observed[2:4])
    misfit = value - seen
    for i in range(6):
        for s in range(2):
            w = [weights[k][s : s + 1, :] for k in range(3)]
            pot[s, i] = prim[s, i + 3] + w[0] * f0[s, i + 3] + w[1] * f1[s, i + 3] + w[2] * f2[s, i + 3]

    picked = cells[...]
    lane_of = picked - (picked // lanes) * lanes
    lane_hot = one_hot(lanes, 0, lane_of)
    for s in range(2):
        spread = jnp.where(lane_hot, misfit[s : s + 1], 0.0)
        for k, piece in enumerate(pieces_of(spread)):
            heavy[k, pl.ds(s * lanes, lanes)] = piece
    placed = [
        lax.dot_general(hot[...], heavy[k], (((1,), (1,)), ((), ())), preferred_element_type=F32)
        for k in range(3)
    ]
    source = placed[0] + placed[1] + placed[2]
    for i in range(10):
        inverse = dinv[i + 1]
        for s in range(2):
            a0[s, i + 1] = inverse * source[i * rows : (i + 1) * rows, s * lanes : (s + 1) * lanes]
    moments = krylov(a0, a1, a2, kx, ky, kz, dinv, dg)
    for k in range(CHIPS):
        sent[k] = moments
    for near, deep in ((b0, a0), (b1, a1), (b2, a2)):
        near[...] = deep[:, 3:9]


def gradient_kernel(got, a0, a1, a2, pot, kept, given, adj):
    core = lax.axis_index("c")
    moments = got[0]
    for k in range(1, CHIPS):
        moments = moments + got[k]
    weights = weights_of(moments)
    rows, lanes = pot.shape[2], pot.shape[3]
    row_at = lax.broadcasted_iota(jnp.int32, (rows, lanes), 0)
    lane_at = lax.broadcasted_iota(jnp.int32, (rows, lanes), 1)
    for i in range(6):
        for s in range(2):
            w = [weights[k][s : s + 1, :] for k in range(3)]
            adj[s, i] = w[0] * a0[s, i] + w[1] * a1[s, i] + w[2] * a2[s, i]

    def along(mid_p, mid_a, axis, at):
        last = mid_p.shape[axis] - 1
        next_p = jnp.where(at == last, 0.0, ahead(mid_p, axis))
        next_a = jnp.where(at == last, 0.0, ahead(mid_a, axis))
        upper = (mid_p - next_p) * (mid_a - next_a)
        lower = jnp.where(at == 0, mid_p * mid_a, behind(upper, axis))
        return upper + lower

    for target, first in ((given, 1 + 2 * (1 - core)), (kept, 1 + 2 * core)):
        for j in range(2):
            i = first + j
            sums = [0.0, 0.0, 0.0]
            for s in range(2):
                mid_p, mid_a = pot[s, i], adj[s, i]
                upper = (mid_p - pot[s, i + 1]) * (mid_a - adj[s, i + 1])
                lower = (mid_p - pot[s, i - 1]) * (mid_a - adj[s, i - 1])
                sums[0] = sums[0] + upper + lower
                sums[1] = sums[1] + along(mid_p, mid_a, 0, row_at)
                sums[2] = sums[2] + along(mid_p, mid_a, 1, lane_at)
            for k in range(3):
                target[:, 2 * k + j] = (-0.5 * sums[k]).reshape(target.shape[0], target.shape[2], lanes)


def call(kernel, limit, outs, scratch=()):
    vmem = pl.BlockSpec(memory_space=pltpu.VMEM)

    def run(*args):
        return pl.pallas_call(
            kernel,
            out_shape=tuple(jax.ShapeDtypeStruct(x, kind) for x, kind in outs),
            in_specs=[vmem] * len(args),
            out_specs=tuple([vmem] * len(outs)),
            scratch_shapes=list(scratch),
            compiler_params=pltpu.CompilerParams(vmem_limit_bytes=limit * MEBI),
        )(*args)

    return run


NAMES = ("xh", "y", "xl", "c")


def routes(sizes, move):
    pairs = []
    nx, ny = sizes
    index = lambda h, y, l, c: ((h * ny + y) * 2 + l) * 2 + c
    for h in range(nx):
        for y in range(ny):
            for l in range(2):
                for c in range(2):
                    target = move(h, y, l, c)
                    if target is not None:
                        pairs.append((index(h, y, l, c), index(*target)))
    return pairs


def per_device(high_count, primary, conductivity, observed, receivers):
    chain = CHIPS // 2
    sizes = (high_count, chain)
    def step(by, around):
        def move(h, y, l, c):
            block = 2 * y + l + by
            if block < 0 or block >= CHIPS:
                return None
            side = 2 * h + l
            if around:
                wrap = 1 if (l == 1) else -1
                side = (side + wrap) % (2 * high_count)
                return (side // 2, block // 2, side % 2, c)
            return (h, block // 2, block % 2, c)

        return routes(sizes, move)

    def send(x, pairs):
        return lax.ppermute(x, NAMES, pairs)

    fields = primary[0]
    swap = routes(sizes, lambda h, y, l, c: (h, y, l, 1 - c))
    p_low = send(fields, step(1, False))
    p_high = send(fields, step(-1, False))
    c_low = send(conductivity, step(1, True))
    c_high = send(conductivity, step(-1, True))

    rows, lanes = primary.shape[3], primary.shape[4]
    count = receivers.shape[1]
    f32 = lambda *shape: (shape, F32)
    deep = f32(DEEP, rows, lanes)
    pairs = f32(2, DEEP, rows, lanes)
    four = f32(KEPT, rows, lanes)
    hot, hot_own = call(
        hot_kernel, 4, [((10 * rows, count), BF16), ((3 * KEPT * rows, count), BF16)]
    )(receivers)
    own_c, p_pair = lax.optimization_barrier((conductivity, send(fields, swap)))
    c_pair = send(own_c, swap)
    p_mid, c_mid, ky_mid, kz_mid, dg_mid, p_sample = call(
        own_kernel,
        8,
        [f32(2, KEPT, rows, lanes), four, four, four, four, f32(2, count)],
        [pltpu.VMEM((2 * lanes, 3 * KEPT * rows), BF16)],
    )(fields, p_pair, conductivity, c_pair, receivers, hot_own)
    c_low, c_high, p_sample = lax.optimization_barrier((c_low, c_high, p_sample))
    c_low_pair, c_high_pair = send(c_low, swap), send(c_high, swap)
    p_low, p_high, p_sample = lax.optimization_barrier((p_low, p_high, p_sample))
    p_low_pair, p_high_pair = send(p_low, swap), send(p_high, swap)
    kx, ky, kz, dinv, dg, prim, f0, f1, f2, sent = call(
        forward_kernel,
        20,
        [deep] * 5 + [pairs] * 4 + [f32(CHIPS, 8, count + 128)],
        [
            pltpu.VMEM((DEEP, rows, lanes), F32),
            pltpu.VMEM((6 * lanes, 3 * KEPT * rows), BF16),
            pltpu.VMEM((6, count), F32),
        ],
    )(
        p_mid, p_low, p_low_pair, p_high, p_high_pair,
        c_mid, c_low, c_low_pair, c_high, c_high_pair, ky_mid, kz_mid, dg_mid, receivers, hot_own, p_sample,
    )
    got = lax.all_to_all(sent, ("y", "xl"), 0, 0, tiled=True)
    six = (2, 6, rows, lanes)
    a0, a1, a2, pot, pred, sent = call(
        adjoint_kernel,
        18,
        [f32(*six)] * 4 + [f32(2, count), f32(CHIPS, 8, 128)],
        [pltpu.VMEM((3, 2 * lanes, count), BF16)] + [pltpu.VMEM((2, DEEP, rows, lanes), F32)] * 3,
    )(got, observed[0], receivers, hot, kx, ky, kz, dinv, dg, prim, f0, f1, f2)
    got = lax.all_to_all(sent, ("y", "xl"), 0, 0, tiled=True)
    slabs = lax.axis_size("z")
    chunks = (slabs, 6, rows // slabs, lanes)
    kept, given = call(gradient_kernel, 8, [f32(*chunks)] * 2, [pltpu.VMEM(six, F32)])(got, a0, a1, a2, pot)
    given, pred = lax.optimization_barrier((given, pred))
    total = kept + send(given, swap)
    pred_pair = send(pred, swap)
    even = lax.axis_index("c") == 0
    predicted = jnp.where(even, jnp.concatenate([pred, pred_pair]), jnp.concatenate([pred_pair, pred]))
    parts = lax.all_to_all(total, "z", 0, 0, tiled=True)
    share = jnp.sum(parts, axis=0, keepdims=True)
    if high_count > 1:
        share = share + lax.ppermute(share, "xh", [(0, 1), (1, 0)])
    spread = jnp.broadcast_to(share, chunks)
    whole = lax.all_to_all(spread, "z", 0, 0, tiled=True)
    grad = jnp.transpose(whole, (1, 0, 2, 3)).reshape(3, 2, rows, lanes)
    return grad, predicted[None]


def solution(mesh):
    groups = mesh.shape["src"]
    high = 2 if groups > 1 else 1
    devices = mesh.devices.reshape(groups // high, high, CHIPS // 2, 2, 2)
    inner = Mesh(devices, ("z", "xh", "y", "xl", "c"))
    src, dom = ("z", "xh"), ("y", "xl", "c")
    return jax.shard_map(
        functools.partial(per_device, high),
        mesh=inner,
        in_specs=(P(src, None, dom, None, None), P(None, dom, None, None), P(src, None, None), P(src, None)),
        out_specs=(P(None, dom, None, None), P(src, None, None)),
        check_vma=False,
    )
```

```python
import functools
import jax
import jax.numpy as jnp
from jax import lax
from jax.experimental import pallas as pl
from jax.experimental.pallas import tpu as pltpu
from jax.sharding import Mesh, PartitionSpec as P

F32 = jnp.float32
BF16 = jnp.bfloat16
MEBI = 1024 * 1024
DEEP = 12
KEPT = 4
CHIPS = 8
LANES = 128


def pieces_of(values):
    first = values.astype(BF16)
    rest = values - first.astype(F32)
    second = rest.astype(BF16)
    third = (rest - second.astype(F32)).astype(BF16)
    return first, second, third


def fold(plane):
    return jnp.sum(plane.reshape(plane.shape[0] // 8, 8, plane.shape[1]), axis=0)


def ahead(plane, axis):
    return pltpu.roll(plane, plane.shape[axis] - 1, axis)


def behind(plane, axis):
    return pltpu.roll(plane, 1, axis)


def neighbours(field, s, i, kx, ky, kz):
    mid = field[s, i]
    total = kx[i] * field[s, i + 1] + kx[i - 1] * field[s, i - 1]
    total = total + ky[i] * ahead(mid, 0) + behind(ky[i] * mid, 0)
    return total + kz[i] * ahead(mid, 1) + behind(kz[i] * mid, 1)


def krylov(t0, t1, t2, kx, ky, kz, dinv, dg):
    sources = t0.shape[0]

    def apply_planes(source, target, first, last):
        def body(i, carry):
            for s in range(sources):
                target[s, i] = source[s, i] - dinv[i] * neighbours(source, s, i, kx, ky, kz)
            return carry

        lax.fori_loop(first, last + 1, body, 0, unroll=True)

    apply_planes(t0, t1, 2, 9)
    apply_planes(t1, t2, 3, 8)

    def body(i, sums):
        sums = list(sums)
        for s in range(sources):
            a0, a1, a2 = t0[s, i], t1[s, i], t2[s, i]
            a3 = a2 - dinv[i] * neighbours(t2, s, i, kx, ky, kz)
            d = dg[i]
            b1 = a0 - a1
            b2 = b1 - (a1 - a2)
            b3 = b2 - ((a1 - a2) - (a2 - a3))
            d0, d1, d2, e1, e2 = d * a0, d * a1, d * a2, d * b1, d * b2
            terms = [
                d0 * a0, d0 * a1, d1 * a1, d1 * a2, d2 * a2, d2 * a3,
                d0 * b1, e1 * b1, e1 * b2, e2 * b2, e2 * b3,
            ]
            for k, term in enumerate(terms):
                sums[k * sources + s] = sums[k * sources + s] + fold(term)
        return tuple(sums)

    zero = jnp.zeros((8, t0.shape[3]), F32)
    sums = lax.fori_loop(4, 8, body, (zero,) * (11 * sources), unroll=True)
    row_at = lax.broadcasted_iota(jnp.int32, (8, 128), 0)
    lane_at = lax.broadcasted_iota(jnp.int32, (8, 128), 1)
    packed = jnp.zeros((8, 128), F32)
    for n, x in enumerate(sums):
        here = jnp.logical_and(row_at == n % sources, lane_at == n // sources)
        packed = jnp.where(here, jnp.sum(x), packed)
    return packed


def weights_of(moments):
    t = [moments[0:2, k : k + 1] for k in range(6)]
    m = [t[0]] + [moments[0:2, k : k + 1] for k in range(6, 11)]
    near = t[1] < 0.5 * t[0]
    g = [jnp.where(near, t[k + 1], m[k] - m[k + 1]) for k in range(5)]
    h = [jnp.where(near, t[k], m[k]) for k in range(3)]
    l1 = g[1] / g[0]
    l2 = g[2] / g[0]
    d1 = g[2] - l1 * g[1]
    e2 = g[3] - l2 * g[1]
    l21 = e2 / d1
    d2 = g[4] - l2 * g[2] - l21 * e2
    y1 = h[1] - l1 * h[0]
    y2 = h[2] - l2 * h[0] - l21 * y1
    c2 = y2 / d2
    c1 = y1 / d1 - l21 * c2
    c0 = h[0] / g[0] - l1 * c1 - l2 * c2
    w0 = jnp.where(near, c0, c0 + c1 + c2)
    w1 = jnp.where(near, c1, -(c1 + 2.0 * c2))
    return w0, w1, c2


def one_hot(count, first, picked):
    place = lax.broadcasted_iota(jnp.int32, (count, picked.shape[1]), 0) + first
    return place == picked


def edges(rows, lanes):
    row_at = lax.broadcasted_iota(jnp.int32, (rows, lanes), 0)
    lane_at = lax.broadcasted_iota(jnp.int32, (rows, lanes), 1)
    mask_y = jnp.where(row_at < rows - 1, 1.0, 0.0).astype(F32)
    mask_z = jnp.where(lane_at < lanes - 1, 1.0, 0.0).astype(F32)
    return row_at, lane_at, mask_y, mask_z


def in_plane(along_y, along_z):
    rows, lanes = along_y.shape
    row_at, lane_at, mask_y, mask_z = edges(rows, lanes)
    up_y = 0.5 * (along_y + ahead(along_y, 0)) * mask_y
    up_z = 0.5 * (along_z + ahead(along_z, 1)) * mask_z
    low_y = jnp.where(row_at == 0, 0.5 * along_y, behind(up_y, 0))
    low_z = jnp.where(lane_at == 0, 0.5 * along_z, behind(up_z, 1))
    top_y = jnp.where(row_at == rows - 1, 0.5 * along_y, up_y)
    top_z = jnp.where(lane_at == lanes - 1, 0.5 * along_z, up_z)
    return up_y, up_z, top_y + low_y + top_z + low_z


def hot_kernel(cells, hot, hot_own):
    block = 2 * lax.axis_index("y") + lax.axis_index("xl")
    rows = hot.shape[0] // 10
    row_of = cells[...] // LANES
    for i in range(10):
        rows_hot = one_hot(rows, (4 * block - 3 + i) * rows, row_of)
        rows_hot = jnp.where(rows_hot, 1.0, 0.0).astype(BF16)
        hot[pl.ds(i * rows, rows)] = rows_hot
        if 3 <= i < 7:
            for piece in range(3):
                hot_own[pl.ds((piece * KEPT + i - 3) * rows, rows)] = rows_hot


def own_kernel(p_own, p_pair, c_own, c_pair, cells, hot_own, prim, first, ky, kz, plane_dg, sample, left):
    core = lax.axis_index("c")
    here = pl.ds(2 * core, 2)
    other = pl.ds(2 - 2 * core, 2)
    prim[:, here] = p_own[here]
    prim[:, other] = p_pair[here]
    first[here] = c_own[0]
    first[other] = c_pair[0]
    rows, lanes = prim.shape[2], prim.shape[3]
    for source, base in ((c_own, 2 * core), (c_pair, 2 - 2 * core)):
        for j in range(2):
            up_y, up_z, part = in_plane(source[1, j], source[2, j])
            ky[base + j] = up_y
            kz[base + j] = up_z
            plane_dg[base + j] = part
    picked = cells[...]
    lane_of = picked - (picked // lanes) * lanes
    gather([(prim, 0)], left, hot_own, one_hot(lanes, 0, lane_of), sample)


def gather(fields, left, hot_own, lane_hot, sample):
    lanes = lane_hot.shape[0]
    for f, (field, first) in enumerate(fields):
        rows = field.shape[2]
        for s in range(2):
            for j in range(KEPT):
                parts = pieces_of(jnp.transpose(field[s, first + j]))
                for k in range(3):
                    start = (k * KEPT + j) * rows
                    left[pl.ds((2 * f + s) * lanes, lanes), start : start + rows] = parts[k]
    spread = jnp.dot(left[...], hot_own[...], preferred_element_type=F32)
    found = [
        jnp.sum(jnp.where(lane_hot, spread[k * lanes : (k + 1) * lanes], 0.0), axis=0, keepdims=True)
        for k in range(2 * len(fields))
    ]
    sample[...] = jnp.concatenate(found, axis=0)


def forward_kernel(
    p_mid, p_low, p_low_pair, p_high, p_high_pair,
    c_mid, c_low, c_low_pair, c_high, c_high_pair, ky_mid, kz_mid, dg_mid, cells, hot_own, p_sample,
    kx, ky, kz, dinv, dg, prim, t0, t1, t2, sent, cond, left, found,
):
    block = 2 * lax.axis_index("y") + lax.axis_index("xl")
    core = lax.axis_index("c")
    here = pl.ds(2 * core, 2)
    prim[:, 4:8] = p_mid[...]
    cond[4:8] = c_mid[...]
    for base, first, second in ((0, p_low, p_low_pair), (8, p_high, p_high_pair)):
        prim[:, pl.ds(base + 2 * core, 2)] = first[here]
        prim[:, pl.ds(base + 2 - 2 * core, 2)] = second[here]
    for base, first, second in ((0, c_low, c_low_pair), (8, c_high, c_high_pair)):
        cond[pl.ds(base + 2 * core, 2)] = first[0]
        cond[pl.ds(base + 2 - 2 * core, 2)] = second[0]
        for source, start in ((first, base + 2 * core), (second, base + 2 - 2 * core)):
            for j in range(2):
                up_y, up_z, part = in_plane(source[1, j], source[2, j])
                ky[start + j] = up_y
                kz[start + j] = up_z
                dg[start + j] = part
    ky[4:8] = ky_mid[...]
    kz[4:8] = kz_mid[...]
    dg[4:8] = dg_mid[...]
    rows, lanes = prim.shape[2], prim.shape[3]
    row_at, lane_at, mask_y, mask_z = edges(rows, lanes)
    edge = jnp.where(row_at == 0, 0.5, 0.0) + jnp.where(row_at == rows - 1, 0.5, 0.0)
    edge = edge + jnp.where(lane_at == 0, 0.5, 0.0) + jnp.where(lane_at == lanes - 1, 0.5, 0.0)
    unit = (6.0 - edge).astype(F32)
    layers = 4 * CHIPS

    kx[0] = 0.5 * (cond[0] + cond[1])

    def coefficients(i, carry):
        layer = 4 * block - 4 + i
        inside = jnp.where(jnp.logical_and(layer >= 0, layer < layers), 1.0, 0.0).astype(F32)
        first = 0.5 * (cond[i] + cond[i + 1])
        kx[i] = first
        diagonal = first + kx[i - 1] + dg[i]
        inverse = jnp.where(inside > 0.5, 1.0 / diagonal, 0.0)
        dg[i] = diagonal
        dinv[i] = inverse
        return carry

    lax.fori_loop(1, 11, coefficients, 0)

    def right_side(i, carry):
        layer = 4 * block - 4 + i
        outer = jnp.where(jnp.logical_or(layer == 0, layer == layers - 1), 0.5, 0.0).astype(F32)
        diagonal = (unit - outer) - dg[i]
        upper, lower = 1.0 - kx[i], 1.0 - kx[i - 1]
        diff_y = mask_y - ky[i]
        diff_z = mask_z - kz[i]
        inverse = dinv[i]
        for s in range(2):
            mid = prim[s, i]
            total = diagonal * mid - upper * prim[s, i + 1] - lower * prim[s, i - 1]
            total = total - diff_y * ahead(mid, 0) - behind(diff_y * mid, 0)
            total = total - diff_z * ahead(mid, 1) - behind(diff_z * mid, 1)
            t0[s, i] = inverse * total
        return carry

    lax.fori_loop(1, 11, right_side, 0, unroll=True)
    moments = krylov(t0, t1, t2, kx, ky, kz, dinv, dg)

    picked = cells[...]
    lane_of = picked - (picked // lanes) * lanes
    count = picked.shape[1]
    gather([(t0, 4), (t1, 4), (t2, 4)], left, hot_own, one_hot(lanes, 0, lane_of), found)
    for k in range(CHIPS):
        sent[k, 0:2, :count] = p_sample[...]
        sent[k, 2:8, :count] = found[...]
        sent[k, :, count:] = moments


def adjoint_kernel(
    got, observed, cells, hot, kx, ky, kz, dinv, dg, prim, f0, f1, f2,
    b0, b1, b2, pot, predicted, sent, heavy, a0, a1, a2,
):
    core = lax.axis_index("c")
    rows, lanes = prim.shape[2], prim.shape[3]
    count = cells.shape[1]
    total = got[0]
    for k in range(1, CHIPS):
        total = total + got[k]
    weights = weights_of(total[:, count:])
    sample = total[:, :count]
    value = sample[0:2]
    for k in range(3):
        value = value + weights[k] * sample[2 * k + 2 : 2 * k + 4]
    predicted[...] = value
    seen = jnp.where(core == 0, observed[0:2], observed[2:4])
    misfit = value - seen
    for i in range(6):
        for s in range(2):
            w = [weights[k][s : s + 1, :] for k in range(3)]
            pot[s, i] = prim[s, i + 3] + w[0] * f0[s, i + 3] + w[1] * f1[s, i + 3] + w[2] * f2[s, i + 3]

    picked = cells[...]
    lane_of = picked - (picked // lanes) * lanes
    lane_hot = one_hot(lanes, 0, lane_of)
    for s in range(2):
        spread = jnp.where(lane_hot, misfit[s : s + 1], 0.0)
        for k, piece in enumerate(pieces_of(spread)):
            heavy[k, pl.ds(s * lanes, lanes)] = piece
    placed = [
        lax.dot_general(hot[...], heavy[k], (((1,), (1,)), ((), ())), preferred_element_type=F32)
        for k in range(3)
    ]
    source = placed[0] + placed[1] + placed[2]
    for i in range(10):
        inverse = dinv[i + 1]
        for s in range(2):
            a0[s, i + 1] = inverse * source[i * rows : (i + 1) * rows, s * lanes : (s + 1) * lanes]
    moments = krylov(a0, a1, a2, kx, ky, kz, dinv, dg)
    for k in range(CHIPS):
        sent[k] = moments
    for near, deep in ((b0, a0), (b1, a1), (b2, a2)):
        near[...] = deep[:, 3:9]


def gradient_kernel(got, a0, a1, a2, pot, kept, given, adj):
    core = lax.axis_index("c")
    moments = got[0]
    for k in range(1, CHIPS):
        moments = moments + got[k]
    weights = weights_of(moments)
    rows, lanes = pot.shape[2], pot.shape[3]
    row_at = lax.broadcasted_iota(jnp.int32, (rows, lanes), 0)
    lane_at = lax.broadcasted_iota(jnp.int32, (rows, lanes), 1)
    for i in range(6):
        for s in range(2):
            w = [weights[k][s : s + 1, :] for k in range(3)]
            adj[s, i] = w[0] * a0[s, i] + w[1] * a1[s, i] + w[2] * a2[s, i]

    def along(mid_p, mid_a, axis, at):
        last = mid_p.shape[axis] - 1
        next_p = jnp.where(at == last, 0.0, ahead(mid_p, axis))
        next_a = jnp.where(at == last, 0.0, ahead(mid_a, axis))
        upper = (mid_p - next_p) * (mid_a - next_a)
        lower = jnp.where(at == 0, mid_p * mid_a, behind(upper, axis))
        return upper + lower

    for target, first in ((given, 1 + 2 * (1 - core)), (kept, 1 + 2 * core)):
        for j in range(2):
            i = first + j
            sums = [0.0, 0.0, 0.0]
            for s in range(2):
                mid_p, mid_a = pot[s, i], adj[s, i]
                upper = (mid_p - pot[s, i + 1]) * (mid_a - adj[s, i + 1])
                lower = (mid_p - pot[s, i - 1]) * (mid_a - adj[s, i - 1])
                sums[0] = sums[0] + upper + lower
                sums[1] = sums[1] + along(mid_p, mid_a, 0, row_at)
                sums[2] = sums[2] + along(mid_p, mid_a, 1, lane_at)
            for k in range(3):
                target[:, 2 * k + j] = (-0.5 * sums[k]).reshape(target.shape[0], target.shape[2], lanes)


def call(kernel, limit, outs, scratch=()):
    vmem = pl.BlockSpec(memory_space=pltpu.VMEM)

    def run(*args):
        return pl.pallas_call(
            kernel,
            out_shape=tuple(jax.ShapeDtypeStruct(x, kind) for x, kind in outs),
            in_specs=[vmem] * len(args),
            out_specs=tuple([vmem] * len(outs)),
            scratch_shapes=list(scratch),
            compiler_params=pltpu.CompilerParams(vmem_limit_bytes=limit * MEBI),
        )(*args)

    return run


NAMES = ("xh", "y", "xl", "c")


def routes(sizes, move):
    pairs = []
    nx, ny = sizes
    index = lambda h, y, l, c: ((h * ny + y) * 2 + l) * 2 + c
    for h in range(nx):
        for y in range(ny):
            for l in range(2):
                for c in range(2):
                    target = move(h, y, l, c)
                    if target is not None:
                        pairs.append((index(h, y, l, c), index(*target)))
    return pairs


def per_device(high_count, primary, conductivity, observed, receivers):
    chain = CHIPS // 2
    sizes = (high_count, chain)
    def step(by, around):
        def move(h, y, l, c):
            block = 2 * y + l + by
            if block < 0 or block >= CHIPS:
                return None
            side = 2 * h + l
            if around:
                wrap = 1 if (l == 1) else -1
                side = (side + wrap) % (2 * high_count)
                return (side // 2, block // 2, side % 2, c)
            return (h, block // 2, block % 2, c)

        return routes(sizes, move)

    def send(x, pairs):
        return lax.ppermute(x, NAMES, pairs)

    fields = primary[0]
    swap = routes(sizes, lambda h, y, l, c: (h, y, l, 1 - c))
    p_low = send(fields, step(1, False))
    p_high = send(fields, step(-1, False))
    c_low = send(conductivity, step(1, True))
    c_high = send(conductivity, step(-1, True))

    rows, lanes = primary.shape[3], primary.shape[4]
    count = receivers.shape[1]
    f32 = lambda *shape: (shape, F32)
    deep = f32(DEEP, rows, lanes)
    pairs = f32(2, DEEP, rows, lanes)
    four = f32(KEPT, rows, lanes)
    hot, hot_own = call(
        hot_kernel, 4, [((10 * rows, count), BF16), ((3 * KEPT * rows, count), BF16)]
    )(receivers)
    own_c, p_pair = lax.optimization_barrier((conductivity, send(fields, swap)))
    c_pair = send(own_c, swap)
    p_mid, c_mid, ky_mid, kz_mid, dg_mid, p_sample = call(
        own_kernel,
        8,
        [f32(2, KEPT, rows, lanes), four, four, four, four, f32(2, count)],
        [pltpu.VMEM((2 * lanes, 3 * KEPT * rows), BF16)],
    )(fields, p_pair, conductivity, c_pair, receivers, hot_own)
    ready = p_sample
    pairs_of = []
    for x in (p_low, p_high, c_low, c_high):
        x, token = lax.optimization_barrier((x, ready))
        pairs_of.append(send(x, swap))
    p_low_pair, p_high_pair, c_low_pair, c_high_pair = pairs_of
    kx, ky, kz, dinv, dg, prim, f0, f1, f2, sent = call(
        forward_kernel,
        20,
        [deep] * 5 + [pairs] * 4 + [f32(CHIPS, 8, count + 128)],
        [
            pltpu.VMEM((DEEP, rows, lanes), F32),
            pltpu.VMEM((6 * lanes, 3 * KEPT * rows), BF16),
            pltpu.VMEM((6, count), F32),
        ],
    )(
        p_mid, p_low, p_low_pair, p_high, p_high_pair,
        c_mid, c_low, c_low_pair, c_high, c_high_pair, ky_mid, kz_mid, dg_mid, receivers, hot_own, p_sample,
    )
    got = lax.all_to_all(sent, ("y", "xl"), 0, 0, tiled=True)
    six = (2, 6, rows, lanes)
    a0, a1, a2, pot, pred, sent = call(
        adjoint_kernel,
        18,
        [f32(*six)] * 4 + [f32(2, count), f32(CHIPS, 8, 128)],
        [pltpu.VMEM((3, 2 * lanes, count), BF16)] + [pltpu.VMEM((2, DEEP, rows, lanes), F32)] * 3,
    )(got, observed[0], receivers, hot, kx, ky, kz, dinv, dg, prim, f0, f1, f2)
    got = lax.all_to_all(sent, ("y", "xl"), 0, 0, tiled=True)
    slabs = lax.axis_size("z")
    chunks = (slabs, 6, rows // slabs, lanes)
    kept, given = call(gradient_kernel, 8, [f32(*chunks)] * 2, [pltpu.VMEM(six, F32)])(got, a0, a1, a2, pot)
    given, pred = lax.optimization_barrier((given, pred))
    total = kept + send(given, swap)
    pred_pair = send(pred, swap)
    even = lax.axis_index("c") == 0
    predicted = jnp.where(even, jnp.concatenate([pred, pred_pair]), jnp.concatenate([pred_pair, pred]))
    parts = lax.all_to_all(total, "z", 0, 0, tiled=True)
    share = jnp.sum(parts, axis=0, keepdims=True)
    if high_count > 1:
        share = share + lax.ppermute(share, "xh", [(0, 1), (1, 0)])
    spread = jnp.broadcast_to(share, chunks)
    whole = lax.all_to_all(spread, "z", 0, 0, tiled=True)
    grad = jnp.transpose(whole, (1, 0, 2, 3)).reshape(3, 2, rows, lanes)
    return grad, predicted[None]


def solution(mesh):
    groups = mesh.shape["src"]
    high = 2 if groups > 1 else 1
    devices = mesh.devices.reshape(groups // high, high, CHIPS // 2, 2, 2)
    inner = Mesh(devices, ("z", "xh", "y", "xl", "c"))
    src, dom = ("z", "xh"), ("y", "xl", "c")
    return jax.shard_map(
        functools.partial(per_device, high),
        mesh=inner,
        in_specs=(P(src, None, dom, None, None), P(None, dom, None, None), P(src, None, None), P(src, None)),
        out_specs=(P(None, dom, None, None), P(src, None, None)),
        check_vma=False,
    )
```

```python
import functools
import jax
import jax.numpy as jnp
from jax import lax
from jax.experimental import pallas as pl
from jax.experimental.pallas import tpu as pltpu
from jax.sharding import Mesh, PartitionSpec as P

F32 = jnp.float32
BF16 = jnp.bfloat16
MEBI = 1024 * 1024
DEEP = 12
KEPT = 4
CHIPS = 8
LANES = 128


def pieces_of(values):
    first = values.astype(BF16)
    rest = values - first.astype(F32)
    second = rest.astype(BF16)
    third = (rest - second.astype(F32)).astype(BF16)
    return first, second, third


class Planes:
    def __init__(self, low, high, cut):
        self.low, self.high, self.cut = low, high, cut
        self.shape = low.shape

    def place(self, key):
        lead, i = (key[:-1], key[-1]) if isinstance(key, tuple) else ((), key)
        return (self.low, lead + (i,)) if i < self.cut else (self.high, lead + (i - self.cut,))

    def __getitem__(self, key):
        ref, at = self.place(key)
        return ref[at]

    def __setitem__(self, key, value):
        ref, at = self.place(key)
        ref[at] = value


def fold(plane):
    return jnp.sum(plane.reshape(plane.shape[0] // 8, 8, plane.shape[1]), axis=0)


def ahead(plane, axis):
    return pltpu.roll(plane, plane.shape[axis] - 1, axis)


def behind(plane, axis):
    return pltpu.roll(plane, 1, axis)


def neighbours(field, s, i, kx, ky, kz):
    mid = field[s, i]
    total = kx[i] * field[s, i + 1] + kx[i - 1] * field[s, i - 1]
    total = total + ky[i] * ahead(mid, 0) + behind(ky[i] * mid, 0)
    return total + kz[i] * ahead(mid, 1) + behind(kz[i] * mid, 1)


def apply_planes(source, target, first, last, kx, ky, kz, dinv):
    for i in range(first, last + 1):
        for s in range(source.shape[0]):
            target[s, i] = source[s, i] - dinv[i] * neighbours(source, s, i, kx, ky, kz)


def krylov(t0, t1, t2, kx, ky, kz, dinv, dg, first=(2, 3)):
    sources = t0.shape[0]
    apply_planes(t0, t1, first[0], 9, kx, ky, kz, dinv)
    apply_planes(t1, t2, first[1], 8, kx, ky, kz, dinv)

    def body(i, sums):
        sums = list(sums)
        for s in range(sources):
            a0, a1, a2 = t0[s, i], t1[s, i], t2[s, i]
            a3 = a2 - dinv[i] * neighbours(t2, s, i, kx, ky, kz)
            d = dg[i]
            b1 = a0 - a1
            b2 = b1 - (a1 - a2)
            b3 = b2 - ((a1 - a2) - (a2 - a3))
            d0, d1, d2, e1, e2 = d * a0, d * a1, d * a2, d * b1, d * b2
            terms = [
                d0 * a0, d0 * a1, d1 * a1, d1 * a2, d2 * a2, d2 * a3,
                d0 * b1, e1 * b1, e1 * b2, e2 * b2, e2 * b3,
            ]
            for k, term in enumerate(terms):
                sums[k * sources + s] = sums[k * sources + s] + fold(term)
        return tuple(sums)

    sums = (jnp.zeros((8, t0.shape[3]), F32),) * (11 * sources)
    for i in range(4, 8):
        sums = body(i, sums)
    row_at = lax.broadcasted_iota(jnp.int32, (8, 128), 0)
    lane_at = lax.broadcasted_iota(jnp.int32, (8, 128), 1)
    packed = jnp.zeros((8, 128), F32)
    for n, x in enumerate(sums):
        here = jnp.logical_and(row_at == n % sources, lane_at == n // sources)
        packed = jnp.where(here, jnp.sum(x), packed)
    return packed


def weights_of(moments):
    t = [moments[0:2, k : k + 1] for k in range(6)]
    m = [t[0]] + [moments[0:2, k : k + 1] for k in range(6, 11)]
    near = t[1] < 0.5 * t[0]
    g = [jnp.where(near, t[k + 1], m[k] - m[k + 1]) for k in range(5)]
    h = [jnp.where(near, t[k], m[k]) for k in range(3)]
    l1 = g[1] / g[0]
    l2 = g[2] / g[0]
    d1 = g[2] - l1 * g[1]
    e2 = g[3] - l2 * g[1]
    l21 = e2 / d1
    d2 = g[4] - l2 * g[2] - l21 * e2
    y1 = h[1] - l1 * h[0]
    y2 = h[2] - l2 * h[0] - l21 * y1
    c2 = y2 / d2
    c1 = y1 / d1 - l21 * c2
    c0 = h[0] / g[0] - l1 * c1 - l2 * c2
    w0 = jnp.where(near, c0, c0 + c1 + c2)
    w1 = jnp.where(near, c1, -(c1 + 2.0 * c2))
    return w0, w1, c2


def one_hot(count, first, picked):
    place = lax.broadcasted_iota(jnp.int32, (count, picked.shape[1]), 0) + first
    return place == picked


def edges(rows, lanes):
    row_at = lax.broadcasted_iota(jnp.int32, (rows, lanes), 0)
    lane_at = lax.broadcasted_iota(jnp.int32, (rows, lanes), 1)
    mask_y = jnp.where(row_at < rows - 1, 1.0, 0.0).astype(F32)
    mask_z = jnp.where(lane_at < lanes - 1, 1.0, 0.0).astype(F32)
    return row_at, lane_at, mask_y, mask_z


def in_plane(along_y, along_z):
    rows, lanes = along_y.shape
    row_at, lane_at, mask_y, mask_z = edges(rows, lanes)
    up_y = 0.5 * (along_y + ahead(along_y, 0)) * mask_y
    up_z = 0.5 * (along_z + ahead(along_z, 1)) * mask_z
    low_y = jnp.where(row_at == 0, 0.5 * along_y, behind(up_y, 0))
    low_z = jnp.where(lane_at == 0, 0.5 * along_z, behind(up_z, 1))
    top_y = jnp.where(row_at == rows - 1, 0.5 * along_y, up_y)
    top_z = jnp.where(lane_at == lanes - 1, 0.5 * along_z, up_z)
    return up_y, up_z, top_y + low_y + top_z + low_z


def hot_kernel(cells, hot, hot_own):
    block = 2 * lax.axis_index("y") + lax.axis_index("xl")
    rows = hot.shape[0] // 10
    row_of = cells[...] // LANES
    for i in range(10):
        rows_hot = one_hot(rows, (4 * block - 3 + i) * rows, row_of)
        rows_hot = jnp.where(rows_hot, 1.0, 0.0).astype(BF16)
        hot[pl.ds(i * rows, rows)] = rows_hot
        if 3 <= i < 7:
            for piece in range(3):
                hot_own[pl.ds((piece * KEPT + i - 3) * rows, rows)] = rows_hot


def own_kernel(p_own, p_pair, c_own, c_pair, cells, hot_own, prim, first, ky, kz, plane_dg, sample, left):
    core = lax.axis_index("c")
    here = pl.ds(2 * core, 2)
    other = pl.ds(2 - 2 * core, 2)
    prim[:, here] = p_own[here]
    prim[:, other] = p_pair[here]
    first[here] = c_own[0]
    first[other] = c_pair[0]
    rows, lanes = prim.shape[2], prim.shape[3]
    for source, base in ((c_own, 2 * core), (c_pair, 2 - 2 * core)):
        for j in range(2):
            up_y, up_z, part = in_plane(source[1, j], source[2, j])
            ky[base + j] = up_y
            kz[base + j] = up_z
            plane_dg[base + j] = part
    picked = cells[...]
    lane_of = picked - (picked // lanes) * lanes
    gather([(prim, 0)], left, hot_own, one_hot(lanes, 0, lane_of), sample)


def gather(fields, left, hot_own, lane_hot, sample):
    lanes = lane_hot.shape[0]
    for f, (field, first) in enumerate(fields):
        rows = field.shape[2]
        for s in range(2):
            for j in range(KEPT):
                parts = pieces_of(jnp.transpose(field[s, first + j]))
                for k in range(3):
                    start = (k * KEPT + j) * rows
                    left[pl.ds((2 * f + s) * lanes, lanes), start : start + rows] = parts[k]
    spread = jnp.dot(left[...], hot_own[...], preferred_element_type=F32)
    found = [
        jnp.sum(jnp.where(lane_hot, spread[k * lanes : (k + 1) * lanes], 0.0), axis=0, keepdims=True)
        for k in range(2 * len(fields))
    ]
    sample[...] = jnp.concatenate(found, axis=0)


def unit_of(rows, lanes):
    row_at, lane_at, mask_y, mask_z = edges(rows, lanes)
    edge = jnp.where(row_at == 0, 0.5, 0.0) + jnp.where(row_at == rows - 1, 0.5, 0.0)
    edge = edge + jnp.where(lane_at == 0, 0.5, 0.0) + jnp.where(lane_at == lanes - 1, 0.5, 0.0)
    return mask_y, mask_z, (6.0 - edge).astype(F32)


def halo_planes(base, core, fields, conductivities, prim, cond, ky, kz, dg):
    here = pl.ds(2 * core, 2)
    starts = (base + 2 * core, base + 2 - 2 * core)
    for source, start in zip(fields, starts):
        prim[:, pl.ds(start, 2)] = source[here]
    for source, start in zip(conductivities, starts):
        cond[pl.ds(start, 2)] = source[0]
        for j in range(2):
            up_y, up_z, part = in_plane(source[1, j], source[2, j])
            ky[start + j] = up_y
            kz[start + j] = up_z
            dg[start + j] = part


def start_planes(block, planes, flat, cond, kx, ky, kz, dinv, dg, prim, t0):
    layers = 4 * CHIPS
    mask_y, mask_z, unit = unit_of(prim.shape[2], prim.shape[3])
    for i in planes:
        layer = 4 * block - 4 + i
        inside = jnp.where(jnp.logical_and(layer >= 0, layer < layers), 1.0, 0.0).astype(F32)
        first = 0.5 * (cond[i] + cond[i + 1])
        kx[i] = first
        diagonal = first + kx[i - 1] + flat[i]
        dg[i] = diagonal
        dinv[i] = jnp.where(inside > 0.5, 1.0 / diagonal, 0.0)
    for i in planes:
        layer = 4 * block - 4 + i
        outer = jnp.where(jnp.logical_or(layer == 0, layer == layers - 1), 0.5, 0.0).astype(F32)
        diagonal = (unit - outer) - dg[i]
        upper, lower = 1.0 - kx[i], 1.0 - kx[i - 1]
        diff_y = mask_y - ky[i]
        diff_z = mask_z - kz[i]
        inverse = dinv[i]
        for s in range(2):
            mid = prim[s, i]
            total = diagonal * mid - upper * prim[s, i + 1] - lower * prim[s, i - 1]
            total = total - diff_y * ahead(mid, 0) - behind(diff_y * mid, 0)
            total = total - diff_z * ahead(mid, 1) - behind(diff_z * mid, 1)
            t0[s, i] = inverse * total


CUTS = (7, 8, 8, 7, 7, 8, 7, 6, 5)


def low_kernel(
    p_mid, p_low, p_low_pair, c_mid, c_low, c_low_pair, ky_mid, kz_mid, dg_mid,
    kx, ky, kz, dinv, dg, prim, t0, t1, t2, cond, flat,
):
    block = 2 * lax.axis_index("y") + lax.axis_index("xl")
    core = lax.axis_index("c")
    prim[:, 4:8] = p_mid[...]
    cond[4:8] = c_mid[...]
    ky[4:8] = ky_mid[...]
    kz[4:8] = kz_mid[...]
    flat[4:8] = dg_mid[...]
    halo_planes(0, core, (p_low, p_low_pair), (c_low, c_low_pair), prim, cond, ky, kz, flat)
    kx[0] = 0.5 * (cond[0] + cond[1])
    start_planes(block, range(1, 7), flat, cond, kx, ky, kz, dinv, dg, prim, t0)
    apply_planes(t0, t1, 2, 5, kx, ky, kz, dinv)
    apply_planes(t1, t2, 3, 4, kx, ky, kz, dinv)


def high_kernel(*refs):
    lows, refs = refs[:9], refs[9:]
    p_high, p_high_pair, c_mid, c_high, c_high_pair, dg_mid, cells, hot_own, p_sample = refs[:9]
    highs, (sent, cond, flat, left, found) = refs[9:18], refs[18:]
    block = 2 * lax.axis_index("y") + lax.axis_index("xl")
    core = lax.axis_index("c")
    kx, ky, kz, dinv, dg, prim, t0, t1, t2 = (Planes(*x) for x in zip(lows, highs, CUTS))
    cond[3] = c_mid[3]
    flat[3] = dg_mid[3]
    here = pl.ds(2 * core, 2)
    starts = (2 * core, 2 - 2 * core)
    for source, start in zip((p_high, p_high_pair), starts):
        prim.high[:, pl.ds(start, 2)] = source[here]
    for source, start in zip((c_high, c_high_pair), starts):
        cond[pl.ds(4 + start, 2)] = source[0]
        for j in range(2):
            up_y, up_z, part = in_plane(source[1, j], source[2, j])
            ky.high[start + j] = up_y
            kz.high[start + j] = up_z
            flat[4 + start + j] = part
    start_planes(block, range(7, 11), Planes(flat, flat, 4), Planes(cond, cond, 4), kx, ky, kz, dinv, dg, prim, t0)
    moments = krylov(t0, t1, t2, kx, ky, kz, dinv, dg, (6, 5))

    picked = cells[...]
    lanes = prim.shape[3]
    lane_of = picked - (picked // lanes) * lanes
    count = picked.shape[1]
    gather([(t0, 4), (t1, 4), (t2, 4)], left, hot_own, one_hot(lanes, 0, lane_of), found)
    for k in range(CHIPS):
        sent[k, 0:2, :count] = p_sample[...]
        sent[k, 2:8, :count] = found[...]
        sent[k, :, count:] = moments


def adjoint_kernel(got, observed, cells, hot, *refs):
    lows, highs = refs[:9], refs[9:18]
    b0, b1, b2, pot, predicted, sent, heavy, a0, a1, a2 = refs[18:]
    kx, ky, kz, dinv, dg, prim, f0, f1, f2 = (Planes(*x) for x in zip(lows, highs, CUTS))
    core = lax.axis_index("c")
    rows, lanes = prim.shape[2], prim.shape[3]
    count = cells.shape[1]
    total = got[0]
    for k in range(1, CHIPS):
        total = total + got[k]
    weights = weights_of(total[:, count:])
    sample = total[:, :count]
    value = sample[0:2]
    for k in range(3):
        value = value + weights[k] * sample[2 * k + 2 : 2 * k + 4]
    predicted[...] = value
    seen = jnp.where(core == 0, observed[0:2], observed[2:4])
    misfit = value - seen
    for i in range(6):
        for s in range(2):
            w = [weights[k][s : s + 1, :] for k in range(3)]
            pot[s, i] = prim[s, i + 3] + w[0] * f0[s, i + 3] + w[1] * f1[s, i + 3] + w[2] * f2[s, i + 3]

    picked = cells[...]
    lane_of = picked - (picked // lanes) * lanes
    lane_hot = one_hot(lanes, 0, lane_of)
    for s in range(2):
        spread = jnp.where(lane_hot, misfit[s : s + 1], 0.0)
        for k, piece in enumerate(pieces_of(spread)):
            heavy[k, pl.ds(s * lanes, lanes)] = piece
    placed = [
        lax.dot_general(hot[...], heavy[k], (((1,), (1,)), ((), ())), preferred_element_type=F32)
        for k in range(3)
    ]
    source = placed[0] + placed[1] + placed[2]
    for i in range(10):
        inverse = dinv[i + 1]
        for s in range(2):
            a0[s, i + 1] = inverse * source[i * rows : (i + 1) * rows, s * lanes : (s + 1) * lanes]
    moments = krylov(a0, a1, a2, kx, ky, kz, dinv, dg)
    for k in range(CHIPS):
        sent[k] = moments
    for near, deep in ((b0, a0), (b1, a1), (b2, a2)):
        near[...] = deep[:, 3:9]


def gradient_kernel(got, a0, a1, a2, pot, kept, given, adj):
    core = lax.axis_index("c")
    moments = got[0]
    for k in range(1, CHIPS):
        moments = moments + got[k]
    weights = weights_of(moments)
    rows, lanes = pot.shape[2], pot.shape[3]
    row_at = lax.broadcasted_iota(jnp.int32, (rows, lanes), 0)
    lane_at = lax.broadcasted_iota(jnp.int32, (rows, lanes), 1)
    for i in range(6):
        for s in range(2):
            w = [weights[k][s : s + 1, :] for k in range(3)]
            adj[s, i] = w[0] * a0[s, i] + w[1] * a1[s, i] + w[2] * a2[s, i]

    def along(mid_p, mid_a, axis, at):
        last = mid_p.shape[axis] - 1
        next_p = jnp.where(at == last, 0.0, ahead(mid_p, axis))
        next_a = jnp.where(at == last, 0.0, ahead(mid_a, axis))
        upper = (mid_p - next_p) * (mid_a - next_a)
        lower = jnp.where(at == 0, mid_p * mid_a, behind(upper, axis))
        return upper + lower

    for target, first in ((given, 1 + 2 * (1 - core)), (kept, 1 + 2 * core)):
        for j in range(2):
            i = first + j
            sums = [0.0, 0.0, 0.0]
            for s in range(2):
                mid_p, mid_a = pot[s, i], adj[s, i]
                upper = (mid_p - pot[s, i + 1]) * (mid_a - adj[s, i + 1])
                lower = (mid_p - pot[s, i - 1]) * (mid_a - adj[s, i - 1])
                sums[0] = sums[0] + upper + lower
                sums[1] = sums[1] + along(mid_p, mid_a, 0, row_at)
                sums[2] = sums[2] + along(mid_p, mid_a, 1, lane_at)
            for k in range(3):
                target[:, 2 * k + j] = (-0.5 * sums[k]).reshape(target.shape[0], target.shape[2], lanes)


def call(kernel, limit, outs, scratch=()):
    vmem = pl.BlockSpec(memory_space=pltpu.VMEM)

    def run(*args):
        return pl.pallas_call(
            kernel,
            out_shape=tuple(jax.ShapeDtypeStruct(x, kind) for x, kind in outs),
            in_specs=[vmem] * len(args),
            out_specs=tuple([vmem] * len(outs)),
            scratch_shapes=list(scratch),
            compiler_params=pltpu.CompilerParams(vmem_limit_bytes=limit * MEBI),
        )(*args)

    return run


NAMES = ("xh", "y", "xl", "c")


def routes(sizes, move):
    pairs = []
    nx, ny = sizes
    index = lambda h, y, l, c: ((h * ny + y) * 2 + l) * 2 + c
    for h in range(nx):
        for y in range(ny):
            for l in range(2):
                for c in range(2):
                    target = move(h, y, l, c)
                    if target is not None:
                        pairs.append((index(h, y, l, c), index(*target)))
    return pairs


def per_device(high_count, primary, conductivity, observed, receivers):
    chain = CHIPS // 2
    sizes = (high_count, chain)
    def step(by, around):
        def move(h, y, l, c):
            block = 2 * y + l + by
            if block < 0 or block >= CHIPS:
                return None
            side = 2 * h + l
            if around:
                wrap = 1 if (l == 1) else -1
                side = (side + wrap) % (2 * high_count)
                return (side // 2, block // 2, side % 2, c)
            return (h, block // 2, block % 2, c)

        return routes(sizes, move)

    def send(x, pairs):
        return lax.ppermute(x, NAMES, pairs)

    fields = primary[0]
    swap = routes(sizes, lambda h, y, l, c: (h, y, l, 1 - c))
    p_low = send(fields, step(1, False))
    p_high = send(fields, step(-1, False))
    c_low = send(conductivity, step(1, True))
    c_high = send(conductivity, step(-1, True))

    rows, lanes = primary.shape[3], primary.shape[4]
    count = receivers.shape[1]
    f32 = lambda *shape: (shape, F32)
    four = f32(KEPT, rows, lanes)
    hot, hot_own = call(
        hot_kernel, 4, [((10 * rows, count), BF16), ((3 * KEPT * rows, count), BF16)]
    )(receivers)
    own_c, p_pair = lax.optimization_barrier((conductivity, send(fields, swap)))
    c_pair = send(own_c, swap)
    p_mid, c_mid, ky_mid, kz_mid, dg_mid, p_sample = call(
        own_kernel,
        8,
        [f32(2, KEPT, rows, lanes), four, four, four, four, f32(2, count)],
        [pltpu.VMEM((2 * lanes, 3 * KEPT * rows), BF16)],
    )(fields, p_pair, conductivity, c_pair, receivers, hot_own)
    def paired(x, ready):
        x, ready = lax.optimization_barrier((x, ready))
        return x, send(x, swap)

    p_low, p_low_pair = paired(p_low, p_sample)
    c_low, c_low_pair = paired(c_low, p_sample)
    eight = f32(8, rows, lanes)
    lows = call(
        low_kernel,
        10,
        [eight] * 5 + [f32(2, 8, rows, lanes)] * 4,
        [pltpu.VMEM((8, rows, lanes), F32)] * 2,
    )(p_mid, p_low, p_low_pair, c_mid, c_low, c_low_pair, ky_mid, kz_mid, dg_mid)
    p_high, p_high_pair = paired(p_high, lows[7])
    c_high, c_high_pair = paired(c_high, lows[7])
    *highs, sent = call(
        high_kernel,
        18,
        [f32(DEEP - cut, rows, lanes) for cut in CUTS[:5]]
        + [f32(2, DEEP - cut, rows, lanes) for cut in CUTS[5:]]
        + [f32(CHIPS, 8, count + 128)],
        [
            pltpu.VMEM((8, rows, lanes), F32),
            pltpu.VMEM((8, rows, lanes), F32),
            pltpu.VMEM((6 * lanes, 3 * KEPT * rows), BF16),
            pltpu.VMEM((6, count), F32),
        ],
    )(
        *lows, p_high, p_high_pair, c_mid, c_high, c_high_pair, dg_mid, receivers, hot_own, p_sample,
    )
    got = lax.all_to_all(sent, ("y", "xl"), 0, 0, tiled=True)
    six = (2, 6, rows, lanes)
    a0, a1, a2, pot, pred, sent = call(
        adjoint_kernel,
        18,
        [f32(*six)] * 4 + [f32(2, count), f32(CHIPS, 8, 128)],
        [pltpu.VMEM((3, 2 * lanes, count), BF16)] + [pltpu.VMEM((2, DEEP, rows, lanes), F32)] * 3,
    )(got, observed[0], receivers, hot, *lows, *highs)
    got = lax.all_to_all(sent, ("y", "xl"), 0, 0, tiled=True)
    slabs = lax.axis_size("z")
    chunks = (slabs, 6, rows // slabs, lanes)
    kept, given = call(gradient_kernel, 8, [f32(*chunks)] * 2, [pltpu.VMEM(six, F32)])(got, a0, a1, a2, pot)
    given, pred = lax.optimization_barrier((given, pred))
    total = kept + send(given, swap)
    pred_pair = send(pred, swap)
    even = lax.axis_index("c") == 0
    predicted = jnp.where(even, jnp.concatenate([pred, pred_pair]), jnp.concatenate([pred_pair, pred]))
    parts = lax.all_to_all(total, "z", 0, 0, tiled=True)
    share = jnp.sum(parts, axis=0, keepdims=True)
    if high_count > 1:
        share = share + lax.ppermute(share, "xh", [(0, 1), (1, 0)])
    spread = jnp.broadcast_to(share, chunks)
    whole = lax.all_to_all(spread, "z", 0, 0, tiled=True)
    grad = jnp.transpose(whole, (1, 0, 2, 3)).reshape(3, 2, rows, lanes)
    return grad, predicted[None]


def solution(mesh):
    groups = mesh.shape["src"]
    high = 2 if groups > 1 else 1
    devices = mesh.devices.reshape(groups // high, high, CHIPS // 2, 2, 2)
    inner = Mesh(devices, ("z", "xh", "y", "xl", "c"))
    src, dom = ("z", "xh"), ("y", "xl", "c")
    return jax.shard_map(
        functools.partial(per_device, high),
        mesh=inner,
        in_specs=(P(src, None, dom, None, None), P(None, dom, None, None), P(src, None, None), P(src, None)),
        out_specs=(P(None, dom, None, None), P(src, None, None)),
        check_vma=False,
    )
```

```python
import functools
import jax
import jax.numpy as jnp
from jax import lax
from jax.experimental import pallas as pl
from jax.experimental.pallas import tpu as pltpu
from jax.sharding import Mesh, PartitionSpec as P

F32 = jnp.float32
BF16 = jnp.bfloat16
MEBI = 1024 * 1024
DEEP = 12
KEPT = 4
CHIPS = 8
LANES = 128


def pieces_of(values):
    first = values.astype(BF16)
    rest = values - first.astype(F32)
    second = rest.astype(BF16)
    third = (rest - second.astype(F32)).astype(BF16)
    return first, second, third


def fold(plane):
    return jnp.sum(plane.reshape(plane.shape[0] // 8, 8, plane.shape[1]), axis=0)


def ahead(plane, axis):
    return pltpu.roll(plane, plane.shape[axis] - 1, axis)


def behind(plane, axis):
    return pltpu.roll(plane, 1, axis)


def neighbours(field, s, i, kx, ky, kz):
    mid = field[s, i]
    total = kx[i] * field[s, i + 1] + kx[i - 1] * field[s, i - 1]
    total = total + ky[i] * ahead(mid, 0) + behind(ky[i] * mid, 0)
    return total + kz[i] * ahead(mid, 1) + behind(kz[i] * mid, 1)


def krylov(t0, t1, t2, kx, ky, kz, dinv, dg):
    sources = t0.shape[0]

    def apply_planes(source, target, first, last):
        def body(i, carry):
            for s in range(sources):
                target[s, i] = source[s, i] - dinv[i] * neighbours(source, s, i, kx, ky, kz)
            return carry

        lax.fori_loop(first, last + 1, body, 0, unroll=True)

    apply_planes(t0, t1, 2, 9)
    apply_planes(t1, t2, 3, 8)

    def body(i, sums):
        sums = list(sums)
        for s in range(sources):
            a0, a1, a2 = t0[s, i], t1[s, i], t2[s, i]
            a3 = a2 - dinv[i] * neighbours(t2, s, i, kx, ky, kz)
            d = dg[i]
            b1 = a0 - a1
            b2 = b1 - (a1 - a2)
            b3 = b2 - ((a1 - a2) - (a2 - a3))
            d0, d1, d2, e1, e2 = d * a0, d * a1, d * a2, d * b1, d * b2
            terms = [
                d0 * a0, d0 * a1, d1 * a1, d1 * a2, d2 * a2, d2 * a3,
                d0 * b1, e1 * b1, e1 * b2, e2 * b2, e2 * b3,
            ]
            for k, term in enumerate(terms):
                sums[k * sources + s] = sums[k * sources + s] + fold(term)
        return tuple(sums)

    zero = jnp.zeros((8, t0.shape[3]), F32)
    sums = lax.fori_loop(4, 8, body, (zero,) * (11 * sources), unroll=True)
    row_at = lax.broadcasted_iota(jnp.int32, (8, 128), 0)
    lane_at = lax.broadcasted_iota(jnp.int32, (8, 128), 1)
    packed = jnp.zeros((8, 128), F32)
    for n, x in enumerate(sums):
        here = jnp.logical_and(row_at == n % sources, lane_at == n // sources)
        packed = jnp.where(here, jnp.sum(x), packed)
    return packed


def weights_of(moments):
    t = [moments[0:2, k : k + 1] for k in range(6)]
    m = [t[0]] + [moments[0:2, k : k + 1] for k in range(6, 11)]
    near = t[1] < 0.5 * t[0]
    g = [jnp.where(near, t[k + 1], m[k] - m[k + 1]) for k in range(5)]
    h = [jnp.where(near, t[k], m[k]) for k in range(3)]
    l1 = g[1] / g[0]
    l2 = g[2] / g[0]
    d1 = g[2] - l1 * g[1]
    e2 = g[3] - l2 * g[1]
    l21 = e2 / d1
    d2 = g[4] - l2 * g[2] - l21 * e2
    y1 = h[1] - l1 * h[0]
    y2 = h[2] - l2 * h[0] - l21 * y1
    c2 = y2 / d2
    c1 = y1 / d1 - l21 * c2
    c0 = h[0] / g[0] - l1 * c1 - l2 * c2
    w0 = jnp.where(near, c0, c0 + c1 + c2)
    w1 = jnp.where(near, c1, -(c1 + 2.0 * c2))
    return w0, w1, c2


def one_hot(count, first, picked):
    place = lax.broadcasted_iota(jnp.int32, (count, picked.shape[1]), 0) + first
    return place == picked


def edges(rows, lanes):
    row_at = lax.broadcasted_iota(jnp.int32, (rows, lanes), 0)
    lane_at = lax.broadcasted_iota(jnp.int32, (rows, lanes), 1)
    mask_y = jnp.where(row_at < rows - 1, 1.0, 0.0).astype(F32)
    mask_z = jnp.where(lane_at < lanes - 1, 1.0, 0.0).astype(F32)
    return row_at, lane_at, mask_y, mask_z


def in_plane(along_y, along_z):
    rows, lanes = along_y.shape
    row_at, lane_at, mask_y, mask_z = edges(rows, lanes)
    up_y = 0.5 * (along_y + ahead(along_y, 0)) * mask_y
    up_z = 0.5 * (along_z + ahead(along_z, 1)) * mask_z
    low_y = jnp.where(row_at == 0, 0.5 * along_y, behind(up_y, 0))
    low_z = jnp.where(lane_at == 0, 0.5 * along_z, behind(up_z, 1))
    top_y = jnp.where(row_at == rows - 1, 0.5 * along_y, up_y)
    top_z = jnp.where(lane_at == lanes - 1, 0.5 * along_z, up_z)
    return up_y, up_z, top_y + low_y + top_z + low_z


def hot_kernel(cells, hot, hot_own):
    block = 2 * lax.axis_index("y") + lax.axis_index("xl")
    rows = hot.shape[0] // 10
    row_of = cells[...] // LANES
    for i in range(10):
        rows_hot = one_hot(rows, (4 * block - 3 + i) * rows, row_of)
        rows_hot = jnp.where(rows_hot, 1.0, 0.0).astype(BF16)
        hot[pl.ds(i * rows, rows)] = rows_hot
        if 3 <= i < 7:
            for piece in range(3):
                hot_own[pl.ds((piece * KEPT + i - 3) * rows, rows)] = rows_hot


def own_kernel(p_own, p_pair, c_own, c_pair, cells, hot_own, prim, first, ky, kz, plane_dg, sample, left):
    core = lax.axis_index("c")
    here = pl.ds(2 * core, 2)
    other = pl.ds(2 - 2 * core, 2)
    prim[:, here] = p_own[here]
    prim[:, other] = p_pair[here]
    first[here] = c_own[0]
    first[other] = c_pair[0]
    rows, lanes = prim.shape[2], prim.shape[3]
    for source, base in ((c_own, 2 * core), (c_pair, 2 - 2 * core)):
        for j in range(2):
            up_y, up_z, part = in_plane(source[1, j], source[2, j])
            ky[base + j] = up_y
            kz[base + j] = up_z
            plane_dg[base + j] = part
    picked = cells[...]
    lane_of = picked - (picked // lanes) * lanes
    gather([(prim, 0)], left, hot_own, one_hot(lanes, 0, lane_of), sample)


def gather(fields, left, hot_own, lane_hot, sample):
    lanes = lane_hot.shape[0]
    for f, (field, first) in enumerate(fields):
        rows = field.shape[2]
        for s in range(2):
            for j in range(KEPT):
                parts = pieces_of(jnp.transpose(field[s, first + j]))
                for k in range(3):
                    start = (k * KEPT + j) * rows
                    left[pl.ds((2 * f + s) * lanes, lanes), start : start + rows] = parts[k]
    spread = jnp.dot(left[...], hot_own[...], preferred_element_type=F32)
    found = [
        jnp.sum(jnp.where(lane_hot, spread[k * lanes : (k + 1) * lanes], 0.0), axis=0, keepdims=True)
        for k in range(2 * len(fields))
    ]
    sample[...] = jnp.concatenate(found, axis=0)


def forward_kernel(
    p_mid, p_near, p_near_pair, p_far, p_far_pair,
    c_mid, c_near, c_near_pair, c_far, c_far_pair, ky_mid, kz_mid, dg_mid, cells, hot_own, p_sample,
    kx, ky, kz, dinv, dg, prim, t0, t1, t2, sent, cond, left, found,
):
    block = 2 * lax.axis_index("y") + lax.axis_index("xl")
    core = lax.axis_index("c")
    here = pl.ds(2 * core, 2)
    prim[:, 4:8] = p_mid[...]
    cond[4:8] = c_mid[...]
    far = 8 * lax.axis_index("xl")
    near = 8 - far
    for base, first, second in ((near, p_near, p_near_pair), (far, p_far, p_far_pair)):
        prim[:, pl.ds(base + 2 * core, 2)] = first[here]
        prim[:, pl.ds(base + 2 - 2 * core, 2)] = second[here]
    for base, first, second in ((near, c_near, c_near_pair), (far, c_far, c_far_pair)):
        cond[pl.ds(base + 2 * core, 2)] = first[0]
        cond[pl.ds(base + 2 - 2 * core, 2)] = second[0]
        for source, start in ((first, base + 2 * core), (second, base + 2 - 2 * core)):
            for j in range(2):
                up_y, up_z, part = in_plane(source[1, j], source[2, j])
                ky[start + j] = up_y
                kz[start + j] = up_z
                dg[start + j] = part
    ky[4:8] = ky_mid[...]
    kz[4:8] = kz_mid[...]
    dg[4:8] = dg_mid[...]
    rows, lanes = prim.shape[2], prim.shape[3]
    row_at, lane_at, mask_y, mask_z = edges(rows, lanes)
    edge = jnp.where(row_at == 0, 0.5, 0.0) + jnp.where(row_at == rows - 1, 0.5, 0.0)
    edge = edge + jnp.where(lane_at == 0, 0.5, 0.0) + jnp.where(lane_at == lanes - 1, 0.5, 0.0)
    unit = (6.0 - edge).astype(F32)
    layers = 4 * CHIPS

    kx[0] = 0.5 * (cond[0] + cond[1])

    def coefficients(i, carry):
        layer = 4 * block - 4 + i
        inside = jnp.where(jnp.logical_and(layer >= 0, layer < layers), 1.0, 0.0).astype(F32)
        first = 0.5 * (cond[i] + cond[i + 1])
        kx[i] = first
        diagonal = first + kx[i - 1] + dg[i]
        inverse = jnp.where(inside > 0.5, 1.0 / diagonal, 0.0)
        dg[i] = diagonal
        dinv[i] = inverse
        return carry

    lax.fori_loop(1, 11, coefficients, 0)

    def right_side(i, carry):
        layer = 4 * block - 4 + i
        outer = jnp.where(jnp.logical_or(layer == 0, layer == layers - 1), 0.5, 0.0).astype(F32)
        diagonal = (unit - outer) - dg[i]
        upper, lower = 1.0 - kx[i], 1.0 - kx[i - 1]
        diff_y = mask_y - ky[i]
        diff_z = mask_z - kz[i]
        inverse = dinv[i]
        for s in range(2):
            mid = prim[s, i]
            total = diagonal * mid - upper * prim[s, i + 1] - lower * prim[s, i - 1]
            total = total - diff_y * ahead(mid, 0) - behind(diff_y * mid, 0)
            total = total - diff_z * ahead(mid, 1) - behind(diff_z * mid, 1)
            t0[s, i] = inverse * total
        return carry

    lax.fori_loop(1, 11, right_side, 0, unroll=True)
    moments = krylov(t0, t1, t2, kx, ky, kz, dinv, dg)

    picked = cells[...]
    lane_of = picked - (picked // lanes) * lanes
    count = picked.shape[1]
    gather([(t0, 4), (t1, 4), (t2, 4)], left, hot_own, one_hot(lanes, 0, lane_of), found)
    for k in range(CHIPS):
        sent[k, 0:2, :count] = p_sample[...]
        sent[k, 2:8, :count] = found[...]
        sent[k, :, count:] = moments


def adjoint_kernel(
    got, observed, cells, hot, kx, ky, kz, dinv, dg, prim, f0, f1, f2,
    b0, b1, b2, pot, predicted, sent, heavy, a0, a1, a2,
):
    core = lax.axis_index("c")
    rows, lanes = prim.shape[2], prim.shape[3]
    count = cells.shape[1]
    total = got[0]
    for k in range(1, CHIPS):
        total = total + got[k]
    weights = weights_of(total[:, count:])
    sample = total[:, :count]
    value = sample[0:2]
    for k in range(3):
        value = value + weights[k] * sample[2 * k + 2 : 2 * k + 4]
    predicted[...] = value
    seen = jnp.where(core == 0, observed[0:2], observed[2:4])
    misfit = value - seen
    for i in range(6):
        for s in range(2):
            w = [weights[k][s : s + 1, :] for k in range(3)]
            pot[s, i] = prim[s, i + 3] + w[0] * f0[s, i + 3] + w[1] * f1[s, i + 3] + w[2] * f2[s, i + 3]

    picked = cells[...]
    lane_of = picked - (picked // lanes) * lanes
    lane_hot = one_hot(lanes, 0, lane_of)
    for s in range(2):
        spread = jnp.where(lane_hot, misfit[s : s + 1], 0.0)
        for k, piece in enumerate(pieces_of(spread)):
            heavy[k, pl.ds(s * lanes, lanes)] = piece
    placed = [
        lax.dot_general(hot[...], heavy[k], (((1,), (1,)), ((), ())), preferred_element_type=F32)
        for k in range(3)
    ]
    source = placed[0] + placed[1] + placed[2]
    for i in range(10):
        inverse = dinv[i + 1]
        for s in range(2):
            a0[s, i + 1] = inverse * source[i * rows : (i + 1) * rows, s * lanes : (s + 1) * lanes]
    moments = krylov(a0, a1, a2, kx, ky, kz, dinv, dg)
    for k in range(CHIPS):
        sent[k] = moments
    for near, deep in ((b0, a0), (b1, a1), (b2, a2)):
        near[...] = deep[:, 3:9]


def gradient_kernel(got, a0, a1, a2, pot, kept, given, adj):
    core = lax.axis_index("c")
    moments = got[0]
    for k in range(1, CHIPS):
        moments = moments + got[k]
    weights = weights_of(moments)
    rows, lanes = pot.shape[2], pot.shape[3]
    row_at = lax.broadcasted_iota(jnp.int32, (rows, lanes), 0)
    lane_at = lax.broadcasted_iota(jnp.int32, (rows, lanes), 1)
    for i in range(6):
        for s in range(2):
            w = [weights[k][s : s + 1, :] for k in range(3)]
            adj[s, i] = w[0] * a0[s, i] + w[1] * a1[s, i] + w[2] * a2[s, i]

    def along(mid_p, mid_a, axis, at):
        last = mid_p.shape[axis] - 1
        next_p = jnp.where(at == last, 0.0, ahead(mid_p, axis))
        next_a = jnp.where(at == last, 0.0, ahead(mid_a, axis))
        upper = (mid_p - next_p) * (mid_a - next_a)
        lower = jnp.where(at == 0, mid_p * mid_a, behind(upper, axis))
        return upper + lower

    for target, first in ((given, 1 + 2 * (1 - core)), (kept, 1 + 2 * core)):
        for j in range(2):
            i = first + j
            sums = [0.0, 0.0, 0.0]
            for s in range(2):
                mid_p, mid_a = pot[s, i], adj[s, i]
                upper = (mid_p - pot[s, i + 1]) * (mid_a - adj[s, i + 1])
                lower = (mid_p - pot[s, i - 1]) * (mid_a - adj[s, i - 1])
                sums[0] = sums[0] + upper + lower
                sums[1] = sums[1] + along(mid_p, mid_a, 0, row_at)
                sums[2] = sums[2] + along(mid_p, mid_a, 1, lane_at)
            for k in range(3):
                target[:, 2 * k + j] = (-0.5 * sums[k]).reshape(target.shape[0], target.shape[2], lanes)


def call(kernel, limit, outs, scratch=()):
    vmem = pl.BlockSpec(memory_space=pltpu.VMEM)

    def run(*args):
        return pl.pallas_call(
            kernel,
            out_shape=tuple(jax.ShapeDtypeStruct(x, kind) for x, kind in outs),
            in_specs=[vmem] * len(args),
            out_specs=tuple([vmem] * len(outs)),
            scratch_shapes=list(scratch),
            compiler_params=pltpu.CompilerParams(vmem_limit_bytes=limit * MEBI),
        )(*args)

    return run


NAMES = ("xh", "y", "xl", "c")


def routes(sizes, move):
    pairs = []
    nx, ny = sizes
    index = lambda h, y, l, c: ((h * ny + y) * 2 + l) * 2 + c
    for h in range(nx):
        for y in range(ny):
            for l in range(2):
                for c in range(2):
                    target = move(h, y, l, c)
                    if target is not None:
                        pairs.append((index(h, y, l, c), index(*target)))
    return pairs


def per_device(high_count, primary, conductivity, observed, receivers):
    chain = CHIPS // 2
    sizes = (high_count, chain)
    def beside(h, y, l, c):
        return (h, y, 1 - l, c)

    def around(h, y, l, c):
        side = (2 * h + l + (1 if l == 1 else -1)) % (2 * high_count)
        return (side // 2, y, side % 2, c)

    def along(sign):
        def move(h, y, l, c):
            target = y + sign * (1 if l == 0 else -1)
            return (h, target, l, c) if 0 <= target < chain else None

        return routes(sizes, move)

    def send(x, pairs):
        return lax.ppermute(x, NAMES, pairs)

    fields = primary[0]
    swap = routes(sizes, lambda h, y, l, c: (h, y, l, 1 - c))
    p_near = send(fields, routes(sizes, beside))
    c_near = send(conductivity, routes(sizes, around))
    c_next = send(conductivity, along(-1))
    p_far = send(p_near, along(1))
    c_far = send(c_next, routes(sizes, beside))

    rows, lanes = primary.shape[3], primary.shape[4]
    count = receivers.shape[1]
    f32 = lambda *shape: (shape, F32)
    deep = f32(DEEP, rows, lanes)
    pairs = f32(2, DEEP, rows, lanes)
    four = f32(KEPT, rows, lanes)
    hot, hot_own = call(
        hot_kernel, 4, [((10 * rows, count), BF16), ((3 * KEPT * rows, count), BF16)]
    )(receivers)
    own_c, p_pair = lax.optimization_barrier((conductivity, send(fields, swap)))
    c_pair = send(own_c, swap)
    p_mid, c_mid, ky_mid, kz_mid, dg_mid, p_sample = call(
        own_kernel,
        8,
        [f32(2, KEPT, rows, lanes), four, four, four, four, f32(2, count)],
        [pltpu.VMEM((2 * lanes, 3 * KEPT * rows), BF16)],
    )(fields, p_pair, conductivity, c_pair, receivers, hot_own)
    ready = p_sample
    pairs_of = []
    for x in (p_near, c_near, c_far, p_far):
        x, token = lax.optimization_barrier((x, ready))
        pairs_of.append(send(x, swap))
    p_near_pair, c_near_pair, c_far_pair, p_far_pair = pairs_of
    kx, ky, kz, dinv, dg, prim, f0, f1, f2, sent = call(
        forward_kernel,
        20,
        [deep] * 5 + [pairs] * 4 + [f32(CHIPS, 8, count + 128)],
        [
            pltpu.VMEM((DEEP, rows, lanes), F32),
            pltpu.VMEM((6 * lanes, 3 * KEPT * rows), BF16),
            pltpu.VMEM((6, count), F32),
        ],
    )(
        p_mid, p_near, p_near_pair, p_far, p_far_pair,
        c_mid, c_near, c_near_pair, c_far, c_far_pair, ky_mid, kz_mid, dg_mid, receivers, hot_own, p_sample,
    )
    got = lax.all_to_all(sent, ("y", "xl"), 0, 0, tiled=True)
    six = (2, 6, rows, lanes)
    a0, a1, a2, pot, pred, sent = call(
        adjoint_kernel,
        18,
        [f32(*six)] * 4 + [f32(2, count), f32(CHIPS, 8, 128)],
        [pltpu.VMEM((3, 2 * lanes, count), BF16)] + [pltpu.VMEM((2, DEEP, rows, lanes), F32)] * 3,
    )(got, observed[0], receivers, hot, kx, ky, kz, dinv, dg, prim, f0, f1, f2)
    got = lax.all_to_all(sent, ("y", "xl"), 0, 0, tiled=True)
    slabs = lax.axis_size("z")
    chunks = (slabs, 6, rows // slabs, lanes)
    kept, given = call(gradient_kernel, 8, [f32(*chunks)] * 2, [pltpu.VMEM(six, F32)])(got, a0, a1, a2, pot)
    given, pred = lax.optimization_barrier((given, pred))
    total = kept + send(given, swap)
    pred_pair = send(pred, swap)
    even = lax.axis_index("c") == 0
    predicted = jnp.where(even, jnp.concatenate([pred, pred_pair]), jnp.concatenate([pred_pair, pred]))
    parts = lax.all_to_all(total, "z", 0, 0, tiled=True)
    share = jnp.sum(parts, axis=0, keepdims=True)
    if high_count > 1:
        share = share + lax.ppermute(share, "xh", [(0, 1), (1, 0)])
    spread = jnp.broadcast_to(share, chunks)
    whole = lax.all_to_all(spread, "z", 0, 0, tiled=True)
    grad = jnp.transpose(whole, (1, 0, 2, 3)).reshape(3, 2, rows, lanes)
    return grad, predicted[None]


def solution(mesh):
    groups = mesh.shape["src"]
    high = 2 if groups > 1 else 1
    devices = mesh.devices.reshape(groups // high, high, CHIPS // 2, 2, 2)
    inner = Mesh(devices, ("z", "xh", "y", "xl", "c"))
    src, dom = ("z", "xh"), ("y", "xl", "c")
    return jax.shard_map(
        functools.partial(per_device, high),
        mesh=inner,
        in_specs=(P(src, None, dom, None, None), P(None, dom, None, None), P(src, None, None), P(src, None)),
        out_specs=(P(None, dom, None, None), P(src, None, None)),
        check_vma=False,
    )
```

```python
import functools
import jax
import jax.numpy as jnp
from jax import lax
from jax.experimental import pallas as pl
from jax.experimental.pallas import tpu as pltpu
from jax.sharding import Mesh, PartitionSpec as P

F32 = jnp.float32
BF16 = jnp.bfloat16
MEBI = 1024 * 1024
DEEP = 12
KEPT = 4
CHIPS = 8
LANES = 128


def pieces_of(values):
    first = values.astype(BF16)
    rest = values - first.astype(F32)
    second = rest.astype(BF16)
    third = (rest - second.astype(F32)).astype(BF16)
    return first, second, third


def fold(plane):
    return jnp.sum(plane.reshape(plane.shape[0] // 8, 8, plane.shape[1]), axis=0)


def ahead(plane, axis):
    return pltpu.roll(plane, plane.shape[axis] - 1, axis)


def behind(plane, axis):
    return pltpu.roll(plane, 1, axis)


def neighbours(field, s, i, kx, ky, kz):
    mid = field[s, i]
    total = kx[i] * field[s, i + 1] + kx[i - 1] * field[s, i - 1]
    total = total + ky[i] * ahead(mid, 0) + behind(ky[i] * mid, 0)
    return total + kz[i] * ahead(mid, 1) + behind(kz[i] * mid, 1)


def krylov(t0, t1, t2, kx, ky, kz, dinv, dg):
    sources = t0.shape[0]

    def apply_planes(source, target, first, last):
        def body(i, carry):
            for s in range(sources):
                target[s, i] = source[s, i] - dinv[i] * neighbours(source, s, i, kx, ky, kz)
            return carry

        lax.fori_loop(first, last + 1, body, 0, unroll=True)

    apply_planes(t0, t1, 2, 9)
    apply_planes(t1, t2, 3, 8)

    def body(i, sums):
        sums = list(sums)
        for s in range(sources):
            a0, a1, a2 = t0[s, i], t1[s, i], t2[s, i]
            a3 = a2 - dinv[i] * neighbours(t2, s, i, kx, ky, kz)
            d = dg[i]
            b1 = a0 - a1
            b2 = b1 - (a1 - a2)
            b3 = b2 - ((a1 - a2) - (a2 - a3))
            d0, d1, d2, e1, e2 = d * a0, d * a1, d * a2, d * b1, d * b2
            terms = [
                d0 * a0, d0 * a1, d1 * a1, d1 * a2, d2 * a2, d2 * a3,
                d0 * b1, e1 * b1, e1 * b2, e2 * b2, e2 * b3,
            ]
            for k, term in enumerate(terms):
                sums[k * sources + s] = sums[k * sources + s] + fold(term)
        return tuple(sums)

    zero = jnp.zeros((8, t0.shape[3]), F32)
    sums = lax.fori_loop(4, 8, body, (zero,) * (11 * sources), unroll=True)
    row_at = lax.broadcasted_iota(jnp.int32, (8, 128), 0)
    lane_at = lax.broadcasted_iota(jnp.int32, (8, 128), 1)
    packed = jnp.zeros((8, 128), F32)
    for n, x in enumerate(sums):
        here = jnp.logical_and(row_at == n % sources, lane_at == n // sources)
        packed = jnp.where(here, jnp.sum(x), packed)
    return packed


def weights_of(moments):
    t = [moments[0:2, k : k + 1] for k in range(6)]
    m = [t[0]] + [moments[0:2, k : k + 1] for k in range(6, 11)]
    near = t[1] < 0.5 * t[0]
    g = [jnp.where(near, t[k + 1], m[k] - m[k + 1]) for k in range(5)]
    h = [jnp.where(near, t[k], m[k]) for k in range(3)]
    l1 = g[1] / g[0]
    l2 = g[2] / g[0]
    d1 = g[2] - l1 * g[1]
    e2 = g[3] - l2 * g[1]
    l21 = e2 / d1
    d2 = g[4] - l2 * g[2] - l21 * e2
    y1 = h[1] - l1 * h[0]
    y2 = h[2] - l2 * h[0] - l21 * y1
    c2 = y2 / d2
    c1 = y1 / d1 - l21 * c2
    c0 = h[0] / g[0] - l1 * c1 - l2 * c2
    w0 = jnp.where(near, c0, c0 + c1 + c2)
    w1 = jnp.where(near, c1, -(c1 + 2.0 * c2))
    return w0, w1, c2


def one_hot(count, first, picked):
    place = lax.broadcasted_iota(jnp.int32, (count, picked.shape[1]), 0) + first
    return place == picked


def edges(rows, lanes):
    row_at = lax.broadcasted_iota(jnp.int32, (rows, lanes), 0)
    lane_at = lax.broadcasted_iota(jnp.int32, (rows, lanes), 1)
    mask_y = jnp.where(row_at < rows - 1, 1.0, 0.0).astype(F32)
    mask_z = jnp.where(lane_at < lanes - 1, 1.0, 0.0).astype(F32)
    return row_at, lane_at, mask_y, mask_z


def in_plane(along_y, along_z):
    rows, lanes = along_y.shape
    row_at, lane_at, mask_y, mask_z = edges(rows, lanes)
    up_y = 0.5 * (along_y + ahead(along_y, 0)) * mask_y
    up_z = 0.5 * (along_z + ahead(along_z, 1)) * mask_z
    low_y = jnp.where(row_at == 0, 0.5 * along_y, behind(up_y, 0))
    low_z = jnp.where(lane_at == 0, 0.5 * along_z, behind(up_z, 1))
    top_y = jnp.where(row_at == rows - 1, 0.5 * along_y, up_y)
    top_z = jnp.where(lane_at == lanes - 1, 0.5 * along_z, up_z)
    return up_y, up_z, top_y + low_y + top_z + low_z


def hot_kernel(cells, hot, hot_own):
    block = 2 * lax.axis_index("y") + lax.axis_index("xl")
    rows = hot.shape[0] // 10
    row_of = cells[...] // LANES
    for i in range(10):
        rows_hot = one_hot(rows, (4 * block - 3 + i) * rows, row_of)
        rows_hot = jnp.where(rows_hot, 1.0, 0.0).astype(BF16)
        hot[pl.ds(i * rows, rows)] = rows_hot
        if 3 <= i < 7:
            for piece in range(3):
                hot_own[pl.ds((piece * KEPT + i - 3) * rows, rows)] = rows_hot


def own_kernel(p_own, p_pair, c_own, c_pair, cells, hot_own, prim, first, ky, kz, plane_dg, sample, left):
    core = lax.axis_index("c")
    here = pl.ds(2 * core, 2)
    other = pl.ds(2 - 2 * core, 2)
    prim[:, here] = p_own[here]
    prim[:, other] = p_pair[here]
    first[here] = c_own[0]
    first[other] = c_pair[0]
    rows, lanes = prim.shape[2], prim.shape[3]
    for source, base in ((c_own, 2 * core), (c_pair, 2 - 2 * core)):
        for j in range(2):
            up_y, up_z, part = in_plane(source[1, j], source[2, j])
            ky[base + j] = up_y
            kz[base + j] = up_z
            plane_dg[base + j] = part
    picked = cells[...]
    lane_of = picked - (picked // lanes) * lanes
    gather([(prim, 0)], left, hot_own, one_hot(lanes, 0, lane_of), sample)


def gather(fields, left, hot_own, lane_hot, sample):
    lanes = lane_hot.shape[0]
    for f, (field, first) in enumerate(fields):
        rows = field.shape[2]
        for s in range(2):
            for j in range(KEPT):
                parts = pieces_of(jnp.transpose(field[s, first + j]))
                for k in range(3):
                    start = (k * KEPT + j) * rows
                    left[pl.ds((2 * f + s) * lanes, lanes), start : start + rows] = parts[k]
    spread = jnp.dot(left[...], hot_own[...], preferred_element_type=F32)
    found = [
        jnp.sum(jnp.where(lane_hot, spread[k * lanes : (k + 1) * lanes], 0.0), axis=0, keepdims=True)
        for k in range(2 * len(fields))
    ]
    sample[...] = jnp.concatenate(found, axis=0)


def forward_kernel(
    p_mid, p_near, p_near_pair, p_far, p_far_pair,
    c_mid, c_near, c_near_pair, c_far, c_far_pair, ky_mid, kz_mid, dg_mid, cells, hot_own, p_sample,
    kx, ky, kz, dinv, dg, prim, t0, t1, t2, sent, cond, left, found,
):
    block = 2 * lax.axis_index("y") + lax.axis_index("xl")
    core = lax.axis_index("c")
    here = pl.ds(2 * core, 2)
    prim[:, 4:8] = p_mid[...]
    cond[4:8] = c_mid[...]
    far = 8 * lax.axis_index("xl")
    near = 8 - far
    for base, first, second in ((near, p_near, p_near_pair), (far, p_far, p_far_pair)):
        prim[:, pl.ds(base + 2 * core, 2)] = first[here]
        prim[:, pl.ds(base + 2 - 2 * core, 2)] = second[here]
    for base, first, second in ((near, c_near, c_near_pair), (far, c_far, c_far_pair)):
        cond[pl.ds(base + 2 * core, 2)] = first[0]
        cond[pl.ds(base + 2 - 2 * core, 2)] = second[0]
        for source, start in ((first, base + 2 * core), (second, base + 2 - 2 * core)):
            for j in range(2):
                up_y, up_z, part = in_plane(source[1, j], source[2, j])
                ky[start + j] = up_y
                kz[start + j] = up_z
                dg[start + j] = part
    ky[4:8] = ky_mid[...]
    kz[4:8] = kz_mid[...]
    dg[4:8] = dg_mid[...]
    rows, lanes = prim.shape[2], prim.shape[3]
    row_at, lane_at, mask_y, mask_z = edges(rows, lanes)
    edge = jnp.where(row_at == 0, 0.5, 0.0) + jnp.where(row_at == rows - 1, 0.5, 0.0)
    edge = edge + jnp.where(lane_at == 0, 0.5, 0.0) + jnp.where(lane_at == lanes - 1, 0.5, 0.0)
    unit = (6.0 - edge).astype(F32)
    layers = 4 * CHIPS

    kx[0] = 0.5 * (cond[0] + cond[1])

    def coefficients(i, carry):
        layer = 4 * block - 4 + i
        inside = jnp.where(jnp.logical_and(layer >= 0, layer < layers), 1.0, 0.0).astype(F32)
        first = 0.5 * (cond[i] + cond[i + 1])
        kx[i] = first
        diagonal = first + kx[i - 1] + dg[i]
        inverse = jnp.where(inside > 0.5, 1.0 / diagonal, 0.0)
        dg[i] = diagonal
        dinv[i] = inverse
        return carry

    lax.fori_loop(1, 11, coefficients, 0)

    def right_side(i, carry):
        layer = 4 * block - 4 + i
        outer = jnp.where(jnp.logical_or(layer == 0, layer == layers - 1), 0.5, 0.0).astype(F32)
        diagonal = (unit - outer) - dg[i]
        upper, lower = 1.0 - kx[i], 1.0 - kx[i - 1]
        diff_y = mask_y - ky[i]
        diff_z = mask_z - kz[i]
        inverse = dinv[i]
        for s in range(2):
            mid = prim[s, i]
            total = diagonal * mid - upper * prim[s, i + 1] - lower * prim[s, i - 1]
            total = total - diff_y * ahead(mid, 0) - behind(diff_y * mid, 0)
            total = total - diff_z * ahead(mid, 1) - behind(diff_z * mid, 1)
            t0[s, i] = inverse * total
        return carry

    lax.fori_loop(1, 11, right_side, 0, unroll=True)
    moments = krylov(t0, t1, t2, kx, ky, kz, dinv, dg)

    picked = cells[...]
    lane_of = picked - (picked // lanes) * lanes
    count = picked.shape[1]
    gather([(t0, 4), (t1, 4), (t2, 4)], left, hot_own, one_hot(lanes, 0, lane_of), found)
    for k in range(CHIPS):
        sent[k, 0:2, :count] = p_sample[...]
        sent[k, 2:8, :count] = found[...]
        sent[k, :, count:] = moments


def adjoint_kernel(
    got, observed, cells, hot, kx, ky, kz, dinv, dg, prim, f0, f1, f2,
    b0, b1, b2, pot, predicted, sent, heavy, a0, a1, a2,
):
    core = lax.axis_index("c")
    rows, lanes = prim.shape[2], prim.shape[3]
    count = cells.shape[1]
    total = got[0]
    for k in range(1, CHIPS):
        total = total + got[k]
    weights = weights_of(total[:, count:])
    sample = total[:, :count]
    value = sample[0:2]
    for k in range(3):
        value = value + weights[k] * sample[2 * k + 2 : 2 * k + 4]
    predicted[...] = value
    seen = jnp.where(core == 0, observed[0:2], observed[2:4])
    misfit = value - seen
    for i in range(6):
        for s in range(2):
            w = [weights[k][s : s + 1, :] for k in range(3)]
            pot[s, i] = prim[s, i + 3] + w[0] * f0[s, i + 3] + w[1] * f1[s, i + 3] + w[2] * f2[s, i + 3]

    picked = cells[...]
    lane_of = picked - (picked // lanes) * lanes
    lane_hot = one_hot(lanes, 0, lane_of)
    for s in range(2):
        spread = jnp.where(lane_hot, misfit[s : s + 1], 0.0)
        for k, piece in enumerate(pieces_of(spread)):
            heavy[k, pl.ds(s * lanes, lanes)] = piece
    placed = [
        lax.dot_general(hot[...], heavy[k], (((1,), (1,)), ((), ())), preferred_element_type=F32)
        for k in range(3)
    ]
    source = placed[0] + placed[1] + placed[2]
    for i in range(10):
        inverse = dinv[i + 1]
        for s in range(2):
            a0[s, i + 1] = inverse * source[i * rows : (i + 1) * rows, s * lanes : (s + 1) * lanes]
    moments = krylov(a0, a1, a2, kx, ky, kz, dinv, dg)
    for k in range(CHIPS):
        sent[k] = moments
    for near, deep in ((b0, a0), (b1, a1), (b2, a2)):
        near[...] = deep[:, 3:9]


def gradient_kernel(got, a0, a1, a2, pot, kept, given, adj):
    core = lax.axis_index("c")
    moments = got[0]
    for k in range(1, CHIPS):
        moments = moments + got[k]
    weights = weights_of(moments)
    rows, lanes = pot.shape[2], pot.shape[3]
    row_at = lax.broadcasted_iota(jnp.int32, (rows, lanes), 0)
    lane_at = lax.broadcasted_iota(jnp.int32, (rows, lanes), 1)
    for i in range(6):
        for s in range(2):
            w = [weights[k][s : s + 1, :] for k in range(3)]
            adj[s, i] = w[0] * a0[s, i] + w[1] * a1[s, i] + w[2] * a2[s, i]

    def along(mid_p, mid_a, axis, at):
        last = mid_p.shape[axis] - 1
        next_p = jnp.where(at == last, 0.0, ahead(mid_p, axis))
        next_a = jnp.where(at == last, 0.0, ahead(mid_a, axis))
        upper = (mid_p - next_p) * (mid_a - next_a)
        lower = jnp.where(at == 0, mid_p * mid_a, behind(upper, axis))
        return upper + lower

    for target, first in ((given, 1 + 2 * (1 - core)), (kept, 1 + 2 * core)):
        for j in range(2):
            i = first + j
            sums = [0.0, 0.0, 0.0]
            for s in range(2):
                mid_p, mid_a = pot[s, i], adj[s, i]
                upper = (mid_p - pot[s, i + 1]) * (mid_a - adj[s, i + 1])
                lower = (mid_p - pot[s, i - 1]) * (mid_a - adj[s, i - 1])
                sums[0] = sums[0] + upper + lower
                sums[1] = sums[1] + along(mid_p, mid_a, 0, row_at)
                sums[2] = sums[2] + along(mid_p, mid_a, 1, lane_at)
            for k in range(3):
                target[:, 2 * k + j] = (-0.5 * sums[k]).reshape(target.shape[0], target.shape[2], lanes)


def call(kernel, limit, outs, scratch=()):
    vmem = pl.BlockSpec(memory_space=pltpu.VMEM)

    def run(*args):
        return pl.pallas_call(
            kernel,
            out_shape=tuple(jax.ShapeDtypeStruct(x, kind) for x, kind in outs),
            in_specs=[vmem] * len(args),
            out_specs=tuple([vmem] * len(outs)),
            scratch_shapes=list(scratch),
            compiler_params=pltpu.CompilerParams(vmem_limit_bytes=limit * MEBI),
        )(*args)

    return run


NAMES = ("xh", "y", "xl", "c")


def routes(sizes, move):
    pairs = []
    nx, ny = sizes
    index = lambda h, y, l, c: ((h * ny + y) * 2 + l) * 2 + c
    for h in range(nx):
        for y in range(ny):
            for l in range(2):
                for c in range(2):
                    target = move(h, y, l, c)
                    if target is not None:
                        pairs.append((index(h, y, l, c), index(*target)))
    return pairs


def per_device(high_count, primary, conductivity, observed, receivers):
    chain = CHIPS // 2
    sizes = (high_count, chain)
    def beside(h, y, l, c):
        return (h, y, 1 - l, c)

    def around(h, y, l, c):
        side = (2 * h + l + (1 if l == 1 else -1)) % (2 * high_count)
        return (side // 2, y, side % 2, c)

    def along(sign):
        def move(h, y, l, c):
            target = y + sign * (1 if l == 0 else -1)
            return (h, target, l, c) if 0 <= target < chain else None

        return routes(sizes, move)

    def send(x, pairs):
        return lax.ppermute(x, NAMES, pairs)

    fields = primary[0]
    swap = routes(sizes, lambda h, y, l, c: (h, y, l, 1 - c))
    p_near = send(fields, routes(sizes, beside))
    c_near = send(conductivity, routes(sizes, around))
    c_next = send(conductivity, along(-1))
    p_near, c_near = lax.optimization_barrier((p_near, c_near))
    p_far = send(p_near, along(1))
    c_far = send(c_next, routes(sizes, beside))

    rows, lanes = primary.shape[3], primary.shape[4]
    count = receivers.shape[1]
    f32 = lambda *shape: (shape, F32)
    deep = f32(DEEP, rows, lanes)
    pairs = f32(2, DEEP, rows, lanes)
    four = f32(KEPT, rows, lanes)
    hot, hot_own = call(
        hot_kernel, 4, [((10 * rows, count), BF16), ((3 * KEPT * rows, count), BF16)]
    )(receivers)
    own_c, p_pair = lax.optimization_barrier((conductivity, send(fields, swap)))
    c_pair = send(own_c, swap)
    p_mid, c_mid, ky_mid, kz_mid, dg_mid, p_sample = call(
        own_kernel,
        8,
        [f32(2, KEPT, rows, lanes), four, four, four, four, f32(2, count)],
        [pltpu.VMEM((2 * lanes, 3 * KEPT * rows), BF16)],
    )(fields, p_pair, conductivity, c_pair, receivers, hot_own)
    def paired(x, ready):
        x, ready = lax.optimization_barrier((x, ready))
        return x, send(x, swap)

    p_near, p_near_pair = paired(p_near, p_sample)
    c_near, c_near_pair = paired(c_near, p_sample)
    c_far, c_far_pair = paired(c_far, p_sample)
    p_far, p_far_pair = paired(p_far, (p_near_pair, c_near_pair, c_far_pair))
    kx, ky, kz, dinv, dg, prim, f0, f1, f2, sent = call(
        forward_kernel,
        20,
        [deep] * 5 + [pairs] * 4 + [f32(CHIPS, 8, count + 128)],
        [
            pltpu.VMEM((DEEP, rows, lanes), F32),
            pltpu.VMEM((6 * lanes, 3 * KEPT * rows), BF16),
            pltpu.VMEM((6, count), F32),
        ],
    )(
        p_mid, p_near, p_near_pair, p_far, p_far_pair,
        c_mid, c_near, c_near_pair, c_far, c_far_pair, ky_mid, kz_mid, dg_mid, receivers, hot_own, p_sample,
    )
    got = lax.all_to_all(sent, ("y", "xl"), 0, 0, tiled=True)
    six = (2, 6, rows, lanes)
    a0, a1, a2, pot, pred, sent = call(
        adjoint_kernel,
        18,
        [f32(*six)] * 4 + [f32(2, count), f32(CHIPS, 8, 128)],
        [pltpu.VMEM((3, 2 * lanes, count), BF16)] + [pltpu.VMEM((2, DEEP, rows, lanes), F32)] * 3,
    )(got, observed[0], receivers, hot, kx, ky, kz, dinv, dg, prim, f0, f1, f2)
    got = lax.all_to_all(sent, ("y", "xl"), 0, 0, tiled=True)
    slabs = lax.axis_size("z")
    chunks = (slabs, 6, rows // slabs, lanes)
    kept, given = call(gradient_kernel, 8, [f32(*chunks)] * 2, [pltpu.VMEM(six, F32)])(got, a0, a1, a2, pot)
    given, pred = lax.optimization_barrier((given, pred))
    total = kept + send(given, swap)
    pred_pair = send(pred, swap)
    even = lax.axis_index("c") == 0
    predicted = jnp.where(even, jnp.concatenate([pred, pred_pair]), jnp.concatenate([pred_pair, pred]))
    parts = lax.all_to_all(total, "z", 0, 0, tiled=True)
    share = jnp.sum(parts, axis=0, keepdims=True)
    if high_count > 1:
        share = share + lax.ppermute(share, "xh", [(0, 1), (1, 0)])
    spread = jnp.broadcast_to(share, chunks)
    whole = lax.all_to_all(spread, "z", 0, 0, tiled=True)
    grad = jnp.transpose(whole, (1, 0, 2, 3)).reshape(3, 2, rows, lanes)
    return grad, predicted[None]


def solution(mesh):
    groups = mesh.shape["src"]
    high = 2 if groups > 1 else 1
    devices = mesh.devices.reshape(groups // high, high, CHIPS // 2, 2, 2)
    inner = Mesh(devices, ("z", "xh", "y", "xl", "c"))
    src, dom = ("z", "xh"), ("y", "xl", "c")
    return jax.shard_map(
        functools.partial(per_device, high),
        mesh=inner,
        in_specs=(P(src, None, dom, None, None), P(None, dom, None, None), P(src, None, None), P(src, None)),
        out_specs=(P(None, dom, None, None), P(src, None, None)),
        check_vma=False,
    )
```

```python
import functools
import jax
import jax.numpy as jnp
from jax import lax
from jax.experimental import pallas as pl
from jax.experimental.pallas import tpu as pltpu
from jax.sharding import Mesh, PartitionSpec as P

F32 = jnp.float32
BF16 = jnp.bfloat16
MEBI = 1024 * 1024
DEEP = 12
KEPT = 4
CHIPS = 8
LANES = 128


def pieces_of(values):
    first = values.astype(BF16)
    rest = values - first.astype(F32)
    second = rest.astype(BF16)
    third = (rest - second.astype(F32)).astype(BF16)
    return first, second, third


def fold(plane):
    return jnp.sum(plane.reshape(plane.shape[0] // 8, 8, plane.shape[1]), axis=0)


def ahead(plane, axis):
    return pltpu.roll(plane, plane.shape[axis] - 1, axis)


def behind(plane, axis):
    return pltpu.roll(plane, 1, axis)


def neighbours(field, s, i, kx, ky, kz):
    mid = field[s, i]
    total = kx[i] * field[s, i + 1] + kx[i - 1] * field[s, i - 1]
    total = total + ky[i] * ahead(mid, 0) + behind(ky[i] * mid, 0)
    return total + kz[i] * ahead(mid, 1) + behind(kz[i] * mid, 1)


def krylov(t0, t1, t2, kx, ky, kz, dinv, dg):
    sources = t0.shape[0]

    def apply_planes(source, target, first, last):
        def body(i, carry):
            for s in range(sources):
                target[s, i] = source[s, i] - dinv[i] * neighbours(source, s, i, kx, ky, kz)
            return carry

        lax.fori_loop(first, last + 1, body, 0, unroll=True)

    apply_planes(t0, t1, 2, 9)
    apply_planes(t1, t2, 3, 8)

    def body(i, sums):
        sums = list(sums)
        for s in range(sources):
            a0, a1, a2 = t0[s, i], t1[s, i], t2[s, i]
            a3 = a2 - dinv[i] * neighbours(t2, s, i, kx, ky, kz)
            d = dg[i]
            b1 = a0 - a1
            b2 = b1 - (a1 - a2)
            b3 = b2 - ((a1 - a2) - (a2 - a3))
            d0, d1, d2, e1, e2 = d * a0, d * a1, d * a2, d * b1, d * b2
            terms = [
                d0 * a0, d0 * a1, d1 * a1, d1 * a2, d2 * a2, d2 * a3,
                d0 * b1, e1 * b1, e1 * b2, e2 * b2, e2 * b3,
            ]
            for k, term in enumerate(terms):
                sums[k * sources + s] = sums[k * sources + s] + fold(term)
        return tuple(sums)

    zero = jnp.zeros((8, t0.shape[3]), F32)
    sums = lax.fori_loop(4, 8, body, (zero,) * (11 * sources), unroll=True)
    row_at = lax.broadcasted_iota(jnp.int32, (8, 128), 0)
    lane_at = lax.broadcasted_iota(jnp.int32, (8, 128), 1)
    packed = jnp.zeros((8, 128), F32)
    for n, x in enumerate(sums):
        here = jnp.logical_and(row_at == n % sources, lane_at == n // sources)
        packed = jnp.where(here, jnp.sum(x), packed)
    return packed


def weights_of(moments):
    t = [moments[0:2, k : k + 1] for k in range(6)]
    m = [t[0]] + [moments[0:2, k : k + 1] for k in range(6, 11)]
    near = t[1] < 0.5 * t[0]
    g = [jnp.where(near, t[k + 1], m[k] - m[k + 1]) for k in range(5)]
    h = [jnp.where(near, t[k], m[k]) for k in range(3)]
    l1 = g[1] / g[0]
    l2 = g[2] / g[0]
    d1 = g[2] - l1 * g[1]
    e2 = g[3] - l2 * g[1]
    l21 = e2 / d1
    d2 = g[4] - l2 * g[2] - l21 * e2
    y1 = h[1] - l1 * h[0]
    y2 = h[2] - l2 * h[0] - l21 * y1
    c2 = y2 / d2
    c1 = y1 / d1 - l21 * c2
    c0 = h[0] / g[0] - l1 * c1 - l2 * c2
    w0 = jnp.where(near, c0, c0 + c1 + c2)
    w1 = jnp.where(near, c1, -(c1 + 2.0 * c2))
    return w0, w1, c2


def one_hot(count, first, picked):
    place = lax.broadcasted_iota(jnp.int32, (count, picked.shape[1]), 0) + first
    return place == picked


def edges(rows, lanes):
    row_at = lax.broadcasted_iota(jnp.int32, (rows, lanes), 0)
    lane_at = lax.broadcasted_iota(jnp.int32, (rows, lanes), 1)
    mask_y = jnp.where(row_at < rows - 1, 1.0, 0.0).astype(F32)
    mask_z = jnp.where(lane_at < lanes - 1, 1.0, 0.0).astype(F32)
    return row_at, lane_at, mask_y, mask_z


def in_plane(along_y, along_z):
    rows, lanes = along_y.shape
    row_at, lane_at, mask_y, mask_z = edges(rows, lanes)
    up_y = 0.5 * (along_y + ahead(along_y, 0)) * mask_y
    up_z = 0.5 * (along_z + ahead(along_z, 1)) * mask_z
    low_y = jnp.where(row_at == 0, 0.5 * along_y, behind(up_y, 0))
    low_z = jnp.where(lane_at == 0, 0.5 * along_z, behind(up_z, 1))
    top_y = jnp.where(row_at == rows - 1, 0.5 * along_y, up_y)
    top_z = jnp.where(lane_at == lanes - 1, 0.5 * along_z, up_z)
    return up_y, up_z, top_y + low_y + top_z + low_z


def hot_kernel(cells, hot, hot_own):
    block = 2 * lax.axis_index("y") + lax.axis_index("xl")
    rows = hot.shape[0] // 10
    row_of = cells[...] // LANES
    for i in range(10):
        rows_hot = one_hot(rows, (4 * block - 3 + i) * rows, row_of)
        rows_hot = jnp.where(rows_hot, 1.0, 0.0).astype(BF16)
        hot[pl.ds(i * rows, rows)] = rows_hot
        if 3 <= i < 7:
            for piece in range(3):
                hot_own[pl.ds((piece * KEPT + i - 3) * rows, rows)] = rows_hot


def own_kernel(p_own, p_pair, c_own, c_pair, cells, hot_own, prim, first, ky, kz, plane_dg, sample, left):
    core = lax.axis_index("c")
    here = pl.ds(2 * core, 2)
    other = pl.ds(2 - 2 * core, 2)
    prim[:, here] = p_own[here]
    prim[:, other] = p_pair[here]
    first[here] = c_own[0]
    first[other] = c_pair[0]
    rows, lanes = prim.shape[2], prim.shape[3]
    for source, base in ((c_own, 2 * core), (c_pair, 2 - 2 * core)):
        for j in range(2):
            up_y, up_z, part = in_plane(source[1, j], source[2, j])
            ky[base + j] = up_y
            kz[base + j] = up_z
            plane_dg[base + j] = part
    picked = cells[...]
    lane_of = picked - (picked // lanes) * lanes
    gather([(prim, 0)], left, hot_own, one_hot(lanes, 0, lane_of), sample)


def gather(fields, left, hot_own, lane_hot, sample):
    lanes = lane_hot.shape[0]
    for f, (field, first) in enumerate(fields):
        rows = field.shape[2]
        for s in range(2):
            for j in range(KEPT):
                parts = pieces_of(jnp.transpose(field[s, first + j]))
                for k in range(3):
                    start = (k * KEPT + j) * rows
                    left[pl.ds((2 * f + s) * lanes, lanes), start : start + rows] = parts[k]
    spread = jnp.dot(left[...], hot_own[...], preferred_element_type=F32)
    found = [
        jnp.sum(jnp.where(lane_hot, spread[k * lanes : (k + 1) * lanes], 0.0), axis=0, keepdims=True)
        for k in range(2 * len(fields))
    ]
    sample[...] = jnp.concatenate(found, axis=0)


def forward_kernel(
    p_mid, p_near, p_near_pair, p_far, p_far_pair,
    c_mid, c_near, c_near_pair, c_far, c_far_pair, ky_mid, kz_mid, dg_mid, cells, hot_own, p_sample,
    kx, ky, kz, dinv, dg, prim, t0, t1, t2, sent, cond, left, found,
):
    block = 2 * lax.axis_index("y") + lax.axis_index("xl")
    core = lax.axis_index("c")
    here = pl.ds(2 * core, 2)
    prim[:, 4:8] = p_mid[...]
    cond[4:8] = c_mid[...]
    far = 8 * lax.axis_index("xl")
    near = 8 - far
    for base, first, second in ((near, p_near, p_near_pair), (far, p_far, p_far_pair)):
        prim[:, pl.ds(base + 2 * core, 2)] = first[here]
        prim[:, pl.ds(base + 2 - 2 * core, 2)] = second[here]
    for base, first, second in ((near, c_near, c_near_pair), (far, c_far, c_far_pair)):
        cond[pl.ds(base + 2 * core, 2)] = first[0]
        cond[pl.ds(base + 2 - 2 * core, 2)] = second[0]
        for source, start in ((first, base + 2 * core), (second, base + 2 - 2 * core)):
            for j in range(2):
                up_y, up_z, part = in_plane(source[1, j], source[2, j])
                ky[start + j] = up_y
                kz[start + j] = up_z
                dg[start + j] = part
    ky[4:8] = ky_mid[...]
    kz[4:8] = kz_mid[...]
    dg[4:8] = dg_mid[...]
    rows, lanes = prim.shape[2], prim.shape[3]
    row_at, lane_at, mask_y, mask_z = edges(rows, lanes)
    edge = jnp.where(row_at == 0, 0.5, 0.0) + jnp.where(row_at == rows - 1, 0.5, 0.0)
    edge = edge + jnp.where(lane_at == 0, 0.5, 0.0) + jnp.where(lane_at == lanes - 1, 0.5, 0.0)
    unit = (6.0 - edge).astype(F32)
    layers = 4 * CHIPS

    kx[0] = 0.5 * (cond[0] + cond[1])

    def coefficients(i, carry):
        layer = 4 * block - 4 + i
        inside = jnp.where(jnp.logical_and(layer >= 0, layer < layers), 1.0, 0.0).astype(F32)
        first = 0.5 * (cond[i] + cond[i + 1])
        kx[i] = first
        diagonal = first + kx[i - 1] + dg[i]
        inverse = jnp.where(inside > 0.5, 1.0 / diagonal, 0.0)
        dg[i] = diagonal
        dinv[i] = inverse
        return carry

    lax.fori_loop(1, 11, coefficients, 0)

    def right_side(i, carry):
        layer = 4 * block - 4 + i
        outer = jnp.where(jnp.logical_or(layer == 0, layer == layers - 1), 0.5, 0.0).astype(F32)
        diagonal = (unit - outer) - dg[i]
        upper, lower = 1.0 - kx[i], 1.0 - kx[i - 1]
        diff_y = mask_y - ky[i]
        diff_z = mask_z - kz[i]
        inverse = dinv[i]
        for s in range(2):
            mid = prim[s, i]
            total = diagonal * mid - upper * prim[s, i + 1] - lower * prim[s, i - 1]
            total = total - diff_y * ahead(mid, 0) - behind(diff_y * mid, 0)
            total = total - diff_z * ahead(mid, 1) - behind(diff_z * mid, 1)
            t0[s, i] = inverse * total
        return carry

    lax.fori_loop(1, 11, right_side, 0, unroll=True)
    moments = krylov(t0, t1, t2, kx, ky, kz, dinv, dg)

    picked = cells[...]
    lane_of = picked - (picked // lanes) * lanes
    count = picked.shape[1]
    gather([(t0, 4), (t1, 4), (t2, 4)], left, hot_own, one_hot(lanes, 0, lane_of), found)
    for k in range(CHIPS):
        sent[k, 0:2, :count] = p_sample[...]
        sent[k, 2:8, :count] = found[...]
        sent[k, :, count:] = moments


def adjoint_kernel(
    got, observed, cells, hot, kx, ky, kz, dinv, dg, prim, f0, f1, f2,
    b0, b1, b2, pot, predicted, sent, heavy, a0, a1, a2,
):
    core = lax.axis_index("c")
    rows, lanes = prim.shape[2], prim.shape[3]
    count = cells.shape[1]
    total = got[0]
    for k in range(1, CHIPS):
        total = total + got[k]
    weights = weights_of(total[:, count:])
    sample = total[:, :count]
    value = sample[0:2]
    for k in range(3):
        value = value + weights[k] * sample[2 * k + 2 : 2 * k + 4]
    predicted[...] = value
    seen = jnp.where(core == 0, observed[0:2], observed[2:4])
    misfit = value - seen
    for i in range(6):
        for s in range(2):
            w = [weights[k][s : s + 1, :] for k in range(3)]
            pot[s, i] = prim[s, i + 3] + w[0] * f0[s, i + 3] + w[1] * f1[s, i + 3] + w[2] * f2[s, i + 3]

    picked = cells[...]
    lane_of = picked - (picked // lanes) * lanes
    lane_hot = one_hot(lanes, 0, lane_of)
    for s in range(2):
        spread = jnp.where(lane_hot, misfit[s : s + 1], 0.0)
        for k, piece in enumerate(pieces_of(spread)):
            heavy[k, pl.ds(s * lanes, lanes)] = piece
    placed = [
        lax.dot_general(hot[...], heavy[k], (((1,), (1,)), ((), ())), preferred_element_type=F32)
        for k in range(3)
    ]
    source = placed[0] + placed[1] + placed[2]
    for i in range(10):
        inverse = dinv[i + 1]
        for s in range(2):
            a0[s, i + 1] = inverse * source[i * rows : (i + 1) * rows, s * lanes : (s + 1) * lanes]
    moments = krylov(a0, a1, a2, kx, ky, kz, dinv, dg)
    for k in range(CHIPS):
        sent[k] = moments
    for near, deep in ((b0, a0), (b1, a1), (b2, a2)):
        near[...] = deep[:, 3:9]


def gradient_kernel(got, a0, a1, a2, pot, kept, given, adj):
    core = lax.axis_index("c")
    moments = got[0]
    for k in range(1, CHIPS):
        moments = moments + got[k]
    weights = weights_of(moments)
    rows, lanes = pot.shape[2], pot.shape[3]
    row_at = lax.broadcasted_iota(jnp.int32, (rows, lanes), 0)
    lane_at = lax.broadcasted_iota(jnp.int32, (rows, lanes), 1)
    for i in range(6):
        for s in range(2):
            w = [weights[k][s : s + 1, :] for k in range(3)]
            adj[s, i] = w[0] * a0[s, i] + w[1] * a1[s, i] + w[2] * a2[s, i]

    def along(mid_p, mid_a, axis, at):
        last = mid_p.shape[axis] - 1
        next_p = jnp.where(at == last, 0.0, ahead(mid_p, axis))
        next_a = jnp.where(at == last, 0.0, ahead(mid_a, axis))
        upper = (mid_p - next_p) * (mid_a - next_a)
        lower = jnp.where(at == 0, mid_p * mid_a, behind(upper, axis))
        return upper + lower

    for target, first in ((given, 1 + 2 * (1 - core)), (kept, 1 + 2 * core)):
        for j in range(2):
            i = first + j
            sums = [0.0, 0.0, 0.0]
            for s in range(2):
                mid_p, mid_a = pot[s, i], adj[s, i]
                upper = (mid_p - pot[s, i + 1]) * (mid_a - adj[s, i + 1])
                lower = (mid_p - pot[s, i - 1]) * (mid_a - adj[s, i - 1])
                sums[0] = sums[0] + upper + lower
                sums[1] = sums[1] + along(mid_p, mid_a, 0, row_at)
                sums[2] = sums[2] + along(mid_p, mid_a, 1, lane_at)
            for k in range(3):
                target[:, 2 * k + j] = (-0.5 * sums[k]).reshape(target.shape[0], target.shape[2], lanes)


def call(kernel, limit, outs, scratch=()):
    vmem = pl.BlockSpec(memory_space=pltpu.VMEM)

    def run(*args):
        return pl.pallas_call(
            kernel,
            out_shape=tuple(jax.ShapeDtypeStruct(x, kind) for x, kind in outs),
            in_specs=[vmem] * len(args),
            out_specs=tuple([vmem] * len(outs)),
            scratch_shapes=list(scratch),
            compiler_params=pltpu.CompilerParams(vmem_limit_bytes=limit * MEBI),
        )(*args)

    return run


NAMES = ("xh", "y", "xl", "c")


def routes(sizes, move):
    pairs = []
    nx, ny = sizes
    index = lambda h, y, l, c: ((h * ny + y) * 2 + l) * 2 + c
    for h in range(nx):
        for y in range(ny):
            for l in range(2):
                for c in range(2):
                    target = move(h, y, l, c)
                    if target is not None:
                        pairs.append((index(h, y, l, c), index(*target)))
    return pairs


def per_device(high_count, primary, conductivity, observed, receivers):
    chain = CHIPS // 2
    sizes = (high_count, chain)
    def beside(h, y, l, c):
        return (h, y, 1 - l, c)

    def around(h, y, l, c):
        side = (2 * h + l + (1 if l == 1 else -1)) % (2 * high_count)
        return (side // 2, y, side % 2, c)

    def along(sign):
        def move(h, y, l, c):
            target = y + sign * (1 if l == 0 else -1)
            return (h, target, l, c) if 0 <= target < chain else None

        return routes(sizes, move)

    def send(x, pairs):
        return lax.ppermute(x, NAMES, pairs)

    fields = primary[0]
    swap = routes(sizes, lambda h, y, l, c: (h, y, l, 1 - c))
    p_near = send(fields, routes(sizes, beside))
    c_near = send(conductivity, routes(sizes, around))
    c_next = send(conductivity, along(-1))
    p_near, c_near = lax.optimization_barrier((p_near, c_near))
    p_far = send(p_near, along(1))
    c_far = send(c_next, routes(sizes, beside))

    rows, lanes = primary.shape[3], primary.shape[4]
    count = receivers.shape[1]
    f32 = lambda *shape: (shape, F32)
    deep = f32(DEEP, rows, lanes)
    pairs = f32(2, DEEP, rows, lanes)
    four = f32(KEPT, rows, lanes)
    hot, hot_own = call(
        hot_kernel, 4, [((10 * rows, count), BF16), ((3 * KEPT * rows, count), BF16)]
    )(receivers)
    own_c, p_pair = lax.optimization_barrier((conductivity, send(fields, swap)))
    c_pair = send(own_c, swap)
    p_near_pair, c_near_pair = send(p_near, swap), send(c_near, swap)
    hot_own, c_near_pair = lax.optimization_barrier((hot_own, c_near_pair))
    p_mid, c_mid, ky_mid, kz_mid, dg_mid, p_sample = call(
        own_kernel,
        8,
        [f32(2, KEPT, rows, lanes), four, four, four, four, f32(2, count)],
        [pltpu.VMEM((2 * lanes, 3 * KEPT * rows), BF16)],
    )(fields, p_pair, conductivity, c_pair, receivers, hot_own)
    p_far, ready = lax.optimization_barrier((p_far, p_sample))
    p_far_pair, c_far_pair = send(p_far, swap), send(c_far, swap)
    kx, ky, kz, dinv, dg, prim, f0, f1, f2, sent = call(
        forward_kernel,
        20,
        [deep] * 5 + [pairs] * 4 + [f32(CHIPS, 8, count + 128)],
        [
            pltpu.VMEM((DEEP, rows, lanes), F32),
            pltpu.VMEM((6 * lanes, 3 * KEPT * rows), BF16),
            pltpu.VMEM((6, count), F32),
        ],
    )(
        p_mid, p_near, p_near_pair, p_far, p_far_pair,
        c_mid, c_near, c_near_pair, c_far, c_far_pair, ky_mid, kz_mid, dg_mid, receivers, hot_own, p_sample,
    )
    got = lax.all_to_all(sent, ("y", "xl"), 0, 0, tiled=True)
    six = (2, 6, rows, lanes)
    a0, a1, a2, pot, pred, sent = call(
        adjoint_kernel,
        18,
        [f32(*six)] * 4 + [f32(2, count), f32(CHIPS, 8, 128)],
        [pltpu.VMEM((3, 2 * lanes, count), BF16)] + [pltpu.VMEM((2, DEEP, rows, lanes), F32)] * 3,
    )(got, observed[0], receivers, hot, kx, ky, kz, dinv, dg, prim, f0, f1, f2)
    got = lax.all_to_all(sent, ("y", "xl"), 0, 0, tiled=True)
    slabs = lax.axis_size("z")
    chunks = (slabs, 6, rows // slabs, lanes)
    kept, given = call(gradient_kernel, 8, [f32(*chunks)] * 2, [pltpu.VMEM(six, F32)])(got, a0, a1, a2, pot)
    given, pred = lax.optimization_barrier((given, pred))
    total = kept + send(given, swap)
    pred_pair = send(pred, swap)
    even = lax.axis_index("c") == 0
    predicted = jnp.where(even, jnp.concatenate([pred, pred_pair]), jnp.concatenate([pred_pair, pred]))
    parts = lax.all_to_all(total, "z", 0, 0, tiled=True)
    share = jnp.sum(parts, axis=0, keepdims=True)
    if high_count > 1:
        share = share + lax.ppermute(share, "xh", [(0, 1), (1, 0)])
    spread = jnp.broadcast_to(share, chunks)
    whole = lax.all_to_all(spread, "z", 0, 0, tiled=True)
    grad = jnp.transpose(whole, (1, 0, 2, 3)).reshape(3, 2, rows, lanes)
    return grad, predicted[None]


def solution(mesh):
    groups = mesh.shape["src"]
    high = 2 if groups > 1 else 1
    devices = mesh.devices.reshape(groups // high, high, CHIPS // 2, 2, 2)
    inner = Mesh(devices, ("z", "xh", "y", "xl", "c"))
    src, dom = ("z", "xh"), ("y", "xl", "c")
    return jax.shard_map(
        functools.partial(per_device, high),
        mesh=inner,
        in_specs=(P(src, None, dom, None, None), P(None, dom, None, None), P(src, None, None), P(src, None)),
        out_specs=(P(None, dom, None, None), P(src, None, None)),
        check_vma=False,
    )
```

```python
import functools
import jax
import jax.numpy as jnp
from jax import lax
from jax.experimental import pallas as pl
from jax.experimental.pallas import tpu as pltpu
from jax.sharding import Mesh, PartitionSpec as P

F32 = jnp.float32
BF16 = jnp.bfloat16
MEBI = 1024 * 1024
DEEP = 12
KEPT = 4
CHIPS = 8
LANES = 128


def pieces_of(values):
    first = values.astype(BF16)
    rest = values - first.astype(F32)
    second = rest.astype(BF16)
    third = (rest - second.astype(F32)).astype(BF16)
    return first, second, third


def fold(plane):
    return jnp.sum(plane.reshape(plane.shape[0] // 8, 8, plane.shape[1]), axis=0)


def ahead(plane, axis):
    return pltpu.roll(plane, plane.shape[axis] - 1, axis)


def behind(plane, axis):
    return pltpu.roll(plane, 1, axis)


def neighbours(field, s, i, kx, ky, kz):
    mid = field[s, i]
    total = kx[i] * field[s, i + 1] + kx[i - 1] * field[s, i - 1]
    total = total + ky[i] * ahead(mid, 0) + behind(ky[i] * mid, 0)
    return total + kz[i] * ahead(mid, 1) + behind(kz[i] * mid, 1)


def krylov(t0, t1, t2, kx, ky, kz, dinv, dg):
    sources = t0.shape[0]

    def apply_planes(source, target, first, last):
        def body(i, carry):
            for s in range(sources):
                target[s, i] = source[s, i] - dinv[i] * neighbours(source, s, i, kx, ky, kz)
            return carry

        lax.fori_loop(first, last + 1, body, 0, unroll=True)

    apply_planes(t0, t1, 2, 9)
    apply_planes(t1, t2, 3, 8)

    def body(i, sums):
        sums = list(sums)
        for s in range(sources):
            a0, a1, a2 = t0[s, i], t1[s, i], t2[s, i]
            a3 = a2 - dinv[i] * neighbours(t2, s, i, kx, ky, kz)
            d = dg[i]
            b1 = a0 - a1
            b2 = b1 - (a1 - a2)
            b3 = b2 - ((a1 - a2) - (a2 - a3))
            d0, d1, d2, e1, e2 = d * a0, d * a1, d * a2, d * b1, d * b2
            terms = [
                d0 * a0, d0 * a1, d1 * a1, d1 * a2, d2 * a2, d2 * a3,
                d0 * b1, e1 * b1, e1 * b2, e2 * b2, e2 * b3,
            ]
            for k, term in enumerate(terms):
                sums[k * sources + s] = sums[k * sources + s] + fold(term)
        return tuple(sums)

    zero = jnp.zeros((8, t0.shape[3]), F32)
    sums = lax.fori_loop(4, 8, body, (zero,) * (11 * sources), unroll=True)
    row_at = lax.broadcasted_iota(jnp.int32, (8, 128), 0)
    lane_at = lax.broadcasted_iota(jnp.int32, (8, 128), 1)
    packed = jnp.zeros((8, 128), F32)
    for n, x in enumerate(sums):
        here = jnp.logical_and(row_at == n % sources, lane_at == n // sources)
        packed = jnp.where(here, jnp.sum(x), packed)
    return packed


def weights_of(moments):
    t = [moments[0:2, k : k + 1] for k in range(6)]
    m = [t[0]] + [moments[0:2, k : k + 1] for k in range(6, 11)]
    near = t[1] < 0.5 * t[0]
    g = [jnp.where(near, t[k + 1], m[k] - m[k + 1]) for k in range(5)]
    h = [jnp.where(near, t[k], m[k]) for k in range(3)]
    l1 = g[1] / g[0]
    l2 = g[2] / g[0]
    d1 = g[2] - l1 * g[1]
    e2 = g[3] - l2 * g[1]
    l21 = e2 / d1
    d2 = g[4] - l2 * g[2] - l21 * e2
    y1 = h[1] - l1 * h[0]
    y2 = h[2] - l2 * h[0] - l21 * y1
    c2 = y2 / d2
    c1 = y1 / d1 - l21 * c2
    c0 = h[0] / g[0] - l1 * c1 - l2 * c2
    w0 = jnp.where(near, c0, c0 + c1 + c2)
    w1 = jnp.where(near, c1, -(c1 + 2.0 * c2))
    return w0, w1, c2


def one_hot(count, first, picked):
    place = lax.broadcasted_iota(jnp.int32, (count, picked.shape[1]), 0) + first
    return place == picked


def edges(rows, lanes):
    row_at = lax.broadcasted_iota(jnp.int32, (rows, lanes), 0)
    lane_at = lax.broadcasted_iota(jnp.int32, (rows, lanes), 1)
    mask_y = jnp.where(row_at < rows - 1, 1.0, 0.0).astype(F32)
    mask_z = jnp.where(lane_at < lanes - 1, 1.0, 0.0).astype(F32)
    return row_at, lane_at, mask_y, mask_z


def in_plane(along_y, along_z):
    rows, lanes = along_y.shape
    row_at, lane_at, mask_y, mask_z = edges(rows, lanes)
    up_y = 0.5 * (along_y + ahead(along_y, 0)) * mask_y
    up_z = 0.5 * (along_z + ahead(along_z, 1)) * mask_z
    low_y = jnp.where(row_at == 0, 0.5 * along_y, behind(up_y, 0))
    low_z = jnp.where(lane_at == 0, 0.5 * along_z, behind(up_z, 1))
    top_y = jnp.where(row_at == rows - 1, 0.5 * along_y, up_y)
    top_z = jnp.where(lane_at == lanes - 1, 0.5 * along_z, up_z)
    return up_y, up_z, top_y + low_y + top_z + low_z


def hot_kernel(cells, hot, hot_own):
    block = 2 * lax.axis_index("y") + lax.axis_index("xl")
    rows = hot.shape[0] // 10
    row_of = cells[...] // LANES
    for i in range(10):
        rows_hot = one_hot(rows, (4 * block - 3 + i) * rows, row_of)
        rows_hot = jnp.where(rows_hot, 1.0, 0.0).astype(BF16)
        hot[pl.ds(i * rows, rows)] = rows_hot
        if 3 <= i < 7:
            for piece in range(3):
                hot_own[pl.ds((piece * KEPT + i - 3) * rows, rows)] = rows_hot


def own_kernel(p_own, p_pair, c_own, c_pair, cells, hot_own, prim, first, ky, kz, plane_dg, sample, left):
    core = lax.axis_index("c")
    here = pl.ds(2 * core, 2)
    other = pl.ds(2 - 2 * core, 2)
    prim[:, here] = p_own[here]
    prim[:, other] = p_pair[here]
    first[here] = c_own[0]
    first[other] = c_pair[0]
    rows, lanes = prim.shape[2], prim.shape[3]
    for source, base in ((c_own, 2 * core), (c_pair, 2 - 2 * core)):
        for j in range(2):
            up_y, up_z, part = in_plane(source[1, j], source[2, j])
            ky[base + j] = up_y
            kz[base + j] = up_z
            plane_dg[base + j] = part
    picked = cells[...]
    lane_of = picked - (picked // lanes) * lanes
    gather([(prim, 0)], left, hot_own, one_hot(lanes, 0, lane_of), sample)


def gather(fields, left, hot_own, lane_hot, sample):
    lanes = lane_hot.shape[0]
    for f, (field, first) in enumerate(fields):
        rows = field.shape[2]
        for s in range(2):
            for j in range(KEPT):
                parts = pieces_of(jnp.transpose(field[s, first + j]))
                for k in range(3):
                    start = (k * KEPT + j) * rows
                    left[pl.ds((2 * f + s) * lanes, lanes), start : start + rows] = parts[k]
    spread = jnp.dot(left[...], hot_own[...], preferred_element_type=F32)
    found = [
        jnp.sum(jnp.where(lane_hot, spread[k * lanes : (k + 1) * lanes], 0.0), axis=0, keepdims=True)
        for k in range(2 * len(fields))
    ]
    sample[...] = jnp.concatenate(found, axis=0)


def forward_kernel(
    p_mid, p_near, p_near_b, p_near_pair, p_near_pair_b, p_far, p_far_b, p_far_pair, p_far_pair_b,
    c_mid, c_near, c_near_pair, c_far, c_far_pair, ky_mid, kz_mid, dg_mid, cells, hot_own, p_sample,
    kx, ky, kz, dinv, dg, prim, t0, t1, t2, sent, cond, left, found,
):
    block = 2 * lax.axis_index("y") + lax.axis_index("xl")
    core = lax.axis_index("c")
    prim[:, 4:8] = p_mid[...]
    cond[4:8] = c_mid[...]
    far = 8 * lax.axis_index("xl")
    near = 8 - far
    for start, even, odd in (
        (near + 2 * core, p_near, p_near_b),
        (near + 2 - 2 * core, p_near_pair, p_near_pair_b),
        (far + 2 * core, p_far, p_far_b),
        (far + 2 - 2 * core, p_far_pair, p_far_pair_b),
    ):
        prim[:, pl.ds(start, 2)] = jnp.where(core == 0, even[...], odd[...])
    for base, first, second in ((near, c_near, c_near_pair), (far, c_far, c_far_pair)):
        cond[pl.ds(base + 2 * core, 2)] = first[0]
        cond[pl.ds(base + 2 - 2 * core, 2)] = second[0]
        for source, start in ((first, base + 2 * core), (second, base + 2 - 2 * core)):
            for j in range(2):
                up_y, up_z, part = in_plane(source[1, j], source[2, j])
                ky[start + j] = up_y
                kz[start + j] = up_z
                dg[start + j] = part
    ky[4:8] = ky_mid[...]
    kz[4:8] = kz_mid[...]
    dg[4:8] = dg_mid[...]
    rows, lanes = prim.shape[2], prim.shape[3]
    row_at, lane_at, mask_y, mask_z = edges(rows, lanes)
    edge = jnp.where(row_at == 0, 0.5, 0.0) + jnp.where(row_at == rows - 1, 0.5, 0.0)
    edge = edge + jnp.where(lane_at == 0, 0.5, 0.0) + jnp.where(lane_at == lanes - 1, 0.5, 0.0)
    unit = (6.0 - edge).astype(F32)
    layers = 4 * CHIPS

    kx[0] = 0.5 * (cond[0] + cond[1])

    def coefficients(i, carry):
        layer = 4 * block - 4 + i
        inside = jnp.where(jnp.logical_and(layer >= 0, layer < layers), 1.0, 0.0).astype(F32)
        first = 0.5 * (cond[i] + cond[i + 1])
        kx[i] = first
        diagonal = first + kx[i - 1] + dg[i]
        inverse = jnp.where(inside > 0.5, 1.0 / diagonal, 0.0)
        dg[i] = diagonal
        dinv[i] = inverse
        return carry

    lax.fori_loop(1, 11, coefficients, 0)

    def right_side(i, carry):
        layer = 4 * block - 4 + i
        outer = jnp.where(jnp.logical_or(layer == 0, layer == layers - 1), 0.5, 0.0).astype(F32)
        diagonal = (unit - outer) - dg[i]
        upper, lower = 1.0 - kx[i], 1.0 - kx[i - 1]
        diff_y = mask_y - ky[i]
        diff_z = mask_z - kz[i]
        inverse = dinv[i]
        for s in range(2):
            mid = prim[s, i]
            total = diagonal * mid - upper * prim[s, i + 1] - lower * prim[s, i - 1]
            total = total - diff_y * ahead(mid, 0) - behind(diff_y * mid, 0)
            total = total - diff_z * ahead(mid, 1) - behind(diff_z * mid, 1)
            t0[s, i] = inverse * total
        return carry

    lax.fori_loop(1, 11, right_side, 0, unroll=True)
    moments = krylov(t0, t1, t2, kx, ky, kz, dinv, dg)

    picked = cells[...]
    lane_of = picked - (picked // lanes) * lanes
    count = picked.shape[1]
    gather([(t0, 4), (t1, 4), (t2, 4)], left, hot_own, one_hot(lanes, 0, lane_of), found)
    for k in range(CHIPS):
        sent[k, 0:2, :count] = p_sample[...]
        sent[k, 2:8, :count] = found[...]
        sent[k, :, count:] = moments


def adjoint_kernel(
    got, observed, cells, hot, kx, ky, kz, dinv, dg, prim, f0, f1, f2,
    b0, b1, b2, pot, predicted, sent, heavy, a0, a1, a2,
):
    core = lax.axis_index("c")
    rows, lanes = prim.shape[2], prim.shape[3]
    count = cells.shape[1]
    total = got[0]
    for k in range(1, CHIPS):
        total = total + got[k]
    weights = weights_of(total[:, count:])
    sample = total[:, :count]
    value = sample[0:2]
    for k in range(3):
        value = value + weights[k] * sample[2 * k + 2 : 2 * k + 4]
    predicted[...] = value
    seen = jnp.where(core == 0, observed[0:2], observed[2:4])
    misfit = value - seen
    for i in range(6):
        for s in range(2):
            w = [weights[k][s : s + 1, :] for k in range(3)]
            pot[s, i] = prim[s, i + 3] + w[0] * f0[s, i + 3] + w[1] * f1[s, i + 3] + w[2] * f2[s, i + 3]

    picked = cells[...]
    lane_of = picked - (picked // lanes) * lanes
    lane_hot = one_hot(lanes, 0, lane_of)
    for s in range(2):
        spread = jnp.where(lane_hot, misfit[s : s + 1], 0.0)
        for k, piece in enumerate(pieces_of(spread)):
            heavy[k, pl.ds(s * lanes, lanes)] = piece
    placed = [
        lax.dot_general(hot[...], heavy[k], (((1,), (1,)), ((), ())), preferred_element_type=F32)
        for k in range(3)
    ]
    source = placed[0] + placed[1] + placed[2]
    for i in range(10):
        inverse = dinv[i + 1]
        for s in range(2):
            a0[s, i + 1] = inverse * source[i * rows : (i + 1) * rows, s * lanes : (s + 1) * lanes]
    moments = krylov(a0, a1, a2, kx, ky, kz, dinv, dg)
    for k in range(CHIPS):
        sent[k] = moments
    for near, deep in ((b0, a0), (b1, a1), (b2, a2)):
        near[...] = deep[:, 3:9]


def gradient_kernel(got, a0, a1, a2, pot, kept, given, adj):
    core = lax.axis_index("c")
    moments = got[0]
    for k in range(1, CHIPS):
        moments = moments + got[k]
    weights = weights_of(moments)
    rows, lanes = pot.shape[2], pot.shape[3]
    row_at = lax.broadcasted_iota(jnp.int32, (rows, lanes), 0)
    lane_at = lax.broadcasted_iota(jnp.int32, (rows, lanes), 1)
    for i in range(6):
        for s in range(2):
            w = [weights[k][s : s + 1, :] for k in range(3)]
            adj[s, i] = w[0] * a0[s, i] + w[1] * a1[s, i] + w[2] * a2[s, i]

    def along(mid_p, mid_a, axis, at):
        last = mid_p.shape[axis] - 1
        next_p = jnp.where(at == last, 0.0, ahead(mid_p, axis))
        next_a = jnp.where(at == last, 0.0, ahead(mid_a, axis))
        upper = (mid_p - next_p) * (mid_a - next_a)
        lower = jnp.where(at == 0, mid_p * mid_a, behind(upper, axis))
        return upper + lower

    for target, first in ((given, 1 + 2 * (1 - core)), (kept, 1 + 2 * core)):
        for j in range(2):
            i = first + j
            sums = [0.0, 0.0, 0.0]
            for s in range(2):
                mid_p, mid_a = pot[s, i], adj[s, i]
                upper = (mid_p - pot[s, i + 1]) * (mid_a - adj[s, i + 1])
                lower = (mid_p - pot[s, i - 1]) * (mid_a - adj[s, i - 1])
                sums[0] = sums[0] + upper + lower
                sums[1] = sums[1] + along(mid_p, mid_a, 0, row_at)
                sums[2] = sums[2] + along(mid_p, mid_a, 1, lane_at)
            for k in range(3):
                target[:, 2 * k + j] = (-0.5 * sums[k]).reshape(target.shape[0], target.shape[2], lanes)


def call(kernel, limit, outs, scratch=()):
    vmem = pl.BlockSpec(memory_space=pltpu.VMEM)

    def run(*args):
        return pl.pallas_call(
            kernel,
            out_shape=tuple(jax.ShapeDtypeStruct(x, kind) for x, kind in outs),
            in_specs=[vmem] * len(args),
            out_specs=tuple([vmem] * len(outs)),
            scratch_shapes=list(scratch),
            compiler_params=pltpu.CompilerParams(vmem_limit_bytes=limit * MEBI),
        )(*args)

    return run


NAMES = ("xh", "y", "xl", "c")


def routes(sizes, move):
    pairs = []
    nx, ny = sizes
    index = lambda h, y, l, c: ((h * ny + y) * 2 + l) * 2 + c
    for h in range(nx):
        for y in range(ny):
            for l in range(2):
                for c in range(2):
                    target = move(h, y, l, c)
                    if target is not None:
                        pairs.append((index(h, y, l, c), index(*target)))
    return pairs


def per_device(high_count, primary, conductivity, observed, receivers):
    chain = CHIPS // 2
    sizes = (high_count, chain)
    def beside(h, y, l, c):
        return (h, y, 1 - l, c)

    def around(h, y, l, c):
        side = (2 * h + l + (1 if l == 1 else -1)) % (2 * high_count)
        return (side // 2, y, side % 2, c)

    def along(sign):
        def move(h, y, l, c):
            target = y + sign * (1 if l == 0 else -1)
            return (h, target, l, c) if 0 <= target < chain else None

        return routes(sizes, move)

    def send(x, pairs):
        return lax.ppermute(x, NAMES, pairs)

    fields = primary[0]
    swap = routes(sizes, lambda h, y, l, c: (h, y, l, 1 - c))
    halves = (fields[0:2], fields[2:4])
    into = [routes(sizes, lambda h, y, l, c, to=to: (h, y, l, to) if c == 1 - to else None) for to in (0, 1)]
    p_near = [send(x, routes(sizes, beside)) for x in halves]
    c_near = send(conductivity, routes(sizes, around))
    c_next = send(conductivity, along(-1))
    p_far = [send(x, along(1)) for x in p_near]
    c_far = send(c_next, routes(sizes, beside))

    rows, lanes = primary.shape[3], primary.shape[4]
    count = receivers.shape[1]
    f32 = lambda *shape: (shape, F32)
    deep = f32(DEEP, rows, lanes)
    pairs = f32(2, DEEP, rows, lanes)
    four = f32(KEPT, rows, lanes)
    hot, hot_own = call(
        hot_kernel, 4, [((10 * rows, count), BF16), ((3 * KEPT * rows, count), BF16)]
    )(receivers)
    own_c, p_pair = lax.optimization_barrier((conductivity, send(fields, swap)))
    c_pair = send(own_c, swap)
    p_near_pair = [send(x, pairs) for x, pairs in zip(p_near, into)]
    c_near_pair = send(c_near, swap)
    hot_own, c_near_pair = lax.optimization_barrier((hot_own, c_near_pair))
    p_mid, c_mid, ky_mid, kz_mid, dg_mid, p_sample = call(
        own_kernel,
        8,
        [f32(2, KEPT, rows, lanes), four, four, four, four, f32(2, count)],
        [pltpu.VMEM((2 * lanes, 3 * KEPT * rows), BF16)],
    )(fields, p_pair, conductivity, c_pair, receivers, hot_own)
    p_far[1], ready = lax.optimization_barrier((p_far[1], p_sample))
    p_far_pair = [send(x, pairs) for x, pairs in zip(p_far, into)]
    c_far_pair = send(c_far, swap)
    kx, ky, kz, dinv, dg, prim, f0, f1, f2, sent = call(
        forward_kernel,
        20,
        [deep] * 5 + [pairs] * 4 + [f32(CHIPS, 8, count + 128)],
        [
            pltpu.VMEM((DEEP, rows, lanes), F32),
            pltpu.VMEM((6 * lanes, 3 * KEPT * rows), BF16),
            pltpu.VMEM((6, count), F32),
        ],
    )(
        p_mid, *p_near, *p_near_pair, *p_far, *p_far_pair,
        c_mid, c_near, c_near_pair, c_far, c_far_pair, ky_mid, kz_mid, dg_mid, receivers, hot_own, p_sample,
    )
    got = lax.all_to_all(sent, ("y", "xl"), 0, 0, tiled=True)
    six = (2, 6, rows, lanes)
    a0, a1, a2, pot, pred, sent = call(
        adjoint_kernel,
        18,
        [f32(*six)] * 4 + [f32(2, count), f32(CHIPS, 8, 128)],
        [pltpu.VMEM((3, 2 * lanes, count), BF16)] + [pltpu.VMEM((2, DEEP, rows, lanes), F32)] * 3,
    )(got, observed[0], receivers, hot, kx, ky, kz, dinv, dg, prim, f0, f1, f2)
    got = lax.all_to_all(sent, ("y", "xl"), 0, 0, tiled=True)
    slabs = lax.axis_size("z")
    chunks = (slabs, 6, rows // slabs, lanes)
    kept, given = call(gradient_kernel, 8, [f32(*chunks)] * 2, [pltpu.VMEM(six, F32)])(got, a0, a1, a2, pot)
    given, pred = lax.optimization_barrier((given, pred))
    total = kept + send(given, swap)
    pred_pair = send(pred, swap)
    even = lax.axis_index("c") == 0
    predicted = jnp.where(even, jnp.concatenate([pred, pred_pair]), jnp.concatenate([pred_pair, pred]))
    parts = lax.all_to_all(total, "z", 0, 0, tiled=True)
    share = jnp.sum(parts, axis=0, keepdims=True)
    if high_count > 1:
        share = share + lax.ppermute(share, "xh", [(0, 1), (1, 0)])
    spread = jnp.broadcast_to(share, chunks)
    whole = lax.all_to_all(spread, "z", 0, 0, tiled=True)
    grad = jnp.transpose(whole, (1, 0, 2, 3)).reshape(3, 2, rows, lanes)
    return grad, predicted[None]


def solution(mesh):
    groups = mesh.shape["src"]
    high = 2 if groups > 1 else 1
    devices = mesh.devices.reshape(groups // high, high, CHIPS // 2, 2, 2)
    inner = Mesh(devices, ("z", "xh", "y", "xl", "c"))
    src, dom = ("z", "xh"), ("y", "xl", "c")
    return jax.shard_map(
        functools.partial(per_device, high),
        mesh=inner,
        in_specs=(P(src, None, dom, None, None), P(None, dom, None, None), P(src, None, None), P(src, None)),
        out_specs=(P(None, dom, None, None), P(src, None, None)),
        check_vma=False,
    )
```

```python
import functools
import jax
import jax.numpy as jnp
from jax import lax
from jax.experimental import pallas as pl
from jax.experimental.pallas import tpu as pltpu
from jax.sharding import Mesh, PartitionSpec as P

F32 = jnp.float32
BF16 = jnp.bfloat16
MEBI = 1024 * 1024
DEEP = 12
KEPT = 4
CHIPS = 8
LANES = 128


def pieces_of(values):
    first = values.astype(BF16)
    rest = values - first.astype(F32)
    second = rest.astype(BF16)
    third = (rest - second.astype(F32)).astype(BF16)
    return first, second, third


def fold(plane):
    return jnp.sum(plane.reshape(plane.shape[0] // 8, 8, plane.shape[1]), axis=0)


def ahead(plane, axis):
    return pltpu.roll(plane, plane.shape[axis] - 1, axis)


def behind(plane, axis):
    return pltpu.roll(plane, 1, axis)


def neighbours(field, s, i, kx, ky, kz):
    mid = field[s, i]
    total = kx[i] * field[s, i + 1] + kx[i - 1] * field[s, i - 1]
    total = total + ky[i] * ahead(mid, 0) + behind(ky[i] * mid, 0)
    return total + kz[i] * ahead(mid, 1) + behind(kz[i] * mid, 1)


def krylov(t0, t1, t2, kx, ky, kz, dinv, dg):
    sources = t0.shape[0]

    def apply_planes(source, target, first, last):
        def body(i, carry):
            for s in range(sources):
                target[s, i] = source[s, i] - dinv[i] * neighbours(source, s, i, kx, ky, kz)
            return carry

        lax.fori_loop(first, last + 1, body, 0, unroll=True)

    apply_planes(t0, t1, 2, 9)
    apply_planes(t1, t2, 3, 8)

    def body(i, sums):
        sums = list(sums)
        for s in range(sources):
            a0, a1, a2 = t0[s, i], t1[s, i], t2[s, i]
            a3 = a2 - dinv[i] * neighbours(t2, s, i, kx, ky, kz)
            d = dg[i]
            b1 = a0 - a1
            b2 = b1 - (a1 - a2)
            b3 = b2 - ((a1 - a2) - (a2 - a3))
            d0, d1, d2, e1, e2 = d * a0, d * a1, d * a2, d * b1, d * b2
            terms = [
                d0 * a0, d0 * a1, d1 * a1, d1 * a2, d2 * a2, d2 * a3,
                d0 * b1, e1 * b1, e1 * b2, e2 * b2, e2 * b3,
            ]
            for k, term in enumerate(terms):
                sums[k * sources + s] = sums[k * sources + s] + fold(term)
        return tuple(sums)

    zero = jnp.zeros((8, t0.shape[3]), F32)
    sums = lax.fori_loop(4, 8, body, (zero,) * (11 * sources), unroll=True)
    row_at = lax.broadcasted_iota(jnp.int32, (8, 128), 0)
    lane_at = lax.broadcasted_iota(jnp.int32, (8, 128), 1)
    packed = jnp.zeros((8, 128), F32)
    for n, x in enumerate(sums):
        here = jnp.logical_and(row_at == n % sources, lane_at == n // sources)
        packed = jnp.where(here, jnp.sum(x), packed)
    return packed


def weights_of(moments):
    t = [moments[0:2, k : k + 1] for k in range(6)]
    m = [t[0]] + [moments[0:2, k : k + 1] for k in range(6, 11)]
    near = t[1] < 0.5 * t[0]
    g = [jnp.where(near, t[k + 1], m[k] - m[k + 1]) for k in range(5)]
    h = [jnp.where(near, t[k], m[k]) for k in range(3)]
    l1 = g[1] / g[0]
    l2 = g[2] / g[0]
    d1 = g[2] - l1 * g[1]
    e2 = g[3] - l2 * g[1]
    l21 = e2 / d1
    d2 = g[4] - l2 * g[2] - l21 * e2
    y1 = h[1] - l1 * h[0]
    y2 = h[2] - l2 * h[0] - l21 * y1
    c2 = y2 / d2
    c1 = y1 / d1 - l21 * c2
    c0 = h[0] / g[0] - l1 * c1 - l2 * c2
    w0 = jnp.where(near, c0, c0 + c1 + c2)
    w1 = jnp.where(near, c1, -(c1 + 2.0 * c2))
    return w0, w1, c2


def one_hot(count, first, picked):
    place = lax.broadcasted_iota(jnp.int32, (count, picked.shape[1]), 0) + first
    return place == picked


def edges(rows, lanes):
    row_at = lax.broadcasted_iota(jnp.int32, (rows, lanes), 0)
    lane_at = lax.broadcasted_iota(jnp.int32, (rows, lanes), 1)
    mask_y = jnp.where(row_at < rows - 1, 1.0, 0.0).astype(F32)
    mask_z = jnp.where(lane_at < lanes - 1, 1.0, 0.0).astype(F32)
    return row_at, lane_at, mask_y, mask_z


def in_plane(along_y, along_z):
    rows, lanes = along_y.shape
    row_at, lane_at, mask_y, mask_z = edges(rows, lanes)
    up_y = 0.5 * (along_y + ahead(along_y, 0)) * mask_y
    up_z = 0.5 * (along_z + ahead(along_z, 1)) * mask_z
    low_y = jnp.where(row_at == 0, 0.5 * along_y, behind(up_y, 0))
    low_z = jnp.where(lane_at == 0, 0.5 * along_z, behind(up_z, 1))
    top_y = jnp.where(row_at == rows - 1, 0.5 * along_y, up_y)
    top_z = jnp.where(lane_at == lanes - 1, 0.5 * along_z, up_z)
    return up_y, up_z, top_y + low_y + top_z + low_z


def hot_kernel(cells, hot, hot_own):
    block = 2 * lax.axis_index("y") + lax.axis_index("xl")
    rows = hot.shape[0] // 10
    row_of = cells[...] // LANES
    for i in range(10):
        rows_hot = one_hot(rows, (4 * block - 3 + i) * rows, row_of)
        rows_hot = jnp.where(rows_hot, 1.0, 0.0).astype(BF16)
        hot[pl.ds(i * rows, rows)] = rows_hot
        if 3 <= i < 7:
            for piece in range(3):
                hot_own[pl.ds((piece * KEPT + i - 3) * rows, rows)] = rows_hot


def own_kernel(p_own, p_pair, c_own, c_pair, cells, hot_own, prim, first, ky, kz, plane_dg, sample, left):
    core = lax.axis_index("c")
    here = pl.ds(2 * core, 2)
    other = pl.ds(2 - 2 * core, 2)
    prim[:, here] = p_own[here]
    prim[:, other] = p_pair[here]
    first[here] = c_own[0]
    first[other] = c_pair[0]
    rows, lanes = prim.shape[2], prim.shape[3]
    for source, base in ((c_own, 2 * core), (c_pair, 2 - 2 * core)):
        for j in range(2):
            up_y, up_z, part = in_plane(source[1, j], source[2, j])
            ky[base + j] = up_y
            kz[base + j] = up_z
            plane_dg[base + j] = part
    picked = cells[...]
    lane_of = picked - (picked // lanes) * lanes
    gather([(prim, 0)], left, hot_own, one_hot(lanes, 0, lane_of), sample)


def gather(fields, left, hot_own, lane_hot, sample):
    lanes = lane_hot.shape[0]
    for f, (field, first) in enumerate(fields):
        rows = field.shape[2]
        for s in range(2):
            for j in range(KEPT):
                parts = pieces_of(jnp.transpose(field[s, first + j]))
                for k in range(3):
                    start = (k * KEPT + j) * rows
                    left[pl.ds((2 * f + s) * lanes, lanes), start : start + rows] = parts[k]
    spread = jnp.dot(left[...], hot_own[...], preferred_element_type=F32)
    found = [
        jnp.sum(jnp.where(lane_hot, spread[k * lanes : (k + 1) * lanes], 0.0), axis=0, keepdims=True)
        for k in range(2 * len(fields))
    ]
    sample[...] = jnp.concatenate(found, axis=0)


def forward_kernel(
    p_mid, p_near, p_near_pair, p_far, p_far_pair,
    c_mid, c_near, c_near_pair, c_far, c_far_pair, ky_mid, kz_mid, dg_mid, cells, hot_own, p_sample,
    kx, ky, kz, dinv, dg, prim, t0, t1, t2, sent, cond, left, found,
):
    block = 2 * lax.axis_index("y") + lax.axis_index("xl")
    core = lax.axis_index("c")
    here = pl.ds(2 * core, 2)
    prim[:, 4:8] = p_mid[...]
    cond[4:8] = c_mid[...]
    far = 8 * lax.axis_index("xl")
    near = 8 - far
    for base, first, second in ((near, p_near, p_near_pair), (far, p_far, p_far_pair)):
        prim[:, pl.ds(base + 2 * core, 2)] = first[here]
        prim[:, pl.ds(base + 2 - 2 * core, 2)] = second[here]
    for base, first, second in ((near, c_near, c_near_pair), (far, c_far, c_far_pair)):
        cond[pl.ds(base + 2 * core, 2)] = first[0]
        cond[pl.ds(base + 2 - 2 * core, 2)] = second[0]
        for source, start in ((first, base + 2 * core), (second, base + 2 - 2 * core)):
            for j in range(2):
                up_y, up_z, part = in_plane(source[1, j], source[2, j])
                ky[start + j] = up_y
                kz[start + j] = up_z
                dg[start + j] = part
    ky[4:8] = ky_mid[...]
    kz[4:8] = kz_mid[...]
    dg[4:8] = dg_mid[...]
    rows, lanes = prim.shape[2], prim.shape[3]
    row_at, lane_at, mask_y, mask_z = edges(rows, lanes)
    edge = jnp.where(row_at == 0, 0.5, 0.0) + jnp.where(row_at == rows - 1, 0.5, 0.0)
    edge = edge + jnp.where(lane_at == 0, 0.5, 0.0) + jnp.where(lane_at == lanes - 1, 0.5, 0.0)
    unit = (6.0 - edge).astype(F32)
    layers = 4 * CHIPS

    kx[0] = 0.5 * (cond[0] + cond[1])

    def coefficients(i, carry):
        layer = 4 * block - 4 + i
        inside = jnp.where(jnp.logical_and(layer >= 0, layer < layers), 1.0, 0.0).astype(F32)
        first = 0.5 * (cond[i] + cond[i + 1])
        kx[i] = first
        diagonal = first + kx[i - 1] + dg[i]
        inverse = jnp.where(inside > 0.5, 1.0 / diagonal, 0.0)
        dg[i] = diagonal
        dinv[i] = inverse
        return carry

    lax.fori_loop(1, 11, coefficients, 0)

    def right_side(i, carry):
        layer = 4 * block - 4 + i
        outer = jnp.where(jnp.logical_or(layer == 0, layer == layers - 1), 0.5, 0.0).astype(F32)
        diagonal = (unit - outer) - dg[i]
        upper, lower = 1.0 - kx[i], 1.0 - kx[i - 1]
        diff_y = mask_y - ky[i]
        diff_z = mask_z - kz[i]
        inverse = dinv[i]
        for s in range(2):
            mid = prim[s, i]
            total = diagonal * mid - upper * prim[s, i + 1] - lower * prim[s, i - 1]
            total = total - diff_y * ahead(mid, 0) - behind(diff_y * mid, 0)
            total = total - diff_z * ahead(mid, 1) - behind(diff_z * mid, 1)
            t0[s, i] = inverse * total
        return carry

    lax.fori_loop(1, 11, right_side, 0, unroll=True)
    moments = krylov(t0, t1, t2, kx, ky, kz, dinv, dg)

    picked = cells[...]
    lane_of = picked - (picked // lanes) * lanes
    count = picked.shape[1]
    gather([(t0, 4), (t1, 4), (t2, 4)], left, hot_own, one_hot(lanes, 0, lane_of), found)
    for k in range(CHIPS):
        sent[k, 0:2, :count] = p_sample[...]
        sent[k, 2:8, :count] = found[...]
        sent[k, :, count:] = moments


def adjoint_kernel(
    got, observed, cells, hot, kx, ky, kz, dinv, dg, prim, f0, f1, f2,
    b0, b1, b2, pot, predicted, sent, heavy, a0, a1, a2,
):
    core = lax.axis_index("c")
    rows, lanes = prim.shape[2], prim.shape[3]
    count = cells.shape[1]
    total = got[0]
    for k in range(1, CHIPS):
        total = total + got[k]
    weights = weights_of(total[:, count:])
    sample = total[:, :count]
    value = sample[0:2]
    for k in range(3):
        value = value + weights[k] * sample[2 * k + 2 : 2 * k + 4]
    predicted[...] = value
    seen = jnp.where(core == 0, observed[0:2], observed[2:4])
    misfit = value - seen
    for i in range(6):
        for s in range(2):
            w = [weights[k][s : s + 1, :] for k in range(3)]
            pot[s, i] = prim[s, i + 3] + w[0] * f0[s, i + 3] + w[1] * f1[s, i + 3] + w[2] * f2[s, i + 3]

    picked = cells[...]
    lane_of = picked - (picked // lanes) * lanes
    lane_hot = one_hot(lanes, 0, lane_of)
    for s in range(2):
        spread = jnp.where(lane_hot, misfit[s : s + 1], 0.0)
        for k, piece in enumerate(pieces_of(spread)):
            heavy[k, pl.ds(s * lanes, lanes)] = piece
    placed = [
        lax.dot_general(hot[...], heavy[k], (((1,), (1,)), ((), ())), preferred_element_type=F32)
        for k in range(3)
    ]
    source = placed[0] + placed[1] + placed[2]
    for i in range(10):
        inverse = dinv[i + 1]
        for s in range(2):
            a0[s, i + 1] = inverse * source[i * rows : (i + 1) * rows, s * lanes : (s + 1) * lanes]
    moments = krylov(a0, a1, a2, kx, ky, kz, dinv, dg)
    for k in range(CHIPS):
        sent[k] = moments
    for near, deep in ((b0, a0), (b1, a1), (b2, a2)):
        near[...] = deep[:, 3:9]


def gradient_kernel(got, a0, a1, a2, pot, kept, given, adj):
    core = lax.axis_index("c")
    moments = got[0]
    for k in range(1, CHIPS):
        moments = moments + got[k]
    weights = weights_of(moments)
    rows, lanes = pot.shape[2], pot.shape[3]
    row_at = lax.broadcasted_iota(jnp.int32, (rows, lanes), 0)
    lane_at = lax.broadcasted_iota(jnp.int32, (rows, lanes), 1)
    for i in range(6):
        for s in range(2):
            w = [weights[k][s : s + 1, :] for k in range(3)]
            adj[s, i] = w[0] * a0[s, i] + w[1] * a1[s, i] + w[2] * a2[s, i]

    def along(mid_p, mid_a, axis, at):
        last = mid_p.shape[axis] - 1
        next_p = jnp.where(at == last, 0.0, ahead(mid_p, axis))
        next_a = jnp.where(at == last, 0.0, ahead(mid_a, axis))
        upper = (mid_p - next_p) * (mid_a - next_a)
        lower = jnp.where(at == 0, mid_p * mid_a, behind(upper, axis))
        return upper + lower

    for target, first in ((given, 1 + 2 * (1 - core)), (kept, 1 + 2 * core)):
        for j in range(2):
            i = first + j
            sums = [0.0, 0.0, 0.0]
            for s in range(2):
                mid_p, mid_a = pot[s, i], adj[s, i]
                upper = (mid_p - pot[s, i + 1]) * (mid_a - adj[s, i + 1])
                lower = (mid_p - pot[s, i - 1]) * (mid_a - adj[s, i - 1])
                sums[0] = sums[0] + upper + lower
                sums[1] = sums[1] + along(mid_p, mid_a, 0, row_at)
                sums[2] = sums[2] + along(mid_p, mid_a, 1, lane_at)
            for k in range(3):
                target[:, 2 * k + j] = (-0.5 * sums[k]).reshape(target.shape[0], target.shape[2], lanes)


def call(kernel, limit, outs, scratch=()):
    vmem = pl.BlockSpec(memory_space=pltpu.VMEM)

    def run(*args):
        return pl.pallas_call(
            kernel,
            out_shape=tuple(jax.ShapeDtypeStruct(x, kind) for x, kind in outs),
            in_specs=[vmem] * len(args),
            out_specs=tuple([vmem] * len(outs)),
            scratch_shapes=list(scratch),
            compiler_params=pltpu.CompilerParams(vmem_limit_bytes=limit * MEBI),
        )(*args)

    return run


NAMES = ("xh", "y", "xl", "c")


def routes(sizes, move):
    pairs = []
    nx, ny = sizes
    index = lambda h, y, l, c: ((h * ny + y) * 2 + l) * 2 + c
    for h in range(nx):
        for y in range(ny):
            for l in range(2):
                for c in range(2):
                    target = move(h, y, l, c)
                    if target is not None:
                        pairs.append((index(h, y, l, c), index(*target)))
    return pairs


def per_device(high_count, primary, conductivity, observed, receivers):
    chain = CHIPS // 2
    sizes = (high_count, chain)
    def beside(h, y, l, c):
        return (h, y, 1 - l, c)

    def around(h, y, l, c):
        side = (2 * h + l + (1 if l == 1 else -1)) % (2 * high_count)
        return (side // 2, y, side % 2, c)

    def along(sign):
        def move(h, y, l, c):
            target = y + sign * (1 if l == 0 else -1)
            return (h, target, l, c) if 0 <= target < chain else None

        return routes(sizes, move)

    def send(x, pairs):
        return lax.ppermute(x, NAMES, pairs)

    fields = primary[0]
    swap = routes(sizes, lambda h, y, l, c: (h, y, l, 1 - c))
    p_near = send(fields, routes(sizes, beside))
    c_near = send(conductivity, routes(sizes, around))
    c_next = send(conductivity, along(-1))
    p_near, c_near = lax.optimization_barrier((p_near, c_near))
    p_far = send(p_near, along(1))
    c_far = send(c_next, routes(sizes, beside))

    rows, lanes = primary.shape[3], primary.shape[4]
    count = receivers.shape[1]
    f32 = lambda *shape: (shape, F32)
    deep = f32(DEEP, rows, lanes)
    pairs = f32(2, DEEP, rows, lanes)
    four = f32(KEPT, rows, lanes)
    hot, hot_own = call(
        hot_kernel, 4, [((10 * rows, count), BF16), ((3 * KEPT * rows, count), BF16)]
    )(receivers)
    own_c, p_pair = lax.optimization_barrier((conductivity, send(fields, swap)))
    c_pair = send(own_c, swap)
    p_near_pair, c_near_pair = send(p_near, swap), send(c_near, swap)
    hot_own, c_near_pair, p_near_pair = lax.optimization_barrier((hot_own, c_near_pair, p_near_pair))
    p_mid, c_mid, ky_mid, kz_mid, dg_mid, p_sample = call(
        own_kernel,
        8,
        [f32(2, KEPT, rows, lanes), four, four, four, four, f32(2, count)],
        [pltpu.VMEM((2 * lanes, 3 * KEPT * rows), BF16)],
    )(fields, p_pair, conductivity, c_pair, receivers, hot_own)
    p_far, ready = lax.optimization_barrier((p_far, p_sample))
    p_far_pair, c_far_pair = send(p_far, swap), send(c_far, swap)
    kx, ky, kz, dinv, dg, prim, f0, f1, f2, sent = call(
        forward_kernel,
        20,
        [deep] * 5 + [pairs] * 4 + [f32(CHIPS, 8, count + 128)],
        [
            pltpu.VMEM((DEEP, rows, lanes), F32),
            pltpu.VMEM((6 * lanes, 3 * KEPT * rows), BF16),
            pltpu.VMEM((6, count), F32),
        ],
    )(
        p_mid, p_near, p_near_pair, p_far, p_far_pair,
        c_mid, c_near, c_near_pair, c_far, c_far_pair, ky_mid, kz_mid, dg_mid, receivers, hot_own, p_sample,
    )
    got = lax.all_to_all(sent, ("y", "xl"), 0, 0, tiled=True)
    six = (2, 6, rows, lanes)
    a0, a1, a2, pot, pred, sent = call(
        adjoint_kernel,
        18,
        [f32(*six)] * 4 + [f32(2, count), f32(CHIPS, 8, 128)],
        [pltpu.VMEM((3, 2 * lanes, count), BF16)] + [pltpu.VMEM((2, DEEP, rows, lanes), F32)] * 3,
    )(got, observed[0], receivers, hot, kx, ky, kz, dinv, dg, prim, f0, f1, f2)
    got = lax.all_to_all(sent, ("y", "xl"), 0, 0, tiled=True)
    slabs = lax.axis_size("z")
    chunks = (slabs, 6, rows // slabs, lanes)
    kept, given = call(gradient_kernel, 8, [f32(*chunks)] * 2, [pltpu.VMEM(six, F32)])(got, a0, a1, a2, pot)
    given, pred = lax.optimization_barrier((given, pred))
    total = kept + send(given, swap)
    pred_pair = send(pred, swap)
    even = lax.axis_index("c") == 0
    predicted = jnp.where(even, jnp.concatenate([pred, pred_pair]), jnp.concatenate([pred_pair, pred]))
    parts = lax.all_to_all(total, "z", 0, 0, tiled=True)
    share = jnp.sum(parts, axis=0, keepdims=True)
    if high_count > 1:
        share = share + lax.ppermute(share, "xh", [(0, 1), (1, 0)])
    spread = jnp.broadcast_to(share, chunks)
    whole = lax.all_to_all(spread, "z", 0, 0, tiled=True)
    grad = jnp.transpose(whole, (1, 0, 2, 3)).reshape(3, 2, rows, lanes)
    return grad, predicted[None]


def solution(mesh):
    groups = mesh.shape["src"]
    high = 2 if groups > 1 else 1
    devices = mesh.devices.reshape(groups // high, high, CHIPS // 2, 2, 2)
    inner = Mesh(devices, ("z", "xh", "y", "xl", "c"))
    src, dom = ("z", "xh"), ("y", "xl", "c")
    return jax.shard_map(
        functools.partial(per_device, high),
        mesh=inner,
        in_specs=(P(src, None, dom, None, None), P(None, dom, None, None), P(src, None, None), P(src, None)),
        out_specs=(P(None, dom, None, None), P(src, None, None)),
        check_vma=False,
    )
```
